128 devices in a mesh: row: 4 (over x), seq: 4 (over z_hi, core), head: 8 (over z_lo, y).
Axes of the slice: x: 4, y: 4, z: 4 (z_hi: 2, z_lo: 2; z = z_hi * 2 + z_lo), core: 2. Of those that a mesh axis runs over, the one named last changes fastest.
Arguments:
- layer_input: bfloat16 [8, 2048, 2048], P('row', 'seq'), may hold values from -6 to 6
- cotangent: bfloat16 [8, 2048, 2048], P('row', 'seq'), may hold values from -6 to 6
- lengths: int32 [8], P('row'), may hold values from 768 to 2048, as said below
- gain_attn: float32 [2048], replicated, may hold values from 0.5 to 1.5
- gain_ffn: float32 [2048], replicated, may hold values from 0.5 to 1.5
- query_key_value_weight: bfloat16 [3, 2048, 2048], P(None, None, 'head'), may hold values from -0.125 to 0.125
- m_qkv: float32 [3, 2048], P(None, 'head'), may hold values from 0.8 to 1.8
- query_key_value_left: float32 [3, 2048, 16], replicated, may hold values from -0.125 to 0.125
- query_key_value_right: float32 [3, 16, 2048], P(None, None, 'head'), may hold values from -0.3125 to 0.3125
- output_weight: bfloat16 [2048, 2048], P('head'), may hold values from -0.125 to 0.125
- m_out: float32 [2048], replicated, may hold values from 4 to 16
- output_factor_left: float32 [2048, 16], P('head'), may hold values from -0.125 to 0.125
- output_factor_right: float32 [16, 2048], replicated, may hold values from -0.3125 to 0.3125
- gate_up_weight: bfloat16 [2, 2048, 5632], P(None, None, 'head'), may hold values from -0.125 to 0.125
- m_gu: float32 [2, 5632], P(None, 'head'), may hold values from 0.8 to 1.6
- gate_up_factor_left: float32 [2, 2048, 16], replicated, may hold values from -0.125 to 0.125
- gate_up_factor_right: float32 [2, 16, 5632], P(None, None, 'head'), may hold values from -0.3125 to 0.3125
- down_weight: bfloat16 [5632, 2048], P('head'), may hold values from -0.078125 to 0.078125
- m_down: float32 [2048], replicated, may hold values from 1 to 4
- down_factor_left: float32 [5632, 16], P('head'), may hold values from -0.078125 to 0.078125
- down_factor_right: float32 [16, 2048], replicated, may hold values from -0.3125 to 0.3125
Outputs:
- output: bfloat16 [8, 2048, 2048], P('row', 'seq')
- grad_x: bfloat16 [8, 2048, 2048], P('row', 'seq')
- grad_m_qkv: float32 [3, 2048], P(None, 'head')
- grad_a_qkv: float32 [3, 2048, 16], replicated
- grad_b_qkv: float32 [3, 16, 2048], P(None, None, 'head')
- grad_m_out: float32 [2048], replicated
- grad_a_out: float32 [2048, 16], P('head')
- grad_b_out: float32 [16, 2048], replicated
- grad_m_gu: float32 [2, 5632], P(None, 'head')
- grad_a_gu: float32 [2, 2048, 16], replicated
- grad_b_gu: float32 [2, 16, 5632], P(None, None, 'head')
- grad_m_down: float32 [2048], replicated
- grad_a_down: float32 [5632, 16], P('head')
- grad_b_down: float32 [16, 2048], replicated
The draws below stay inside these ranges and needn't reach their ends.
Inputs may be any that keep to these rules, and one draw needn't show every extreme that they name: `lengths`: each row holds one document starting at its first slot. In every draw one row is full (2048) and another has the least length.
All inputs are finite; a program needn't handle non-finite values.
Results may differ from the reference program's by a relative error of at most 0.024.
Values may be sent and summed in bfloat16 or wider, within the bound.
A program may use at most 320 MiB of HBM per device.

```python
import math
import jax
import jax.numpy as jnp
from jax import lax

D = 2048
HEADS = 16
HD = 128
FF = 5632
ADAPTER_RANK = 16
SLOT = 2048
ROWS = 8


def draw_lengths(key, part):
    key = jax.random.fold_in(key, 7)
    first_factor, second_factor = jax.random.split(key)
    drawn = jax.random.randint(first_factor, (ROWS,), 3 * SLOT // 8, SLOT + 1, dtype=jnp.int32)
    order = jax.random.permutation(second_factor, ROWS)
    places = jnp.arange(ROWS, dtype=jnp.int32)
    drawn = jnp.where(places == order[0], SLOT, drawn)
    drawn = jnp.where(places == order[1], 3 * SLOT // 8, drawn)
    return drawn.astype(jnp.int32)


def levels(key, extent, pieces, least, top_value):
    factor_of = 1.0
    for position, shards_of in pieces:
        steps = jax.random.uniform(jax.random.fold_in(jax.random.fold_in(key, 6), position), (shards_of,), jnp.float32, least / len(pieces), top_value / len(pieces))
        factor_of = factor_of * jnp.repeat(jnp.exp(steps), extent[position] // shards_of).reshape((-1,) + (1,) * (len(extent) - 1 - position))
    return factor_of


def normal_values(stream_key, shape, scale, most, cuts=(), held_as=jnp.bfloat16):
    entries = scale * jax.random.normal(stream_key, shape, jnp.float32)
    if cuts:
        entries = entries * levels(stream_key, shape, cuts, -0.22, 0.18)
    return jnp.clip(entries, -most, most).astype(held_as)


def setup_inputs(seed: int = 0) -> dict:
    keys = jax.random.split(jax.random.key(seed), 22)
    layer_input = normal_values(keys[0], (ROWS, SLOT, D), 1.0, 6.0, ((0, 4), (1, 4)))
    cotangent = normal_values(keys[1], (ROWS, SLOT, D), 1.0, 6.0, ((0, 4), (1, 4)))
    lengths = draw_lengths(jax.random.fold_in(keys[21], 71), 0)
    gain_attn = jnp.clip(1.0 + 0.1 * jax.random.normal(keys[3], (D,), jnp.float32), 0.5, 1.5)
    gain_ffn = jnp.clip(1.0 + 0.1 * jax.random.normal(keys[4], (D,), jnp.float32), 0.5, 1.5)
    query_key_value_weight = normal_values(keys[5], (3, D, D), D ** -0.5, 0.125, ((2, 8),))
    m_qkv = jnp.clip(jnp.exp(math.log(1.8) - 0.8109302 * jax.random.uniform(keys[6], (3, D), jnp.float32) ** levels(keys[6], (3, D), ((1, 8),), -0.2, 0.2)), 0.8, 1.8)
    query_key_value_left = normal_values(keys[7], (3, D, ADAPTER_RANK), D ** -0.5, 0.125, (), jnp.float32)
    query_key_value_right = normal_values(keys[8], (3, ADAPTER_RANK, D), (25 * ADAPTER_RANK) ** -0.5, 0.3125, ((2, 8),), jnp.float32)
    output_weight = normal_values(keys[9], (D, D), D ** -0.5, 0.125, ((0, 8),))
    m_out = jnp.clip(jnp.exp(jax.random.uniform(keys[10], (D,), jnp.float32, math.log(4.0), math.log(16.0))), 4.0, 16.0)
    output_factor_left = normal_values(keys[11], (D, ADAPTER_RANK), D ** -0.5, 0.125, ((0, 8),), jnp.float32)
    output_factor_right = normal_values(keys[12], (ADAPTER_RANK, D), (25 * ADAPTER_RANK) ** -0.5, 0.3125, (), jnp.float32)
    gate_up_weight = normal_values(keys[13], (2, D, FF), D ** -0.5, 0.125, ((2, 8),))
    m_gu = jnp.clip(jnp.exp(math.log(1.6) - 0.6931472 * jax.random.uniform(keys[14], (2, FF), jnp.float32) ** levels(keys[14], (2, FF), ((1, 8),), -0.2, 0.2)), 0.8, 1.6)
    gate_up_factor_left = normal_values(keys[15], (2, D, ADAPTER_RANK), D ** -0.5, 0.125, (), jnp.float32)
    gate_up_factor_right = normal_values(keys[16], (2, ADAPTER_RANK, FF), (25 * ADAPTER_RANK) ** -0.5, 0.3125, ((2, 8),), jnp.float32)
    down_weight = normal_values(keys[17], (FF, D), FF ** -0.5, 0.078125, ((0, 8),))
    m_down = jnp.clip(jnp.exp(jax.random.uniform(keys[18], (D,), jnp.float32, math.log(1.0), math.log(4.0))), 1.0, 4.0)
    down_factor_left = normal_values(keys[19], (FF, ADAPTER_RANK), FF ** -0.5, 0.078125, ((0, 8),), jnp.float32)
    down_factor_right = normal_values(keys[20], (ADAPTER_RANK, D), (25 * ADAPTER_RANK) ** -0.5, 0.3125, (), jnp.float32)
    return dict(layer_input=layer_input, cotangent=cotangent, lengths=lengths, gain_attn=gain_attn, gain_ffn=gain_ffn, query_key_value_weight=query_key_value_weight, m_qkv=m_qkv, query_key_value_left=query_key_value_left, query_key_value_right=query_key_value_right, output_weight=output_weight, m_out=m_out, output_factor_left=output_factor_left, output_factor_right=output_factor_right, gate_up_weight=gate_up_weight, m_gu=m_gu, gate_up_factor_left=gate_up_factor_left, gate_up_factor_right=gate_up_factor_right, down_weight=down_weight, m_down=m_down, down_factor_left=down_factor_left, down_factor_right=down_factor_right)


@jax.custom_vjp
def low(v):
    return lax.optimization_barrier(v.astype(jnp.bfloat16)).astype(jnp.float32)

@jax.custom_vjp
def low_back(v):
    return v

def low_keep(v):
    return (low(v), None)

def low_pass(kept, grad):
    return (grad,)

def back_keep(v):
    return (v, None)

def back_low(kept, grad):
    return (low(grad),)
low.defvjp(low_keep, low_pass)
low_back.defvjp(back_keep, back_low)
adapter_alpha_value = 32.0
norm_eps = 1e-05
rope_base = 10000.0
masked_score = -1000000000.0
precise_matmul = lax.Precision.HIGHEST

def angles(positions):
    freqs = rope_base ** (-jnp.arange(HD // 2, dtype=jnp.float32) * 2.0 / HD)
    turned = positions[:, None] * freqs[None, :]
    return (jnp.cos(turned)[:, None, :], jnp.sin(turned)[:, None, :])

def rotate(values, cosines, sines):
    half = values.shape[-1] // 2
    first_factor = values[..., :half]
    second_factor = values[..., half:]
    return jnp.concatenate([first_factor * cosines - second_factor * sines, second_factor * cosines + first_factor * sines], axis=-1)

def rms_scale(values):
    return values * lax.rsqrt(lax.optimization_barrier(jnp.mean(values * values, axis=-1, keepdims=True)) + norm_eps)

def merge(weight_matrix, magnitude, first_factor, second_factor):
    unit_direction = weight_matrix + adapter_alpha_value / ADAPTER_RANK * jnp.matmul(first_factor, second_factor, precision=precise_matmul)
    norm = jnp.sqrt(lax.optimization_barrier(jnp.sum(unit_direction * unit_direction, axis=-2, keepdims=True)))
    return low(magnitude[..., None, :] * unit_direction / norm)

def row_forward(rows, length, gain_attn, gain_ffn, merged_qkv, merged_out, merged_gu, merged_down):
    positions = jnp.arange(SLOT, dtype=jnp.int32)
    live = (positions < length).astype(jnp.float32)
    cosines, sines = angles(positions.astype(jnp.float32))
    normed1 = low(rms_scale(rows) * gain_attn)
    query = low_back(jnp.dot(normed1, merged_qkv[0], precision=precise_matmul))
    key = low_back(jnp.dot(normed1, merged_qkv[1], precision=precise_matmul))
    value = low(low_back(jnp.dot(normed1, merged_qkv[2], precision=precise_matmul)))
    query = low(rotate(query.reshape(SLOT, HEADS, HD), cosines, sines))
    key = low(rotate(key.reshape(SLOT, HEADS, HD), cosines, sines))
    scores = low_back(jnp.einsum('qhd,khd->hqk', query, key, precision=precise_matmul) * HD ** (-0.5))
    allowed = (positions[None, :] <= positions[:, None]) & (positions[None, :] < length)
    masked = jnp.where(allowed[None], scores, masked_score)
    expo = jnp.exp(masked - lax.optimization_barrier(jnp.max(masked, axis=-1, keepdims=True)))
    probs = low(expo / lax.optimization_barrier(jnp.sum(expo, axis=-1, keepdims=True)))
    mixed = jnp.einsum('hqk,khd->qhd', probs, value.reshape(SLOT, HEADS, HD), precision=precise_matmul)
    mixed = low(low_back(mixed.reshape(SLOT, D)))
    hidden1 = rows + low_back(jnp.dot(mixed, merged_out, precision=precise_matmul))
    normed2 = low(rms_scale(hidden1) * gain_ffn)
    gate = low_back(jnp.dot(normed2, merged_gu[0], precision=precise_matmul))
    up = low_back(jnp.dot(normed2, merged_gu[1], precision=precise_matmul))
    inner = low(gate * jax.nn.sigmoid(gate) * up)
    result = hidden1 + jnp.dot(inner, merged_down, precision=precise_matmul)
    return result * live[:, None]

def reference(layer_input, cotangent, lengths, gain_attn, gain_ffn, query_key_value_weight, m_qkv, query_key_value_left, query_key_value_right, output_weight, m_out, output_factor_left, output_factor_right, gate_up_weight, m_gu, gate_up_factor_left, gate_up_factor_right, down_weight, m_down, down_factor_left, down_factor_right):
    inputs = layer_input.astype(jnp.float32)
    frozen_qkv = query_key_value_weight.astype(jnp.float32)
    frozen_out = output_weight.astype(jnp.float32)
    frozen_gu = gate_up_weight.astype(jnp.float32)
    frozen_down = down_weight.astype(jnp.float32)

    def forward(rows_all, mag_qkv, fa_qkv, fb_qkv, mag_out, fa_out, fb_out, mag_gu, fa_gu, fb_gu, mag_down, fa_down, fb_down):
        merged_qkv = merge(frozen_qkv, mag_qkv, fa_qkv, fb_qkv)
        merged_out = merge(frozen_out, mag_out, fa_out, fb_out)
        merged_gu = merge(frozen_gu, mag_gu, fa_gu, fb_gu)
        merged_down = merge(frozen_down, mag_down, fa_down, fb_down)

        def one_row(item):
            rows, length = item
            return row_forward(rows, length, gain_attn, gain_ffn, merged_qkv, merged_out, merged_gu, merged_down)
        return lax.map(jax.checkpoint(one_row), (rows_all, lengths.astype(jnp.int32)))
    result, pullback = jax.vjp(forward, inputs, m_qkv, query_key_value_left, query_key_value_right, m_out, output_factor_left, output_factor_right, m_gu, gate_up_factor_left, gate_up_factor_right, m_down, down_factor_left, down_factor_right)
    grads = pullback(cotangent.astype(jnp.float32))
    return (result.astype(jnp.bfloat16), grads[0].astype(jnp.bfloat16), grads[1], grads[2], grads[3], grads[4], grads[5], grads[6], grads[7], grads[8], grads[9], grads[10], grads[11], grads[12])
```

```python
import functools

import jax
import jax.numpy as jnp
from jax import lax
from jax.experimental import pallas as pl
from jax.experimental.pallas import tpu as pltpu
from jax.sharding import PartitionSpec as P

HD = 128
RANK = 16
SCALE = 2.0
EPS = 1e-05
ROPE_BASE = 10000.0
MASKED = -1000000000.0
F32 = jnp.float32
BF16 = jnp.bfloat16


def pad_to(n, m=256):
    return -(-n // m) * m


def mm(a, b, dims):
    return lax.dot_general(a, b, (dims, ((), ())), preferred_element_type=F32)


def nn(a, b):
    return mm(a, b, ((1,), (0,)))


def nt(a, b):
    return mm(a, b, ((1,), (1,)))


def tn(a, b):
    return mm(a, b, ((0,), (0,)))


MESH = pl.DeviceIdType.MESH
VMEM = pl.BlockSpec(memory_space=pltpu.VMEM)
ROOM = 60 * 2**20
RING = 4
PARTS = 8


class Place:
    def __init__(self):
        self.row, self.seq, self.me = (lax.axis_index(n) for n in ("row", "seq", "head"))
        self.y = lax.rem(self.me, RING)
        self.z = self.me // RING
        self.far = 1 - self.z
        self.cross = self.far * RING + self.y

    def side(self, step):
        return lax.rem(self.y + step, RING)

    def at(self, head):
        return (self.row, self.seq, head)

    def greet(self):
        barrier = pltpu.get_barrier_semaphore()
        for step in range(1, PARTS):
            pl.semaphore_signal(
                barrier, inc=1, device_id=self.at(lax.rem(self.me + step, PARTS)), device_id_type=MESH
            )
        pl.semaphore_wait(barrier, PARTS - 1)

    def send(self, source, target, sems, index, head):
        copy = pltpu.make_async_remote_copy(
            src_ref=source,
            dst_ref=target,
            send_sem=sems[0].at[index],
            recv_sem=sems[1].at[index],
            device_id=self.at(head),
            device_id_type=MESH,
        )
        copy.start()
        return copy


def rows_of(index, count):
    return pl.ds(pl.multiple_of(index * count, count), count)


class Gather:
    def __init__(self, place, buf, chunk, cut, sems, stride=None, offset=0):
        self.place, self.buf, self.chunk, self.cut, self.sems = place, buf, chunk, cut, sems
        self.stride, self.offset = stride or chunk, offset

    def view(self, head, which):
        first = head * self.stride + self.offset * self.chunk
        rows = pl.ds(pl.multiple_of(first, self.chunk), self.chunk)
        if which == "a":
            return self.buf.at[rows, : self.cut]
        if which == "b":
            return self.buf.at[rows, self.cut :]
        return self.buf.at[rows]

    def pass_on(self, head, which, index, to):
        view = self.view(head, which)
        return self.place.send(view, view, self.sems, index, to)

    def start(self):
        p = self.place
        self.across = [self.pass_on(p.me, "a", 0, p.cross)]
        self.ring = [
            self.pass_on(p.me, "all", step, p.z * RING + p.side(step)) for step in (1, 3, 2)
        ]
        self.across.append(self.pass_on(p.me, "b", 4, p.cross))

    def middle(self):
        p = self.place
        self.across[0].wait_recv()
        self.around = [
            self.pass_on(p.cross, "a", 4 + step, p.z * RING + p.side(step)) for step in (1, 3, 2)
        ]
        for copy, step in zip(self.ring, (1, 3, 2)):
            copy.wait_recv()
            from_head = p.z * RING + p.side(RING - step)
            self.across.append(self.pass_on(from_head, "b", 7 + step, p.cross))

    def end(self):
        for copy in self.across[1:] + self.around:
            copy.wait_recv()
        for copy in self.across + self.ring + self.around:
            copy.wait_send()


GATHER_SEMS = 11


class Scatter:
    def __init__(self, place, src, out, chunk, cut, scratch):
        self.place, self.src, self.out, self.chunk, self.cut = place, src, out, chunk, cut
        self.far_q, self.land_q, self.hold_q, self.land_p, self.hold_p, self.far_p, s, r = scratch
        self.sems = (s, r)

    @staticmethod
    def scratch(chunk, cut, width):
        rest = width - cut
        return [
            pltpu.VMEM((RING * chunk, cut), BF16),
            pltpu.VMEM((RING - 1, chunk, cut), BF16),
            pltpu.VMEM((RING - 1, chunk, cut), BF16),
            pltpu.VMEM((RING - 1, 2, chunk, rest), BF16),
            pltpu.VMEM((chunk, rest), BF16),
            pltpu.VMEM((chunk, rest), BF16),
            pltpu.SemaphoreType.DMA((11,)),
            pltpu.SemaphoreType.DMA((11,)),
        ]

    def start(self):
        p = self.place
        half = rows_of(p.far, RING * self.chunk)
        self.first = p.send(self.src.at[half, : self.cut], self.far_q, self.sems, 0, p.cross)
        self.ring = []
        for step in (1, 3, 2):
            to = p.side(step)
            for plane in range(2):
                view = self.src.at[rows_of(plane * RING + to, self.chunk), self.cut :]
                target = self.land_p.at[step - 1, plane]
                self.ring.append(
                    p.send(view, target, self.sems, 1 + 2 * (step - 1) + plane, p.z * RING + to)
                )

    def middle(self):
        p = self.place
        self.first.wait_recv()
        self.around = []
        for step in (1, 3, 2):
            to = p.side(step)
            mine = self.src[rows_of(p.z * RING + to, self.chunk), : self.cut].astype(F32)
            theirs = self.far_q[rows_of(to, self.chunk), :].astype(F32)
            self.hold_q[step - 1] = (mine + theirs).astype(BF16)
            self.around.append(
                p.send(
                    self.hold_q.at[step - 1],
                    self.land_q.at[step - 1],
                    self.sems,
                    6 + step,
                    p.z * RING + to,
                )
            )
        for copy in self.ring:
            copy.wait_recv()
        total = self.src[rows_of(p.cross, self.chunk), self.cut :].astype(F32)
        for step in range(RING - 1):
            total += self.land_p[step, p.far].astype(F32)
        self.hold_p[...] = total.astype(BF16)
        self.last = p.send(self.hold_p, self.far_p, self.sems, 10, p.cross)
        self.out[:, : self.cut] = self.src[rows_of(p.me, self.chunk), : self.cut].astype(
            F32
        ) + self.far_q[rows_of(p.y, self.chunk), :].astype(F32)
        total = self.src[rows_of(p.me, self.chunk), self.cut :].astype(F32)
        for step in range(RING - 1):
            total += self.land_p[step, p.z].astype(F32)
        self.out[:, self.cut :] = total

    def end(self):
        for copy in self.around:
            copy.wait_recv()
        for step in range(RING - 1):
            self.out[:, : self.cut] += self.land_q[step].astype(F32)
        self.last.wait_recv()
        self.out[:, self.cut :] += self.far_p[...].astype(F32)
        for copy in [self.first, self.last] + self.ring + self.around:
            copy.wait_send()


def feed_kernel(
    span,
    lengths,
    mixed_ref,
    s_out,
    gain,
    s_gu,
    s_down,
    b_gu,
    at_gu,
    at_down,
    b_down,
    b_out,
    at_out,
    x_hbm,
    cot_hbm,
    vout_hbm,
    vgu_hbm,
    vdown_hbm,
    ffn_ref,
    h1_ref,
    dh1_ref,
    dmix_ref,
    ga_gu,
    gb_gu,
    e_gu,
    ga_down,
    gb_down,
    ga_out,
    gb_out,
    e_out,
    vout,
    vgu,
    vdown,
    dys,
    xn2,
    part,
    dhid,
    hid,
    dgu,
    x_own,
    mixed_own,
    dmix_own,
    attn,
    sum_own,
    local_sems,
    swap_s,
    swap_r,
    back_s,
    back_r,
    gather_s,
    gather_r,
    *scatter_scratch,
):
    tokens, width = xn2.shape
    chunk = tokens // PARTS
    block = tokens // 2
    cols = mixed_ref.shape[1]
    hpad = hid.shape[1]
    tile = 256
    p = Place()
    own = rows_of(p.me, chunk)
    loads = []
    for i, (src, dst) in enumerate(
        [
            (cot_hbm, dys),
            (vdown_hbm, vdown),
            (x_hbm.at[own], x_own),
            (vout_hbm, vout),
            (vgu_hbm, vgu),
        ]
    ):
        loads.append(pltpu.make_async_copy(src, dst, local_sems.at[i]))
        loads[-1].start()
    p.greet()

    my_cols = rows_of(p.me, cols)
    swaps = []
    for step in range(1, PARTS):
        to = lax.rem(p.me + step, PARTS)
        swaps.append(
            p.send(
                mixed_ref.at[rows_of(to, chunk)],
                mixed_own.at[:, my_cols],
                (swap_s, swap_r),
                step - 1,
                to,
            )
        )
    mixed_own[:, my_cols] = mixed_ref[own, :]

    loads[0].wait()
    loads[1].wait()
    seq = lax.axis_index("seq")

    @pl.loop(0, PARTS)
    def _(i):
        rows = rows_of(i, chunk)
        base = lax.rem(i * chunk, span)
        length = lengths[0]
        for r in range(1, tokens // span):
            length = jnp.where(i * chunk >= r * span, lengths[r], length)
        pos = seq * span + base + lax.broadcasted_iota(jnp.int32, (chunk, 1), 0)
        live = (pos < length).astype(F32)
        dys[rows, :] = (dys[rows, :].astype(F32) * live * s_down[...]).astype(BF16)

    @pl.loop(0, hpad // tile)
    def _(n):
        part_cols = rows_of(n, tile)
        for half in range(2):
            rows = slice(half * block, (half + 1) * block)
            dhid[rows, part_cols] = nt(dys[rows, :], vdown[part_cols, :])

    for copy in swaps:
        copy.wait_recv()
    loads[2].wait()
    loads[3].wait()

    @pl.loop(0, width // 512)
    def _(n):
        part_cols = rows_of(n, 512)
        attn[:, part_cols] = nn(mixed_own[...], vout[:, part_cols]) * s_out[:, part_cols]

    h1_ref[...] = x_own[...].astype(F32) + attn[...]
    inv2 = lax.rsqrt(jnp.mean(h1_ref[...] * h1_ref[...], axis=-1, keepdims=True) + EPS)
    xn2[own, :] = (h1_ref[...] * inv2 * gain[...]).astype(BF16)
    gather = Gather(p, xn2, chunk, 768, (gather_s, gather_r))
    gather.start()
    e_gu[...] = jnp.zeros_like(e_gu)
    loads[4].wait()

    def hidden_units(plane):
        rows = rows_of(plane, block)

        @pl.loop(0, hpad // tile)
        def _(n):
            at_gate = rows_of(n, tile)
            at_up = rows_of(n + hpad // tile, tile)
            gate = nt(xn2[rows, :], vgu[at_gate, :]) * s_gu[:, at_gate]
            up = nt(xn2[rows, :], vgu[at_up, :]) * s_gu[:, at_up]
            sigma = jax.nn.sigmoid(gate)
            active = gate * sigma
            hid[rows, at_gate] = (active * up).astype(BF16)
            back = dhid[rows, at_gate]
            grad_gate = back * up * sigma * (1.0 + gate * (1.0 - sigma))
            grad_up = back * active
            e_gu[:, at_gate] += jnp.sum(grad_gate * gate, axis=0, keepdims=True)
            e_gu[:, at_up] += jnp.sum(grad_up * up, axis=0, keepdims=True)
            dgu[rows, at_gate] = (grad_gate * s_gu[:, at_gate]).astype(BF16)
            dgu[rows, at_up] = (grad_up * s_gu[:, at_up]).astype(BF16)

        @pl.loop(0, width // 512)
        def _(n):
            part_cols = rows_of(n, 512)
            part[rows, part_cols] = nn(dgu[rows, :], vgu[:, part_cols]).astype(BF16)

    gather.middle()
    hidden_units(p.z)
    gather.end()
    hidden_units(p.far)

    scatter = Scatter(p, part, sum_own, chunk, 1280, scatter_scratch)
    scatter.start()

    @pl.loop(0, width // 512)
    def _(n):
        part_cols = rows_of(n, 512)
        for half in range(2):
            rows = slice(half * block, (half + 1) * block)
            ffn_ref[rows, part_cols] = nn(hid[rows, :], vdown[:, part_cols]).astype(BF16)

    scatter.middle()
    t_gu = []
    for k in range(2):
        part_cols = slice(k * hpad, (k + 1) * hpad)
        t_gu.append(nt(b_gu[:, part_cols], dgu[:, part_cols]).astype(BF16))
    t_gu = jnp.concatenate(t_gu, axis=0)
    x_gu = nt(at_gu[...], xn2[...]).astype(BF16)
    for n in range(0, width, 512):
        ga_gu[:, n : n + 512] = nn(t_gu, xn2[:, n : n + 512])
    for k in range(2):
        part_cols = slice(k * hpad, (k + 1) * hpad)
        gb_gu[:, part_cols] = nn(x_gu[k * RANK : (k + 1) * RANK], dgu[:, part_cols])
    t_down = nt(b_down[...], dys[...]).astype(BF16)
    ga_down[...] = nn(t_down, hid[...])
    x_down = nt(at_down[...], hid[...]).astype(BF16)
    for n in range(0, width, 512):
        gb_down[:, n : n + 512] = nn(x_down, dys[:, n : n + 512])
    scatter.end()

    length = lengths[0]
    for r in range(1, tokens // span):
        length = jnp.where(p.me * chunk >= r * span, lengths[r], length)
    pos = seq * span + lax.rem(p.me * chunk, span) + lax.broadcasted_iota(jnp.int32, (chunk, 1), 0)
    live = (pos < length).astype(F32)
    dy_copy = pltpu.make_async_copy(cot_hbm.at[own], x_own, local_sems.at[5])
    dy_copy.start()
    scaled = sum_own[...] * gain[...]
    h1 = h1_ref[...]
    mean = jnp.mean(scaled * h1, axis=-1, keepdims=True)
    dy_copy.wait()
    grad = x_own[...].astype(F32) * live + inv2 * (scaled - h1 * (inv2 * inv2 * mean))
    dh1_ref[...] = grad
    low = grad.astype(BF16).astype(F32)
    e_out[...] = jnp.sum(low * attn[...], axis=0, keepdims=True)
    das = (low * s_out[...]).astype(BF16)

    @pl.loop(0, width // 512)
    def _(n):
        part_cols = rows_of(n, 512)
        dmix_own[:, part_cols] = nt(das, vout[part_cols, :]).astype(BF16)

    backs = []
    for step in range(1, PARTS):
        to = lax.rem(p.me + step, PARTS)
        backs.append(
            p.send(
                dmix_own.at[:, rows_of(to, cols)],
                dmix_ref.at[own],
                (back_s, back_r),
                step - 1,
                to,
            )
        )
    dmix_ref[own, :] = dmix_own[:, my_cols]
    t_out = nt(b_out[...], das).astype(BF16)
    ga_out[...] = nn(t_out, mixed_own[...])
    x_out = nt(at_out[...], mixed_own[...]).astype(BF16)
    gb_out[...] = nn(x_out, das)
    for copy in backs:
        copy.wait_recv()
    for copy in swaps + backs:
        copy.wait_send()


def feed(span, lengths, mixed, s_out, gain, s_gu, s_down, b_gu, at_gu, at_down, b_down, b_out, at_out, x, cot, vout, vgu, vdown):
    tokens, cols = mixed.shape
    width = x.shape[1]
    hpad = vdown.shape[0]
    chunk = tokens // PARTS
    shape = jax.ShapeDtypeStruct
    out_shape = (
        shape((tokens, width), BF16),
        shape((chunk, width), F32),
        shape((chunk, width), F32),
        shape((tokens, cols), BF16),
        shape((2 * RANK, width), F32),
        shape((RANK, 2 * hpad), F32),
        shape((1, 2 * hpad), F32),
        shape((RANK, hpad), F32),
        shape((RANK, width), F32),
        shape((RANK, width), F32),
        shape((RANK, width), F32),
        shape((1, width), F32),
    )
    dma = pltpu.SemaphoreType.DMA
    scratch = [
        pltpu.VMEM((width, width), BF16),
        pltpu.VMEM((2 * hpad, width), BF16),
        pltpu.VMEM((hpad, width), BF16),
        pltpu.VMEM((tokens, width), BF16),
        pltpu.VMEM((tokens, width), BF16),
        pltpu.VMEM((tokens, width), BF16),
        pltpu.VMEM((tokens, hpad), F32),
        pltpu.VMEM((tokens, hpad), BF16),
        pltpu.VMEM((tokens, 2 * hpad), BF16),
        pltpu.VMEM((chunk, width), BF16),
        pltpu.VMEM((chunk, width), BF16),
        pltpu.VMEM((chunk, width), BF16),
        pltpu.VMEM((chunk, width), F32),
        pltpu.VMEM((chunk, width), F32),
        dma((6,)),
        dma((PARTS - 1,)),
        dma((PARTS - 1,)),
        dma((PARTS - 1,)),
        dma((PARTS - 1,)),
        dma((GATHER_SEMS,)),
        dma((GATHER_SEMS,)),
    ] + Scatter.scratch(chunk, 1280, width)
    anywhere = pl.BlockSpec(memory_space=pl.ANY)
    return pl.pallas_call(
        functools.partial(feed_kernel, span),
        out_shape=out_shape,
        in_specs=[pl.BlockSpec(memory_space=pltpu.SMEM)] + [VMEM] * 11 + [anywhere] * 5,
        out_specs=[VMEM] * len(out_shape),
        scratch_shapes=scratch,
        compiler_params=pltpu.CompilerParams(
            collective_id=1, has_side_effects=True, vmem_limit_bytes=ROOM
        ),
    )(lengths, mixed, s_out, gain, s_gu, s_down, b_gu, at_gu, at_down, b_down, b_out, at_out, x, cot, vout, vgu, vdown)


def turn(values, cosines, sines):
    return values * cosines + pltpu.roll(values, HD // 2, 1) * sines


def scores_of(q, keys, query_pos, key_pos, first, length):
    scores = nt(q, keys) * HD ** (-0.5)
    at = key_pos + first
    return jnp.where((at <= query_pos) & (at < length), scores, MASKED)


def back_kernel(
    rows,
    lengths,
    q_ref,
    kv_ref,
    mixed_ref,
    lse_ref,
    dmix_ref,
    ffn_ref,
    kept_ref,
    cosines,
    sines,
    s_qkv,
    s_down,
    h1_ref,
    cot_hbm,
    dqkv_ref,
    e_qkv,
    out_ref,
    e_down,
    dkv,
    sib_far,
    hold,
    far,
    sib,
    dq,
    total_own,
    dy_own,
    local_sem,
    send_sems,
    recv_sems,
    *scatter_scratch,
):
    tokens, cols = q_ref.shape
    span = tokens // rows
    heads = cols // HD
    chunk = tokens // PARTS
    p = Place()
    core = lax.rem(p.seq, 2)
    upper = p.seq // 2
    sibling = upper * 2 + 1 - core
    load = pltpu.make_async_copy(cot_hbm.at[rows_of(p.me, chunk)], dy_own, local_sem)
    load.start()
    barrier = pltpu.get_barrier_semaphore()
    for step in range(1, PARTS):
        place = p.at(lax.rem(p.me + step, PARTS))
        pl.semaphore_signal(barrier, inc=1, device_id=place, device_id_type=MESH)
    for seq in (sibling, (1 - upper) * 2 + core):
        pl.semaphore_signal(barrier, inc=1, device_id=(p.row, seq, p.me), device_id_type=MESH)
    pl.semaphore_wait(barrier, PARTS + 1)

    def over(source, target, index, seq):
        return pltpu.make_async_remote_copy(
            src_ref=source,
            dst_ref=target,
            send_sem=send_sems.at[index],
            recv_sem=recv_sems.at[index],
            device_id=(p.row, seq, p.me),
            device_id_type=MESH,
        )

    to_sib_far = []
    to_sib = []
    to_far = []
    for r in range(rows):
        part = slice(r * span, (r + 1) * span)
        to_sib_far.append(over(dkv.at[1 - core, part], sib_far.at[part], r, sibling))
        to_sib.append(over(dkv.at[upper * 2, part], sib.at[part], rows + r, sibling))
        to_far.append(over(hold.at[part], far.at[part], 2 * rows + r, core))

    scatter = Scatter(p, ffn_ref, total_own, chunk, 1280, scatter_scratch)
    scatter.start()
    query_pos = p.seq * span + lax.broadcasted_iota(jnp.int32, (span, span), 0)
    key_pos = lax.broadcasted_iota(jnp.int32, (span, span), 1)

    def one_head(r, head):
        part = slice(r * span, (r + 1) * span)
        kcols = slice(head * HD, (head + 1) * HD)
        vcols = slice(cols + head * HD, cols + (head + 1) * HD)
        q = q_ref[part, kcols]
        do = dmix_ref[part, kcols]
        lse = lse_ref[part, head * HD : head * HD + 1]
        inner = jnp.sum(
            do.astype(F32) * mixed_ref[part, kcols].astype(F32), axis=-1, keepdims=True
        )
        dq[part, kcols] = jnp.zeros((span, HD), F32)

        @pl.loop(0, p.seq + 1)
        def _(j):
            scores = scores_of(q, kv_ref[j, part, kcols], query_pos, key_pos, j * span, lengths[r])
            probs = jnp.exp(scores - lse)
            dkv[j, part, vcols] = tn(probs.astype(BF16), do).astype(BF16)
            grad = (probs * (nt(do, kv_ref[j, part, vcols]) - inner)).astype(BF16)
            dq[part, kcols] += nn(grad, kv_ref[j, part, kcols])
            dkv[j, part, kcols] = (tn(grad, q) * HD ** (-0.5)).astype(BF16)

    def near(r):
        @pl.when(upper == 1)
        def _():
            to_sib_far[r].start()

        @pl.when(core == 1)
        def _():
            to_sib[r].start()

    def onward(r):
        part = slice(r * span, (r + 1) * span)

        @pl.when(upper == 1)
        def _():
            to_sib_far[r].wait_recv()
            hold[part] = (dkv[core, part].astype(F32) + sib_far[part].astype(F32)).astype(BF16)
            to_far[r].start()

    for r in range(rows):
        for head in range(heads):
            one_head(r, head)
            if r and head == 0:
                onward(r - 1)
        near(r)
    onward(rows - 1)
    scatter.middle()

    e_qkv[...] = jnp.zeros_like(e_qkv)

    def emit(part, at, grad, which):
        held = kept_ref[part, at].astype(F32)
        e_qkv[:, at] += jnp.sum(grad * held, axis=0, keepdims=True)
        dqkv_ref[part, at] = (grad * s_qkv[:, at]).astype(BF16)

    for r in range(rows):
        part = slice(r * span, (r + 1) * span)
        for head in range(heads):
            at = slice(head * HD, (head + 1) * HD)
            grad = turn(dq[part, at] * HD ** (-0.5), cosines[...], -sines[...])
            emit(part, at, grad, 0)
    scatter.end()
    load.wait()
    length = lengths[0]
    for r in range(1, rows):
        length = jnp.where(p.me * chunk >= r * span, lengths[r], length)
    pos = p.seq * span + lax.rem(p.me * chunk, span) + lax.broadcasted_iota(jnp.int32, (chunk, 1), 0)
    live = (pos < length).astype(F32)
    ffn = total_own[...] * s_down[...]
    out_ref[...] = ((h1_ref[...] + ffn) * live).astype(BF16)
    e_down[...] = jnp.sum(dy_own[...].astype(F32) * live * ffn, axis=0, keepdims=True)

    for r in range(rows):
        part = slice(r * span, (r + 1) * span)

        @pl.when(core == 0)
        def _(r=r):
            to_sib[r].wait_recv()

        @pl.when(upper == 0)
        def _(r=r):
            to_far[r].wait_recv()

        with_sib = (core == 0).astype(F32)
        with_far = (upper == 0).astype(F32)
        for head in range(2 * heads):
            at = slice(head * HD, (head + 1) * HD)
            grad = dkv[p.seq, part, at].astype(F32)
            grad = grad + jnp.where(core == 0, sib[part, at].astype(F32), 0.0)
            grad = grad + jnp.where(upper == 0, far[part, at].astype(F32), 0.0)
            if head < heads:
                grad = turn(grad, cosines[...], -sines[...])
            emit(part, slice(cols + head * HD, cols + (head + 1) * HD), grad, 1)

    for r in range(rows):

        @pl.when(upper == 1)
        def _(r=r):
            to_sib_far[r].wait_send()
            to_far[r].wait_send()

        @pl.when(core == 1)
        def _(r=r):
            to_sib[r].wait_send()


def back(rows, lengths, q, kv, mixed, lse, dmix, ffn, kept, cosines, sines, s_qkv, s_down, h1, cot):
    tokens, cols = q.shape
    width = ffn.shape[1]
    chunk = tokens // PARTS
    shape = jax.ShapeDtypeStruct
    dma = pltpu.SemaphoreType.DMA
    out_shape = (
        shape((tokens, 3 * cols), BF16),
        shape((1, 3 * cols), F32),
        shape((chunk, width), BF16),
        shape((1, width), F32),
    )
    scratch = [
        pltpu.VMEM(kv.shape, BF16),
        pltpu.VMEM((tokens, 2 * cols), BF16),
        pltpu.VMEM((tokens, 2 * cols), BF16),
        pltpu.VMEM((tokens, 2 * cols), BF16),
        pltpu.VMEM((tokens, 2 * cols), BF16),
        pltpu.VMEM((tokens, cols), F32),
        pltpu.VMEM((chunk, width), F32),
        pltpu.VMEM((chunk, width), BF16),
        dma,
        dma((3 * rows,)),
        dma((3 * rows,)),
    ] + Scatter.scratch(chunk, 1280, width)
    return pl.pallas_call(
        functools.partial(back_kernel, rows),
        out_shape=out_shape,
        in_specs=[pl.BlockSpec(memory_space=pltpu.SMEM)]
        + [VMEM] * 12
        + [pl.BlockSpec(memory_space=pl.ANY)],
        out_specs=[VMEM] * len(out_shape),
        scratch_shapes=scratch,
        compiler_params=pltpu.CompilerParams(
            collective_id=2, has_side_effects=True, vmem_limit_bytes=ROOM
        ),
    )(lengths, q, kv, mixed, lse, dmix, ffn, kept, cosines, sines, s_qkv, s_down, h1, cot)


COMMON = 176
PACKED = 224


class Total:
    def __init__(self, place, scratch):
        self.p = place
        self.send_buf, self.land, self.mine, self.across, self.held, *sems = scratch
        self.sems = sems
        p = place
        self.group = self.send_buf.shape[0]
        self.here = p.row * RING + p.seq
        self.peers = []
        for step in range(1, self.group):
            peer = lax.rem(self.here + step, self.group)
            self.peers.append((peer, (peer // RING, lax.rem(peer, RING), p.me)))

    @staticmethod
    def scratch(group):
        dma = pltpu.SemaphoreType.DMA
        return [
            pltpu.VMEM((group, PACKED, 128), BF16),
            pltpu.VMEM((group - 1, PACKED, 128), BF16),
            pltpu.VMEM((PACKED, 128), BF16),
            pltpu.VMEM((PARTS - 1, COMMON, 128), BF16),
            pltpu.VMEM((group, PACKED, 128), BF16),
            dma((group - 1,)),
            dma((group - 1,)),
            dma((PARTS - 1,)),
            dma((PARTS - 1,)),
            dma((group - 1,)),
            dma((group - 1,)),
        ]

    def greet(self):
        barrier = pltpu.get_barrier_semaphore()
        for _, place in self.peers:
            pl.semaphore_signal(barrier, inc=1, device_id=place, device_id_type=MESH)
        for step in range(1, PARTS):
            place = self.p.at(lax.rem(self.p.me + step, PARTS))
            pl.semaphore_signal(barrier, inc=1, device_id=place, device_id_type=MESH)
        pl.semaphore_wait(barrier, self.group + PARTS - 2)

    def copies(self, source, target, ends, first_sem):
        made = []
        for step, place in enumerate(ends):
            made.append(
                pltpu.make_async_remote_copy(
                    src_ref=source(step),
                    dst_ref=target(step),
                    send_sem=self.sems[first_sem].at[step],
                    recv_sem=self.sems[first_sem + 1].at[step],
                    device_id=place,
                    device_id_type=MESH,
                )
            )
            made[-1].start()
        return made

    def start(self):
        self.first = self.copies(
            lambda step: self.send_buf.at[self.peers[step][0]],
            lambda step: self.land.at[step],
            [place for _, place in self.peers],
            0,
        )

    def middle(self):
        for copy in self.first:
            copy.wait()
        total = self.send_buf[self.here].astype(F32)
        for step in range(self.group - 1):
            total += self.land[step].astype(F32)
        self.mine[...] = total.astype(BF16)
        ends = [self.p.at(lax.rem(self.p.me + step, PARTS)) for step in range(1, PARTS)]
        self.second = self.copies(
            lambda step: self.mine.at[:COMMON], lambda step: self.across.at[step], ends, 2
        )

    def late(self):
        for copy in self.second:
            copy.wait()
        shared = self.mine[:COMMON].astype(F32)
        for step in range(PARTS - 1):
            shared += self.across[step].astype(F32)
        self.held[self.here, :COMMON] = shared.astype(BF16)
        self.held[self.here, COMMON:] = self.mine[COMMON:]
        view = self.held.at[self.here]
        self.third = self.copies(
            lambda step: view, lambda step: view, [place for _, place in self.peers], 4
        )

    def end(self, out):
        for copy in self.third:
            copy.wait()
        for piece in range(self.group):
            out[:, piece * 128 : (piece + 1) * 128] = self.held[piece].astype(F32)


def close_kernel(
    cols,
    hpad,
    chunk_ref,
    dqkv_ref,
    vqkv,
    xn1,
    x_hbm,
    gain,
    dh1_ref,
    b_qkv,
    t_qkv,
    e_qkv,
    inv_n2,
    ga_gu,
    gb_gu,
    e_gu,
    ga_down,
    gb_down,
    ga_out,
    gb_out,
    e_out,
    e_down,
    av_out,
    av_down,
    out_ref,
    gx_ref,
    sum_ref,
    part,
    pack,
    x_own,
    total_own,
    local_sem,
    gather_s,
    gather_r,
    again_s,
    again_r,
    *scratch,
):
    tokens, width = xn1.shape
    chunk = tokens // PARTS
    p = Place()
    own = rows_of(p.me, chunk)
    totals = Total(p, scratch[:11])
    load = pltpu.make_async_copy(x_hbm.at[own], x_own, local_sem)
    load.start()
    totals.greet()

    @pl.loop(0, width // 256)
    def _(n):
        at = rows_of(n, 256)
        part[:, at] = nt(dqkv_ref[...], vqkv[at, :]).astype(BF16)

    scatter = Scatter(p, part, total_own, chunk, 1280, scratch[11:])
    scatter.start()
    out_ref[own, :] = chunk_ref[...]
    gather = Gather(p, out_ref, chunk, 768, (gather_s, gather_r))
    gather.start()

    ratio = e_qkv[...] * inv_n2[...]
    back_qkv = (b_qkv[...].astype(F32) * ratio).astype(BF16)
    t_one = nt(b_qkv[...], dqkv_ref[...]).astype(BF16)
    t_two = nt(t_qkv[...], xn1[...]).astype(BF16)
    for n in range(0, width, 512):
        at = slice(n, n + 512)
        pack[: 3 * RANK, at] = nn(t_one, xn1[:, at]) - nt(back_qkv, vqkv[at, :])
    gb = nn(t_two, dqkv_ref[...]) - nn(t_qkv[...], vqkv[...]) * ratio
    at = 3 * RANK
    for piece in (ga_gu, gb_out, gb_down, ga_out, av_out, av_down):
        pack[at : at + piece.shape[0], :] = piece[...]
        at += piece.shape[0]
    pack[at:, :] = jnp.zeros((PACKED - at, width), F32)
    pack[at : at + 1, :] = e_out[...]
    pack[at + 1 : at + 2, :] = e_down[...]
    gb_rows = slice(COMMON, COMMON + RANK)
    fold_rows = slice(COMMON + RANK, COMMON + 2 * RANK)
    e_row = COMMON + 2 * RANK
    for k in range(3):
        pack[gb_rows, k * cols : (k + 1) * cols] = gb[
            k * RANK : (k + 1) * RANK, k * cols : (k + 1) * cols
        ]
    pack[e_row : e_row + 1, : 3 * cols] = e_qkv[...]
    fits = width - 3 * cols
    pack[gb_rows, 3 * cols :] = gb_gu[:, :fits]
    pack[e_row : e_row + 1, 3 * cols :] = e_gu[:, :fits]
    rest = 2 * hpad - fits
    pack[fold_rows, :rest] = gb_gu[:, fits:]
    pack[e_row + 1 : e_row + 2, :rest] = e_gu[:, fits:]
    pack[fold_rows, rest : rest + hpad] = ga_down[...]
    for piece in range(width // 128):
        totals.send_buf[piece] = pack[:, piece * 128 : (piece + 1) * 128].astype(BF16)

    scatter.middle()
    totals.start()
    gather.middle()
    load.wait()
    x = x_own[...].astype(F32)
    inv1 = lax.rsqrt(jnp.mean(x * x, axis=-1, keepdims=True) + EPS)
    scatter.end()
    scaled = total_own[...] * gain[...]
    mean = jnp.mean(scaled * x, axis=-1, keepdims=True)
    grad = dh1_ref[...] + inv1 * (scaled - x * (inv1 * inv1 * mean))
    gx_ref[own, :] = grad.astype(BF16)
    again = Gather(p, gx_ref, chunk, 768, (again_s, again_r))
    again.start()
    totals.middle()
    gather.end()
    totals.late()
    again.middle()
    totals.end(sum_ref)
    again.end()


def close(cols, hpad, chunk_out, dqkv, vqkv, xn1, x, *rest):
    tokens, width = xn1.shape
    chunk = tokens // PARTS
    group = lax.axis_size("row") * lax.axis_size("seq")
    shape = jax.ShapeDtypeStruct
    dma = pltpu.SemaphoreType.DMA
    out_shape = (
        shape((tokens, width), BF16),
        shape((tokens, width), BF16),
        shape((PACKED, width), F32),
    )
    scratch = [
        pltpu.VMEM((tokens, width), BF16),
        pltpu.VMEM((PACKED, width), F32),
        pltpu.VMEM((chunk, width), BF16),
        pltpu.VMEM((chunk, width), F32),
        dma,
        dma((GATHER_SEMS,)),
        dma((GATHER_SEMS,)),
        dma((GATHER_SEMS,)),
        dma((GATHER_SEMS,)),
    ]
    scratch += Total.scratch(group) + Scatter.scratch(chunk, 1280, width)
    return pl.pallas_call(
        functools.partial(close_kernel, cols, hpad),
        out_shape=out_shape,
        in_specs=[VMEM] * 4 + [pl.BlockSpec(memory_space=pl.ANY)] + [VMEM] * len(rest),
        out_specs=[VMEM] * 3,
        scratch_shapes=scratch,
        compiler_params=pltpu.CompilerParams(
            collective_id=3, has_side_effects=True, vmem_limit_bytes=ROOM
        ),
    )(chunk_out, dqkv, vqkv, xn1, x, *rest)


def three_terms(left, right):
    def split(a):
        high = a.astype(BF16)
        return high, (a - high.astype(F32)).astype(BF16)

    left_high, left_low = split(left)
    right_high, right_low = split(right)
    return (
        jnp.concatenate([left_high, left_low, left_high], axis=0),
        jnp.concatenate([right_high, right_high, right_low], axis=0),
    )


def front_kernel(
    rows,
    lengths,
    gain,
    m_qkv,
    t_qkv,
    b_qkv,
    t_out,
    b_out,
    t_gu,
    b_gu,
    t_down,
    b_down,
    cosines,
    sines,
    x_hbm,
    wqkv_hbm,
    wout_hbm,
    wgu_hbm,
    wdown_hbm,
    q_ref,
    kept_ref,
    mixed_ref,
    lse_ref,
    n2_qkv,
    n2_gu,
    n2_model,
    at_out,
    av_out,
    av_down,
    xn1_hbm,
    vqkv_hbm,
    vout_hbm,
    vgu_hbm,
    vdown_hbm,
    kv_hbm,
    x_ref,
    wqkv,
    wout,
    wgu,
    wdown,
    xn1,
    vqkv,
    vout,
    vgu,
    vdown,
    kv,
    acc,
    top,
    weight,
    squares,
    land_squares,
    at_mine,
    load_sems,
    store_sems,
    gather_s,
    gather_r,
    share_s,
    share_r,
    kv_s,
    kv_r,
    square_s,
    square_r,
    at_s,
    at_r,
):
    tokens, width = x_ref.shape
    span = tokens // rows
    cols = q_ref.shape[1]
    heads = cols // HD
    hidden = wdown.shape[0]
    hpad = vdown.shape[0]
    p = Place()
    core = lax.rem(p.seq, 2)
    upper = p.seq // 2
    sibling = upper * 2 + 1 - core
    loads = []
    pairs = [(wout_hbm, wout), (wqkv_hbm, wqkv), (x_hbm, x_ref), (wdown_hbm, wdown), (wgu_hbm, wgu)]
    for i, (src, dst) in enumerate(pairs):
        loads.append(pltpu.make_async_copy(src, dst, load_sems.at[i]))
        loads[-1].start()
    barrier = pltpu.get_barrier_semaphore()
    for step in range(1, PARTS):
        place = p.at(lax.rem(p.me + step, PARTS))
        pl.semaphore_signal(barrier, inc=1, device_id=place, device_id_type=MESH)
    for seq in (sibling, (1 - upper) * 2 + core):
        pl.semaphore_signal(barrier, inc=1, device_id=(p.row, seq, p.me), device_id_type=MESH)

    left, right = three_terms(t_out[...], b_out[...])
    loads[0].wait()
    squares[...] = jnp.zeros_like(squares)
    for n in range(0, width, 512):
        at = slice(n, n + 512)
        v = wout[:, at].astype(F32) + SCALE * tn(left, right[:, at])
        vout[:, at] = v.astype(BF16)
        squares[0:1, at] = jnp.sum(v * v, axis=0, keepdims=True)
    at_mine[...] = t_out[...].astype(BF16)
    my_cols = rows_of(p.me, cols)
    at_out[:, my_cols] = t_out[...].astype(BF16)
    pl.semaphore_wait(barrier, PARTS + 1)
    settle = pltpu.make_async_copy(vout, vout_hbm.at[my_cols], store_sems.at[0])
    settle.start()
    settle.wait()
    gather = Gather(p, vout_hbm, cols // 2, 1536, (gather_s, gather_r), cols, core)
    gather.start()
    at_copies = []
    for step in range(1, PARTS):
        to = lax.rem(p.me + step, PARTS)
        at_copies.append(p.send(at_mine, at_out.at[:, my_cols], (at_s, at_r), step - 1, to))

    loads[1].wait()
    for k in range(3):
        left, right = three_terms(t_qkv[k], b_qkv[k])
        at = slice(k * cols, (k + 1) * cols)
        total = jnp.zeros((1, cols), F32)
        for n in range(0, width, 512):
            part = slice(n, n + 512)
            v = wqkv[k, part, :].astype(F32) + SCALE * tn(left[:, part], right)
            vqkv[part, at] = v.astype(BF16)
            total += jnp.sum(v * v, axis=0, keepdims=True)
        n2_qkv[:, at] = total
    loads[2].wait()

    @pl.loop(0, PARTS)
    def _(i):
        part = rows_of(i, tokens // PARTS)
        x = x_ref[part, :].astype(F32)
        inv = lax.rsqrt(jnp.mean(x * x, axis=-1, keepdims=True) + EPS)
        xn1[part, :] = (x * inv * gain[...]).astype(BF16)

    stores = [
        pltpu.make_async_copy(vqkv, vqkv_hbm, store_sems.at[1]),
        pltpu.make_async_copy(xn1, xn1_hbm, store_sems.at[2]),
    ]
    for copy in stores:
        copy.start()

    def over(source, index, seq):
        return pltpu.make_async_remote_copy(
            src_ref=source,
            dst_ref=source,
            send_sem=kv_s.at[index],
            recv_sem=kv_r.at[index],
            device_id=(p.row, seq, p.me),
            device_id_type=MESH,
        )

    to_sib, to_far, onward = [], [], []
    for r in range(rows):
        part = slice(r * span, (r + 1) * span)
        to_sib.append(over(kv.at[p.seq, part], r, sibling))
        to_far.append(over(kv.at[p.seq, part], rows + r, 2 + core))
        onward.append(over(kv.at[core, part], 2 * rows + r, sibling))
    scales = m_qkv[...] * lax.rsqrt(n2_qkv[...])
    for r in range(rows):
        part = slice(r * span, (r + 1) * span)
        for k in (1, 2, 0):
            at = slice(k * cols, (k + 1) * cols)
            y = nn(xn1[part, :], vqkv[:, at]) * scales[:, at]
            kept_ref[part, at] = y.astype(BF16)
            if k < 2:
                y = jnp.concatenate(
                    [
                        turn(y[:, h * HD : (h + 1) * HD], cosines[...], sines[...])
                        for h in range(heads)
                    ],
                    axis=1,
                )
            if k == 0:
                q_ref[part, :] = y.astype(BF16)
            else:
                kv[p.seq, part, (k - 1) * cols : k * cols] = y.astype(BF16)
            if k == 2:

                @pl.when(upper == 0)
                def _(r=r):
                    to_far[r].start()

                @pl.when(core == 0)
                def _(r=r):
                    to_sib[r].start()

    query_pos = p.seq * span + lax.broadcasted_iota(jnp.int32, (span, span), 0)
    key_pos = lax.broadcasted_iota(jnp.int32, (span, span), 1)

    def absorb(r, j, fresh=False):
        part = slice(r * span, (r + 1) * span)
        for head in range(heads):
            at = slice(head * HD, (head + 1) * HD)
            to = slice(cols + head * HD, cols + (head + 1) * HD)
            one = (slice(None), slice(r * heads + head, r * heads + head + 1))
            scores = scores_of(
                q_ref[part, at], kv[j, part, at], query_pos, key_pos, j * span, lengths[r]
            )
            best = jnp.max(scores, axis=-1, keepdims=True)
            if not fresh:
                best = jnp.maximum(best, top[one])
            expo = jnp.exp(scores - best)
            summed = jnp.sum(expo, axis=-1, keepdims=True)
            mixed = nn(expo.astype(BF16), kv[j, part, to])
            if not fresh:
                fade = jnp.exp(top[one] - best)
                summed += weight[one] * fade
                mixed += acc[part, at] * fade
            top[one] = best
            weight[one] = summed
            acc[part, at] = mixed

    for r in range(rows):
        absorb(r, p.seq, True)

    loads[3].wait()
    vdown[hidden:, :] = jnp.zeros((hpad - hidden, width), BF16)
    left, right = three_terms(t_down[...], b_down[...])
    for n in range(0, width, 512):
        at = slice(n, n + 512)
        v = wdown[:, at].astype(F32) + SCALE * tn(left, right[:, at])
        vdown[:hidden, at] = v.astype(BF16)
        squares[1:2, at] = jnp.sum(v * v, axis=0, keepdims=True)
    square_copies = []
    for step in range(1, PARTS):
        to = lax.rem(p.me + step, PARTS)
        square_copies.append(
            p.send(squares, land_squares.at[step - 1], (square_s, square_r), step - 1, to)
        )
    stores.append(pltpu.make_async_copy(vdown, vdown_hbm, store_sems.at[3]))
    stores[-1].start()
    gather.middle()
    shares = []

    def share(plane, steps):
        for step in steps:
            view = gather.view(plane * RING + p.side(step), "all")
            index = len(shares)
            shares.append(
                pltpu.make_async_remote_copy(
                    src_ref=view,
                    dst_ref=view,
                    send_sem=share_s.at[index],
                    recv_sem=share_r.at[index],
                    device_id=(p.row, sibling, p.me),
                    device_id_type=MESH,
                )
            )

            shares[-1].start()

    loads[4].wait()
    ones = jnp.ones((8, width), BF16)
    for k in range(2):
        left, right = three_terms(b_gu[k], t_gu[k])
        base = k * hpad
        vgu[base + hidden : base + hpad, :] = jnp.zeros((hpad - hidden, width), BF16)
        n2_gu[:, base + hidden : base + hpad] = jnp.ones((1, hpad - hidden), F32)
        for n in range(0, hidden, 128):
            size = min(128, hidden - n)
            v = wgu[k, n : n + size, :].astype(F32) + SCALE * tn(left[:, n : n + size], right)
            vgu[base + n : base + n + size, :] = v.astype(BF16)
            n2_gu[:, base + n : base + n + size] = nt(ones, (v * v).astype(BF16))[:1]
    stores.append(pltpu.make_async_copy(vgu, vgu_hbm, store_sems.at[4]))
    stores[-1].start()

    @pl.when(core == 1)
    def _():
        for r in range(rows):
            to_sib[r].wait_recv()
            absorb(r, p.seq - 1)

    @pl.when(upper == 1)
    def _():
        for r in range(rows):
            to_far[r].wait_recv()
            onward[r].start()
            absorb(r, core)
        for r in range(rows):
            onward[r].wait_recv()
            absorb(r, 1 - core)

    @pl.loop(p.seq + 1, kv.shape[0])
    def _(j):
        kv[j] = jnp.zeros(kv.shape[1:], BF16)

    stores.append(pltpu.make_async_copy(kv, kv_hbm, store_sems.at[5]))
    stores[-1].start()
    for r in range(rows):
        part = slice(r * span, (r + 1) * span)
        for head in range(heads):
            at = slice(head * HD, (head + 1) * HD)
            one = (slice(None), slice(r * heads + head, r * heads + head + 1))
            mixed_ref[part, at] = (acc[part, at] / weight[one]).astype(BF16)
            lse_ref[part, at] = jnp.broadcast_to(top[one] + jnp.log(weight[one]), (span, HD))
    av_out[...] = nn(at_mine[...], vout[...])
    at_down = t_down[...].astype(BF16)
    av_down[...] = nn(at_down, vdown[:hidden, :])
    share(p.z, (1, 2, 3))
    gather.end()
    share(p.far, (0, 1, 2, 3))
    for copy in square_copies:
        copy.wait_recv()
    total = squares[...]
    for step in range(PARTS - 1):
        total += land_squares[step]
    n2_model[...] = total
    for copy in at_copies + shares:
        copy.wait_recv()
    for copy in at_copies + square_copies + shares:
        copy.wait_send()
    for copy in stores:
        copy.wait()

    @pl.when(upper == 0)
    def _():
        for r in range(rows):
            to_far[r].wait_send()

    @pl.when(core == 0)
    def _():
        for r in range(rows):
            to_sib[r].wait_send()

    @pl.when(upper == 1)
    def _():
        for r in range(rows):
            onward[r].wait_send()


def front(rows, seqs, lengths, gain, m_qkv, t_qkv, b_qkv, t_out, b_out, t_gu, b_gu, t_down, b_down, cosines, sines, x, w_qkv, w_out, w_gu, w_down):
    tokens, width = x.shape
    cols = w_qkv.shape[2]
    heads = cols // HD
    hidden = w_down.shape[0]
    hpad = pad_to(hidden)
    span = tokens // rows
    shape = jax.ShapeDtypeStruct
    dma = pltpu.SemaphoreType.DMA
    vmem = pltpu.VMEM
    out_shape = (
        shape((tokens, cols), BF16),
        shape((tokens, 3 * cols), BF16),
        shape((tokens, cols), BF16),
        shape((tokens, cols), F32),
        shape((1, 3 * cols), F32),
        shape((1, 2 * hpad), F32),
        shape((8, width), F32),
        shape((RANK, width), BF16),
        shape((RANK, width), F32),
        shape((RANK, width), F32),
        shape((tokens, width), BF16),
        shape((width, 3 * cols), BF16),
        shape((PARTS * cols, width), BF16),
        shape((2 * hpad, width), BF16),
        shape((hpad, width), BF16),
        shape((seqs, tokens, 2 * cols), BF16),
    )
    scratch = [
        vmem((tokens, width), BF16),
        vmem((3, width, cols), BF16),
        vmem((cols, width), BF16),
        vmem((2, hidden, width), BF16),
        vmem((hidden, width), BF16),
        vmem((tokens, width), BF16),
        vmem((width, 3 * cols), BF16),
        vmem((cols, width), BF16),
        vmem((2 * hpad, width), BF16),
        vmem((hpad, width), BF16),
        vmem((seqs, tokens, 2 * cols), BF16),
        vmem((tokens, cols), F32),
        vmem((span, rows * heads), F32),
        vmem((span, rows * heads), F32),
        vmem((8, width), F32),
        vmem((PARTS - 1, 8, width), F32),
        vmem((RANK, cols), BF16),
        dma((5,)),
        dma((6,)),
        dma((GATHER_SEMS,)),
        dma((GATHER_SEMS,)),
        dma((PARTS,)),
        dma((PARTS,)),
        dma((3 * rows,)),
        dma((3 * rows,)),
    ] + [dma((PARTS - 1,))] * 4
    anywhere = pl.BlockSpec(memory_space=pl.ANY)
    return pl.pallas_call(
        functools.partial(front_kernel, rows),
        out_shape=out_shape,
        in_specs=[pl.BlockSpec(memory_space=pltpu.SMEM)] + [VMEM] * 12 + [anywhere] * 5,
        out_specs=[VMEM] * 10 + [anywhere] * 6,
        scratch_shapes=scratch,
        compiler_params=pltpu.CompilerParams(
            collective_id=4, has_side_effects=True, vmem_limit_bytes=ROOM
        ),
    )(lengths, gain, m_qkv, t_qkv, b_qkv, t_out, b_out, t_gu, b_gu, t_down, b_down, cosines, sines, x, w_qkv, w_out, w_gu, w_down)


def shards(
    layer_input,
    cotangent,
    lengths,
    gain_attn,
    gain_ffn,
    w_qkv,
    m_qkv,
    a_qkv,
    b_qkv,
    w_out,
    m_out,
    a_out,
    b_out,
    w_gu,
    m_gu,
    a_gu,
    b_gu,
    w_down,
    m_down,
    a_down,
    b_down,
):
    rows, span, width = layer_input.shape
    seqs = lax.axis_size("seq")
    me = lax.axis_index("head")
    tokens = rows * span
    cols = w_qkv.shape[2]
    hidden = w_gu.shape[2]
    hpad = pad_to(hidden)

    low = lambda a: a.astype(BF16)
    positions = lax.axis_index("seq") * span + jnp.arange(span, dtype=jnp.int32)
    freqs = ROPE_BASE ** (-jnp.arange(HD // 2, dtype=F32) * 2.0 / HD)
    turned = positions.astype(F32)[:, None] * freqs[None, :]
    cosines = jnp.concatenate([jnp.cos(turned)] * 2, axis=1)
    sines = jnp.concatenate([-jnp.sin(turned), jnp.sin(turned)], axis=1)
    x = layer_input.reshape(tokens, width)
    t_qkv, t_gu = a_qkv.transpose(0, 2, 1), a_gu.transpose(0, 2, 1)
    t_out, t_down = a_out.T, a_down.T
    (
        query,
        kept,
        mixed,
        lse,
        n2_qkv,
        n2_gu,
        n2_model,
        full_t_out,
        av_out,
        av_down,
        normed1,
        vb_qkv,
        full_out,
        vb_gu,
        vb_down,
        pairs,
    ) = front(
        rows,
        seqs,
        lengths,
        gain_attn[None],
        m_qkv.reshape(1, 3 * cols),
        t_qkv,
        b_qkv,
        t_out,
        b_out,
        t_gu,
        b_gu,
        t_down,
        b_down,
        cosines,
        sines,
        x,
        w_qkv,
        w_out,
        w_gu.transpose(0, 2, 1),
        w_down,
    )
    widen = ((0, 0), (0, hpad - hidden))
    t_down_pad = jnp.pad(low(t_down), widen)
    spread = lax.axis_size("row") * seqs
    av_out, av_down = av_out / spread, av_down / spread
    s_qkv = m_qkv.reshape(1, 3 * cols) * lax.rsqrt(n2_qkv)
    s_gu = jnp.pad(m_gu, widen).reshape(1, 2 * hpad) * lax.rsqrt(n2_gu)
    n2_out, n2_down = n2_model[0], n2_model[1]
    s_out = m_out * lax.rsqrt(n2_out)
    s_down = m_down * lax.rsqrt(n2_down)
    b_gu_pad = jnp.concatenate([jnp.pad(low(b_gu[p]), widen) for p in range(2)], axis=1)

    cot = cotangent.reshape(tokens, width)
    (
        ffn_part,
        hidden1,
        grad_h1,
        grad_mixed,
        ga_gu,
        gb_gu,
        e_gu,
        ga_down,
        gb_down,
        ga_out,
        gb_out,
        e_out,
    ) = feed(
        span,
        lengths,
        mixed,
        s_out[None],
        gain_ffn[None],
        s_gu,
        s_down[None],
        b_gu_pad,
        low(t_gu).reshape(2 * RANK, width),
        t_down_pad,
        low(b_down),
        low(b_out),
        full_t_out,
        x,
        cot,
        full_out,
        vb_gu,
        vb_down,
    )
    dqkv, e_qkv, chunk_out, e_down = back(
        rows,
        lengths,
        query,
        pairs,
        mixed,
        lse,
        grad_mixed,
        ffn_part,
        kept,
        cosines,
        sines,
        s_qkv,
        s_down[None],
        hidden1,
        cot,
    )
    ratio_gu = e_gu / n2_gu
    back_gu = low(b_gu_pad.astype(F32) * ratio_gu)
    left_gu = []
    ga_rows = []
    for p in range(2):
        part = slice(p * hpad, (p + 1) * hpad)
        ga_rows.append(ga_gu[p * RANK : (p + 1) * RANK] - nn(back_gu[:, part], vb_gu[part]))
        left_gu.append(nt(low(t_gu[p]), vb_gu[part]))
    ga_gu = jnp.concatenate(ga_rows)
    gb_gu = gb_gu - jnp.concatenate(left_gu, axis=1) * ratio_gu
    diag = jnp.zeros((3 * RANK, 3 * cols), BF16)
    for p in range(3):
        diag = diag.at[p * RANK : (p + 1) * RANK, p * cols : (p + 1) * cols].set(low(b_qkv[p]))
    output, grad_x, summed = close(
        cols,
        hpad,
        chunk_out,
        dqkv,
        vb_qkv,
        normed1,
        x,
        gain_attn[None],
        grad_h1,
        diag,
        low(t_qkv).reshape(3 * RANK, width),
        e_qkv,
        1.0 / n2_qkv,
        ga_gu,
        gb_gu,
        e_gu,
        ga_down,
        gb_down,
        ga_out,
        gb_out,
        e_out,
        e_down,
        av_out,
        av_down,
    )
    cut = lambda first, count: summed[first * RANK : (first + count) * RANK]
    ga_qkv = cut(0, 3).reshape(3, RANK, width).transpose(0, 2, 1)
    ga_gu = cut(3, 2).reshape(2, RANK, width).transpose(0, 2, 1)
    gb_out, gb_down, ga_out = cut(5, 1), cut(6, 1), cut(7, 1)
    av_out, av_down = cut(8, 1), cut(9, 1)
    e_out, e_down = summed[10 * RANK], summed[10 * RANK + 1]
    at = COMMON
    own_gb = jnp.concatenate([summed[at : at + RANK], summed[at + RANK : at + 2 * RANK]], axis=1)
    at += 2 * RANK
    own_e = jnp.concatenate([summed[at], summed[at + 1]])
    gb_qkv = jnp.stack([own_gb[:, p * cols : (p + 1) * cols] for p in range(3)])
    at = 3 * cols
    gb_gu = jnp.stack([own_gb[:, at + p * hpad : at + p * hpad + hidden] for p in range(2)])
    e_qkv = own_e[:at]
    e_gu = jnp.stack([own_e[at + p * hpad : at + p * hpad + hidden] for p in range(2)])
    ga_down = own_gb[:, at + 2 * hpad : at + 2 * hpad + hidden]
    back_out = low(b_out * (e_out / n2_out))
    back_down = low(b_down * (e_down / n2_down))
    vb_out = lax.dynamic_slice_in_dim(full_out, me * cols, cols, axis=0)
    ga_out = lax.dynamic_slice_in_dim(ga_out, me * cols, cols, axis=1) - nt(back_out, vb_out)
    ga_down = ga_down - nt(back_down, vb_down)[:, :hidden]
    gb_out = gb_out - av_out * (e_out / n2_out)
    gb_down = gb_down - av_down * (e_down / n2_down)
    return (
        output.reshape(rows, span, width),
        grad_x.reshape(rows, span, width),
        e_qkv.reshape(3, cols) / m_qkv,
        SCALE * ga_qkv,
        SCALE * gb_qkv,
        e_out / m_out,
        SCALE * ga_out.T,
        SCALE * gb_out,
        e_gu / m_gu,
        SCALE * ga_gu,
        SCALE * gb_gu,
        e_down / m_down,
        SCALE * ga_down.T,
        SCALE * gb_down,
    )


def solution(mesh):
    placed = (
        P("row", "seq", None),
        P("row", "seq", None),
        P("row"),
        P(),
        P(),
        P(None, None, "head"),
        P(None, "head"),
        P(),
        P(None, None, "head"),
        P("head", None),
        P(),
        P("head", None),
        P(),
        P(None, None, "head"),
        P(None, "head"),
        P(),
        P(None, None, "head"),
        P("head", None),
        P(),
        P("head", None),
        P(),
    )
    return jax.shard_map(
        shards,
        mesh=mesh,
        in_specs=placed,
        out_specs=(
            P("row", "seq", None),
            P("row", "seq", None),
            P(None, "head"),
            P(),
            P(None, None, "head"),
            P(),
            P("head", None),
            P(),
            P(None, "head"),
            P(),
            P(None, None, "head"),
            P(),
            P("head", None),
            P(),
        ),
        check_vma=False,
    )
```

```python
import functools

import jax
import jax.numpy as jnp
from jax import lax
from jax.experimental import pallas as pl
from jax.experimental.pallas import tpu as pltpu
from jax.sharding import PartitionSpec as P

HD = 128
RANK = 16
SCALE = 2.0
EPS = 1e-05
ROPE_BASE = 10000.0
MASKED = -1000000000.0
F32 = jnp.float32
BF16 = jnp.bfloat16


def pad_to(n, m=256):
    return -(-n // m) * m


def mm(a, b, dims):
    return lax.dot_general(a, b, (dims, ((), ())), preferred_element_type=F32)


def nn(a, b):
    return mm(a, b, ((1,), (0,)))


def nt(a, b):
    return mm(a, b, ((1,), (1,)))


def tn(a, b):
    return mm(a, b, ((0,), (0,)))


MESH = pl.DeviceIdType.MESH
VMEM = pl.BlockSpec(memory_space=pltpu.VMEM)
ROOM = 60 * 2**20
RING = 4
PARTS = 8


class Place:
    def __init__(self):
        self.row, self.seq, self.me = (lax.axis_index(n) for n in ("row", "seq", "head"))
        self.y = lax.rem(self.me, RING)
        self.z = self.me // RING
        self.far = 1 - self.z
        self.cross = self.far * RING + self.y

    def side(self, step):
        return lax.rem(self.y + step + RING, RING)

    def at(self, head):
        return (self.row, self.seq, head)

    def greet(self):
        barrier = pltpu.get_barrier_semaphore()
        for step in range(1, PARTS):
            pl.semaphore_signal(
                barrier, inc=1, device_id=self.at(lax.rem(self.me + step, PARTS)), device_id_type=MESH
            )
        pl.semaphore_wait(barrier, PARTS - 1)

    def send(self, source, target, sems, index, head):
        copy = pltpu.make_async_remote_copy(
            src_ref=source,
            dst_ref=target,
            send_sem=sems[0].at[index],
            recv_sem=sems[1].at[index],
            device_id=self.at(head),
            device_id_type=MESH,
        )
        copy.start()
        return copy


def rows_of(index, count):
    return pl.ds(pl.multiple_of(index * count, count), count)


EVEN = {"a": (0, 640, 1152), "b": (1152, 1536, 2048)}
RING_FIRST = {"a": (0, 768, 1536), "b": (1536, 1792, 2048)}
UP, DOWN = 1, -1


def span_of(spans, which, half=None):
    first, split, last = spans[which]
    if half == UP:
        last = split
    if half == DOWN:
        first = split
    return first, last


class Gather:
    def __init__(self, place, buf, chunk, sems, spans, stride=None, offset=0):
        self.place, self.buf, self.chunk, self.sems, self.spans = place, buf, chunk, sems, spans
        self.stride, self.offset = stride or chunk, offset
        self.sent = []

    def view(self, head, which=None, half=None):
        first = head * self.stride + self.offset * self.chunk
        rows = pl.ds(pl.multiple_of(first, self.chunk), self.chunk)
        if which is None:
            return self.buf.at[rows]
        first, last = span_of(self.spans, which, half)
        return self.buf.at[rows, first:last]

    def pass_on(self, head, which, half, index, to):
        view = self.view(head, which, half)
        copy = self.place.send(view, view, self.sems, index, to)
        self.sent.append(copy)
        return copy

    def ring(self, head, which, index):
        p = self.place
        return {
            way: self.pass_on(head, which, None, index + i, p.z * RING + p.side(way))
            for i, way in enumerate((UP, DOWN))
        }

    def relay(self, copies, plane, which, index, then=None):
        p = self.place
        made = []
        for i, way in enumerate((UP, DOWN)):
            copies[way].wait_recv()
            head = plane * RING + p.side(-way)
            made.append(self.pass_on(head, which, way, index + i, p.z * RING + p.side(way)))
            if then is not None:
                then(head, i)
        return made

    def start(self):
        p = self.place
        self.rest = []
        self.a_cross = self.pass_on(p.me, "a", None, 0, p.cross)
        self.b_ring = self.ring(p.me, "b", 6)
        self.a_ring = self.ring(p.me, "a", 8)
        self.rest.append(self.pass_on(p.me, "b", None, 1, p.cross))

    def first(self):
        p = self.place

        def across(head, i):
            self.rest.append(self.pass_on(head, "b", None, 2 + i, p.cross))

        self.b_relay = self.relay(self.b_ring, p.z, "b", 10, across)
        self.a_cross.wait_recv()
        self.far_ring = self.ring(p.cross, "a", 14)
        self.a_relay = self.relay(self.a_ring, p.z, "a", 12)

    def middle(self):
        p = self.place
        opposite = p.z * RING + p.side(2)
        for i, way in enumerate((UP, DOWN)):
            self.b_relay[i].wait_recv()
            self.rest.append(self.pass_on(opposite, "b", way, 4 + i, p.cross))
        for copy in self.a_relay:
            copy.wait_recv()

    def late(self):
        self.rest += self.relay(self.far_ring, self.place.far, "a", 16)

    def end(self):
        for copy in self.rest:
            copy.wait_recv()
        for copy in self.sent:
            copy.wait_send()


GATHER_SEMS = 18


class Scatter:
    def __init__(self, place, src, out, chunk, spans, scratch):
        self.place, self.src, self.out, self.chunk = place, src, out, chunk
        self.spans = spans
        self.cut = spans["a"][2]
        (
            self.far_b,
            self.hold_b,
            self.relay_b,
            self.land_b,
            self.hold_a,
            self.relay_a,
            self.land_a,
            self.hold_far,
            self.land_far,
            s,
            r,
        ) = scratch
        self.sems = (s, r)
        self.sent = []
        self.a_relay = [None, None]

    @staticmethod
    def scratch(chunk, width, spans):
        a = spans["a"][2]
        b = width - a
        return [
            pltpu.VMEM((RING, chunk, b), BF16),
            pltpu.VMEM((3, chunk, b), BF16),
            pltpu.VMEM((chunk, b), BF16),
            pltpu.VMEM((2, chunk, b), BF16),
            pltpu.VMEM((2, 2, chunk, a), BF16),
            pltpu.VMEM((2, chunk, a), BF16),
            pltpu.VMEM((2, 2, chunk, a), BF16),
            pltpu.VMEM((chunk, a), BF16),
            pltpu.VMEM((chunk, a), BF16),
            pltpu.SemaphoreType.DMA((17,)),
            pltpu.SemaphoreType.DMA((17,)),
        ]

    def send(self, source, target, index, head):
        copy = self.place.send(source, target, self.sems, index, head)
        self.sent.append(copy)
        return copy

    def mine(self, plane, y, which):
        first, last = span_of(self.spans, which)
        return self.src[rows_of(plane * RING + y, self.chunk), first:last].astype(F32)

    def within(self, which, half):
        base = self.spans[which][0]
        first, last = span_of(self.spans, which, half)
        return slice(first - base, last - base)

    def opposite(self, source, target, which, index):
        p = self.place
        made = {}
        for i, half in enumerate((UP, DOWN)):
            part = self.within(which, half)
            made[half] = self.send(
                source(half, part), target.at[:, part], index + i, p.z * RING + p.side(-half)
            )
        return made

    def start_b(self):
        p = self.place
        self.across = []
        for i, step in enumerate((2, DOWN, UP, 0)):
            view = self.src.at[rows_of(p.far * RING + p.side(step), self.chunk), self.cut :]
            self.across.append(self.send(view, self.far_b.at[i], i, p.cross))

    def start_a(self, k):
        p = self.place
        plane = p.z if k else p.far
        rows = rows_of(plane * RING + p.side(2), self.chunk)

        def source(half, part):
            return self.src.at[rows, part]

        self.a_relay[k] = self.opposite(source, self.relay_a.at[k], "a", 5 + 2 * k)

    def first(self):
        p = self.place
        self.a_direct = []
        for k, plane in enumerate((p.far, p.z)):
            made = {}
            for i, way in enumerate((DOWN, UP)):
                half = -way
                part = self.within("a", half)
                self.a_relay[k][half].wait_recv()
                self.hold_a[k, i] = self.mine(plane, p.side(way), "a").astype(BF16)
                self.hold_a[k, i, :, part] = (
                    self.hold_a[k, i, :, part].astype(F32) + self.relay_a[k, :, part].astype(F32)
                ).astype(BF16)
                made[way] = self.send(
                    self.hold_a.at[k, i],
                    self.land_a.at[k, i],
                    9 + 2 * k + i,
                    p.z * RING + p.side(way),
                )
            self.a_direct.append(made)
        self.across[0].wait_recv()
        total = self.mine(p.z, p.side(2), "b") + self.far_b[0].astype(F32)
        self.hold_b[2] = total.astype(BF16)

        def source(half, part):
            return self.hold_b.at[2, :, part]

        self.b_relay = self.opposite(source, self.relay_b, "b", 13)

    def middle(self):
        p = self.place
        total = self.mine(p.far, p.y, "a")
        for i, way in enumerate((DOWN, UP)):
            self.a_direct[0][way].wait_recv()
            total += self.land_a[0, i].astype(F32)
        self.hold_far[...] = total.astype(BF16)
        self.last = self.send(self.hold_far, self.land_far, 4, p.cross)
        self.b_direct = []
        for i, way in enumerate((DOWN, UP)):
            half = -way
            part = self.within("b", half)
            self.across[1 + i].wait_recv()
            total = self.mine(p.z, p.side(way), "b") + self.far_b[1 + i].astype(F32)
            self.b_relay[half].wait_recv()
            self.hold_b[i] = total.astype(BF16)
            self.hold_b[i, :, part] = (
                total[:, part] + self.relay_b[:, part].astype(F32)
            ).astype(BF16)
            self.b_direct.append(
                self.send(
                    self.hold_b.at[i], self.land_b.at[i], 15 + i, p.z * RING + p.side(way)
                )
            )

    def end(self):
        p = self.place
        total = self.mine(p.z, p.y, "a")
        for i, way in enumerate((DOWN, UP)):
            self.a_direct[1][way].wait_recv()
            total += self.land_a[1, i].astype(F32)
        self.across[3].wait_recv()
        rest = self.mine(p.z, p.y, "b") + self.far_b[3].astype(F32)
        for i in range(2):
            self.b_direct[i].wait_recv()
            rest += self.land_b[i].astype(F32)
        self.out[:, self.cut :] = rest
        self.last.wait_recv()
        self.out[:, : self.cut] = total + self.land_far[...].astype(F32)
        for copy in self.sent:
            copy.wait_send()


def feed_kernel(
    span,
    lengths,
    mixed_ref,
    s_out,
    gain,
    s_gu,
    s_down,
    n2_gu,
    b_gu_raw,
    t_gu,
    t_down,
    b_down,
    b_out,
    at_out,
    av_out,
    av_down,
    x_hbm,
    cot_hbm,
    vout_hbm,
    vgu_hbm,
    vdown_hbm,
    h1_ref,
    dh1_ref,
    dmix_ref,
    pack,
    ffn_hbm,
    ffn_ref,
    vout,
    vgu,
    vdown,
    dys,
    xn2,
    part,
    dhid,
    hid,
    dgu,
    x_own,
    mixed_own,
    dmix_own,
    attn,
    sum_own,
    b_gu,
    at_down,
    local_sems,
    swap_s,
    swap_r,
    back_s,
    back_r,
    gather_s,
    gather_r,
    *scatter_scratch,
):
    tokens, width = xn2.shape
    chunk = tokens // PARTS
    block = tokens // 2
    cols = mixed_ref.shape[1]
    hpad = hid.shape[1]
    tile = 256
    p = Place()
    own = rows_of(p.me, chunk)
    loads = []
    for i, (src, dst) in enumerate(
        [
            (cot_hbm, dys),
            (vdown_hbm, vdown),
            (x_hbm.at[own], x_own),
            (vout_hbm, vout),
            (vgu_hbm, vgu),
        ]
    ):
        loads.append(pltpu.make_async_copy(src, dst, local_sems.at[i]))
        loads[-1].start()
    p.greet()

    my_cols = rows_of(p.me, cols)
    swaps = []
    for step in range(1, PARTS):
        to = lax.rem(p.me + step, PARTS)
        swaps.append(
            p.send(
                mixed_ref.at[rows_of(to, chunk)],
                mixed_own.at[:, my_cols],
                (swap_s, swap_r),
                step - 1,
                to,
            )
        )
    mixed_own[:, my_cols] = mixed_ref[own, :]

    hidden = t_down.shape[1]
    b_gu[...] = jnp.zeros_like(b_gu)
    at_down[...] = jnp.zeros_like(at_down)
    for k in range(2):
        b_gu[:, k * hpad : k * hpad + hidden] = b_gu_raw[k].astype(BF16)
    at_down[:, :hidden] = t_down[...].astype(BF16)
    loads[0].wait()
    loads[1].wait()
    seq = lax.axis_index("seq")

    @pl.loop(0, PARTS)
    def _(i):
        rows = rows_of(i, chunk)
        base = lax.rem(i * chunk, span)
        length = lengths[0]
        for r in range(1, tokens // span):
            length = jnp.where(i * chunk >= r * span, lengths[r], length)
        pos = seq * span + base + lax.broadcasted_iota(jnp.int32, (chunk, 1), 0)
        live = (pos < length).astype(F32)
        dys[rows, :] = (dys[rows, :].astype(F32) * live * s_down[...]).astype(BF16)

    def back_hidden(half):
        rows = slice(half * block, (half + 1) * block)

        @pl.loop(0, hpad // tile)
        def _(n):
            units = rows_of(n, tile)
            dhid[rows, units] = nt(dys[rows, :], vdown[units, :]).astype(BF16)

    back_hidden(0)

    for copy in swaps:
        copy.wait_recv()
    loads[2].wait()
    loads[3].wait()

    @pl.loop(0, width // 512)
    def _(n):
        part_cols = rows_of(n, 512)
        attn[:, part_cols] = nn(mixed_own[...], vout[:, part_cols]) * s_out[:, part_cols]

    h1_ref[...] = x_own[...].astype(F32) + attn[...]
    inv2 = lax.rsqrt(jnp.mean(h1_ref[...] * h1_ref[...], axis=-1, keepdims=True) + EPS)
    xn2[own, :] = (h1_ref[...] * inv2 * gain[...]).astype(BF16)
    gather = Gather(p, xn2, chunk, (gather_s, gather_r), EVEN)
    gather.start()
    own_rows = slice(COMMON_FEED, COMMON_FEED + RANK)
    fold_rows = slice(COMMON_FEED + RANK, COMMON_FEED + OWN_FEED)
    e_row = slice(COMMON_FEED + RANK, COMMON_FEED + RANK + 1)
    e_first = width - 2 * hpad
    pack[...] = jnp.zeros_like(pack)
    at = 5 * RANK
    for piece in (av_out, av_down):
        pack[at : at + RANK, :] = piece[...]
        at += RANK
    back_hidden(1)
    loads[4].wait()

    def hidden_units(plane):
        rows = rows_of(plane, block)

        @pl.loop(0, hpad // tile)
        def _(n):
            at_gate = rows_of(n, tile)
            at_up = rows_of(n + hpad // tile, tile)
            of_gate = rows_of(n + e_first // tile, tile)
            of_up = rows_of(n + (e_first + hpad) // tile, tile)
            gate = nt(xn2[rows, :], vgu[at_gate, :]) * s_gu[:, at_gate]
            up = nt(xn2[rows, :], vgu[at_up, :]) * s_gu[:, at_up]
            sigma = jax.nn.sigmoid(gate)
            active = gate * sigma
            hid[rows, at_gate] = (active * up).astype(BF16)
            back = dhid[rows, at_gate].astype(F32)
            grad_gate = back * up * sigma * (1.0 + gate * (1.0 - sigma))
            grad_up = back * active
            pack[e_row, of_gate] += jnp.sum(grad_gate * gate, axis=0, keepdims=True)
            pack[e_row, of_up] += jnp.sum(grad_up * up, axis=0, keepdims=True)
            dgu[rows, at_gate] = (grad_gate * s_gu[:, at_gate]).astype(BF16)
            dgu[rows, at_up] = (grad_up * s_gu[:, at_up]).astype(BF16)

    def back_part(plane, first, last):
        rows = rows_of(plane, block)

        @pl.loop(first // 512, last // 512)
        def _(n):
            part_cols = rows_of(n, 512)
            part[rows, part_cols] = nn(dgu[rows, :], vgu[:, part_cols]).astype(BF16)

    scatter = Scatter(p, part, sum_own, chunk, EVEN, scatter_scratch)
    gather.first()
    gather.middle()
    hidden_units(p.z)
    gather.late()
    back_part(p.z, 0, width)
    scatter.start_a(1)
    gather.end()
    hidden_units(p.far)
    back_part(p.far, 1024, width)
    scatter.start_b()
    back_part(p.far, 0, 1024)
    scatter.start_a(0)

    def forward_part(half):
        rows = slice(half * block, (half + 1) * block)

        @pl.loop(0, width // 512)
        def _(n):
            part_cols = rows_of(n, 512)
            ffn_ref[rows, part_cols] = nn(hid[rows, :], vdown[:, part_cols]).astype(BF16)

    t_one = []
    for k in range(2):
        part_cols = slice(k * hpad, (k + 1) * hpad)
        t_one.append(nt(b_gu[:, part_cols], dgu[:, part_cols]).astype(BF16))
    t_one = jnp.concatenate(t_one, axis=0)
    left_gu = t_gu[...].astype(BF16)
    x_gu = nt(left_gu, xn2[...]).astype(BF16)
    scatter.first()
    ratio = pack[e_row, e_first:] / n2_gu[...]
    back_gu = (b_gu[...].astype(F32) * ratio).astype(BF16)
    for n in range(0, width, 512):
        at = slice(n, n + 512)
        first = nn(t_one, xn2[:, at])
        for k in range(2):
            units = slice(k * hpad, (k + 1) * hpad)
            pack[k * RANK : (k + 1) * RANK, at] = first[k * RANK : (k + 1) * RANK] - nn(
                back_gu[:, units], vgu[units, at]
            )
    forward_part(0)
    forward_part(1)
    store = pltpu.make_async_copy(ffn_ref, ffn_hbm, local_sems.at[6])
    store.start()
    scatter.middle()
    for k in range(2):
        part_cols = slice(k * hpad, (k + 1) * hpad)
        both = slice(k * RANK, (k + 1) * RANK)
        pack[own_rows, part_cols] = (
            nn(x_gu[both], dgu[:, part_cols])
            - nt(left_gu[both], vgu[part_cols, :]) * ratio[:, part_cols]
        )
    back_down = nt(b_down[...].astype(BF16), dys[...]).astype(BF16)
    ga_down = nn(back_down, hid[...])
    fits = width - 2 * hpad
    pack[own_rows, 2 * hpad :] = ga_down[:, :fits]
    pack[fold_rows, : hpad - fits] = ga_down[:, fits:]
    x_down = nt(at_down[...], hid[...]).astype(BF16)
    for n in range(0, width, 512):
        pack[3 * RANK : 4 * RANK, n : n + 512] = nn(x_down, dys[:, n : n + 512])
    scatter.end()

    length = lengths[0]
    for r in range(1, tokens // span):
        length = jnp.where(p.me * chunk >= r * span, lengths[r], length)
    pos = seq * span + lax.rem(p.me * chunk, span) + lax.broadcasted_iota(jnp.int32, (chunk, 1), 0)
    live = (pos < length).astype(F32)
    dy_copy = pltpu.make_async_copy(cot_hbm.at[own], x_own, local_sems.at[5])
    dy_copy.start()
    scaled = sum_own[...] * gain[...]
    h1 = h1_ref[...]
    mean = jnp.mean(scaled * h1, axis=-1, keepdims=True)
    dy_copy.wait()
    grad = x_own[...].astype(F32) * live + inv2 * (scaled - h1 * (inv2 * inv2 * mean))
    dh1_ref[...] = grad
    low = grad.astype(BF16).astype(F32)
    pack[7 * RANK : 7 * RANK + 1, :] = jnp.sum(low * attn[...], axis=0, keepdims=True)
    das = (low * s_out[...]).astype(BF16)

    @pl.loop(0, width // 512)
    def _(n):
        part_cols = rows_of(n, 512)
        dmix_own[:, part_cols] = nt(das, vout[part_cols, :]).astype(BF16)

    backs = []
    for step in range(1, PARTS):
        to = lax.rem(p.me + step, PARTS)
        backs.append(
            p.send(
                dmix_own.at[:, rows_of(to, cols)],
                dmix_ref.at[own],
                (back_s, back_r),
                step - 1,
                to,
            )
        )
    dmix_ref[own, :] = dmix_own[:, my_cols]
    t_out = nt(b_out[...].astype(BF16), das).astype(BF16)
    pack[4 * RANK : 5 * RANK, :] = nn(t_out, mixed_own[...])
    x_out = nt(at_out[...], mixed_own[...]).astype(BF16)
    pack[2 * RANK : 3 * RANK, :] = nn(x_out, das)
    for copy in backs:
        copy.wait_recv()
    for copy in swaps + backs:
        copy.wait_send()
    store.wait()


def feed(span, lengths, mixed, *rest):
    tokens, cols = mixed.shape
    hpad, width = rest[-1].shape
    chunk = tokens // PARTS
    shape = jax.ShapeDtypeStruct
    out_shape = (
        shape((chunk, width), F32),
        shape((chunk, width), F32),
        shape((tokens, cols), BF16),
        shape((COMMON_FEED + OWN_FEED, width), F32),
        shape((tokens, width), BF16),
    )
    dma = pltpu.SemaphoreType.DMA
    scratch = [
        pltpu.VMEM((tokens, width), BF16),
        pltpu.VMEM((width, width), BF16),
        pltpu.VMEM((2 * hpad, width), BF16),
        pltpu.VMEM((hpad, width), BF16),
        pltpu.VMEM((tokens, width), BF16),
        pltpu.VMEM((tokens, width), BF16),
        pltpu.VMEM((tokens, width), BF16),
        pltpu.VMEM((tokens, hpad), BF16),
        pltpu.VMEM((tokens, hpad), BF16),
        pltpu.VMEM((tokens, 2 * hpad), BF16),
        pltpu.VMEM((chunk, width), BF16),
        pltpu.VMEM((chunk, width), BF16),
        pltpu.VMEM((chunk, width), BF16),
        pltpu.VMEM((chunk, width), F32),
        pltpu.VMEM((chunk, width), F32),
        pltpu.VMEM((RANK, 2 * hpad), BF16),
        pltpu.VMEM((RANK, hpad), BF16),
        dma((7,)),
        dma((PARTS - 1,)),
        dma((PARTS - 1,)),
        dma((PARTS - 1,)),
        dma((PARTS - 1,)),
        dma((GATHER_SEMS,)),
        dma((GATHER_SEMS,)),
    ]
    scratch += Scatter.scratch(chunk, width, EVEN)
    anywhere = pl.BlockSpec(memory_space=pl.ANY)
    return pl.pallas_call(
        functools.partial(feed_kernel, span),
        out_shape=out_shape,
        in_specs=[pl.BlockSpec(memory_space=pltpu.SMEM)] + [VMEM] * 14 + [anywhere] * 5,
        out_specs=[VMEM] * 4 + [anywhere],
        scratch_shapes=scratch,
        compiler_params=pltpu.CompilerParams(
            collective_id=1, has_side_effects=True, vmem_limit_bytes=ROOM
        ),
    )(lengths, mixed, *rest)


def turn(values, cosines, sines):
    return values * cosines + pltpu.roll(values, HD // 2, 1) * sines


def scores_of(q, keys, query_pos, key_pos, first, length):
    scores = nt(q, keys) * HD ** (-0.5)
    at = key_pos + first
    return jnp.where((at <= query_pos) & (at < length), scores, MASKED)


def back_kernel(
    rows,
    lengths,
    q_ref,
    mixed_ref,
    lse_ref,
    dmix_ref,
    kept_ref,
    cosines,
    sines,
    s_qkv,
    s_down,
    h1_ref,
    cot_hbm,
    kv_hbm,
    ffn_hbm,
    dqkv_ref,
    e_qkv,
    out_ref,
    e_down,
    gather_s,
    gather_r,
    kv_ref,
    ffn_ref,
    dkv,
    sib_far,
    hold,
    far,
    sib,
    dq,
    inner,
    total_own,
    dy_own,
    local_sems,
    send_sems,
    recv_sems,
    *scratch,
):
    tokens, cols = q_ref.shape
    span = tokens // rows
    heads = cols // HD
    chunk = tokens // PARTS
    p = Place()
    core = lax.rem(p.seq, 2)
    upper = p.seq // 2
    sibling = upper * 2 + 1 - core
    loads = []
    for i, (src, dst) in enumerate(
        [(ffn_hbm, ffn_ref), (kv_hbm, kv_ref), (cot_hbm.at[rows_of(p.me, chunk)], dy_own)]
    ):
        loads.append(pltpu.make_async_copy(src, dst, local_sems.at[i]))
        loads[-1].start()
    barrier = pltpu.get_barrier_semaphore()
    for step in range(1, PARTS):
        place = p.at(lax.rem(p.me + step, PARTS))
        pl.semaphore_signal(barrier, inc=1, device_id=place, device_id_type=MESH)
    for seq in (sibling, (1 - upper) * 2 + core):
        pl.semaphore_signal(barrier, inc=1, device_id=(p.row, seq, p.me), device_id_type=MESH)
    e_qkv[...] = jnp.zeros_like(e_qkv)
    dq[...] = jnp.zeros_like(dq)
    pl.semaphore_wait(barrier, PARTS + 1)
    loads[0].wait()
    scatter = Scatter(p, ffn_ref, total_own, chunk, RING_FIRST, scratch)
    scatter.start_b()
    scatter.start_a(0)
    scatter.start_a(1)

    def over(source, target, index, seq):
        return pltpu.make_async_remote_copy(
            src_ref=source,
            dst_ref=target,
            send_sem=send_sems.at[index],
            recv_sem=recv_sems.at[index],
            device_id=(p.row, seq, p.me),
            device_id_type=MESH,
        )

    to_sib_far = []
    to_sib = []
    to_far = []
    for r in range(rows):
        part = slice(r * span, (r + 1) * span)
        to_sib_far.append(over(dkv.at[1 - core, part], sib_far.at[part], r, sibling))
        to_sib.append(over(dkv.at[upper * 2, part], sib.at[part], rows + r, sibling))
        to_far.append(over(hold.at[part], far.at[part], 2 * rows + r, core))

    query_pos = p.seq * span + lax.broadcasted_iota(jnp.int32, (span, span), 0)
    key_pos = lax.broadcasted_iota(jnp.int32, (span, span), 1)

    for r in range(rows):
        part = slice(r * span, (r + 1) * span)
        for head in range(heads):
            at = slice(head * HD, (head + 1) * HD)
            i = r * heads + head
            inner[:, i : i + 1] = jnp.sum(
                dmix_ref[part, at].astype(F32) * mixed_ref[part, at].astype(F32),
                axis=-1,
                keepdims=True,
            )

    loads[1].wait()

    def blocks(r, head, first, last):
        part = slice(r * span, (r + 1) * span)
        kcols = slice(head * HD, (head + 1) * HD)
        vcols = slice(cols + head * HD, cols + (head + 1) * HD)
        i = r * heads + head

        @pl.loop(first, last)
        def _(j):
            q = q_ref[part, kcols]
            do = dmix_ref[part, kcols]
            lse = lse_ref[part, head * HD : head * HD + 1]
            scores = scores_of(q, kv_ref[j, part, kcols], query_pos, key_pos, j * span, lengths[r])
            probs = jnp.exp(scores - lse)
            dkv[j, part, vcols] = tn(probs.astype(BF16), do).astype(BF16)
            grad = (probs * (nt(do, kv_ref[j, part, vcols]) - inner[:, i : i + 1])).astype(BF16)
            dq[part, kcols] += nn(grad, kv_ref[j, part, kcols])
            dkv[j, part, kcols] = (tn(grad, q) * HD ** (-0.5)).astype(BF16)

    def onward(r):
        part = slice(r * span, (r + 1) * span)

        @pl.when(upper == 1)
        def _():
            to_sib_far[r].wait_recv()
            hold[part] = (dkv[core, part].astype(F32) + sib_far[part].astype(F32)).astype(BF16)
            to_far[r].start()

    def emit(part, at, grad):
        held = kept_ref[part, at].astype(F32)
        e_qkv[:, at] += jnp.sum(grad * held, axis=0, keepdims=True)
        dqkv_ref[part, at] = (grad * s_qkv[:, at]).astype(BF16)

    def results():
        loads[2].wait()
        length = lengths[0]
        for r in range(1, rows):
            length = jnp.where(p.me * chunk >= r * span, lengths[r], length)
        first = p.seq * span + lax.rem(p.me * chunk, span)
        pos = first + lax.broadcasted_iota(jnp.int32, (chunk, 1), 0)
        live = (pos < length).astype(F32)
        ffn = total_own[...] * s_down[...]
        out_ref[rows_of(p.me, chunk), :] = ((h1_ref[...] + ffn) * live).astype(BF16)
        e_down[...] = jnp.sum(dy_own[...].astype(F32) * live * ffn, axis=0, keepdims=True)

    for r in range(rows):
        for head in range(heads):
            blocks(r, head, 0, 2 * upper)

        @pl.when(upper == 1)
        def _(r=r):
            to_sib_far[r].start()

        if r == 0:
            scatter.first()
        else:
            onward(r - 1)
    for r in range(rows):
        for head in range(heads):
            blocks(r, head, 2 * upper, p.seq + 1)
            if r == 0 and head == 0:
                onward(rows - 1)
                scatter.middle()
            if r == 1 and head == 0:
                scatter.end()
                results()
                gather = Gather(p, out_ref, chunk, (gather_s, gather_r), RING_FIRST)
                gather.start()

        @pl.when(core == 1)
        def _(r=r):
            to_sib[r].start()

    gather.first()
    for r in range(rows):
        part = slice(r * span, (r + 1) * span)
        for head in range(heads):
            at = slice(head * HD, (head + 1) * HD)
            emit(part, at, turn(dq[part, at] * HD ** (-0.5), cosines[...], -sines[...]))
    gather.middle()

    for r in range(rows):
        part = slice(r * span, (r + 1) * span)

        @pl.when(core == 0)
        def _(r=r):
            to_sib[r].wait_recv()

        @pl.when(upper == 0)
        def _(r=r):
            to_far[r].wait_recv()

        for head in range(2 * heads):
            at = slice(head * HD, (head + 1) * HD)
            grad = dkv[p.seq, part, at].astype(F32)
            grad = grad + jnp.where(core == 0, sib[part, at].astype(F32), 0.0)
            grad = grad + jnp.where(upper == 0, far[part, at].astype(F32), 0.0)
            if head < heads:
                grad = turn(grad, cosines[...], -sines[...])
            emit(part, slice(cols + head * HD, cols + (head + 1) * HD), grad)
        if r == 0:
            gather.late()
    gather.end()

    for r in range(rows):

        @pl.when(upper == 1)
        def _(r=r):
            to_sib_far[r].wait_send()
            to_far[r].wait_send()

        @pl.when(core == 1)
        def _(r=r):
            to_sib[r].wait_send()


def back(rows, lengths, q, *rest):
    kv, ffn = rest[-2:]
    tokens, cols = q.shape
    width = ffn.shape[1]
    chunk = tokens // PARTS
    shape = jax.ShapeDtypeStruct
    dma = pltpu.SemaphoreType.DMA
    out_shape = (
        shape((tokens, 3 * cols), BF16),
        shape((1, 3 * cols), F32),
        shape((tokens, width), BF16),
        shape((1, width), F32),
    )
    scratch = [
        dma((GATHER_SEMS,)),
        dma((GATHER_SEMS,)),
        pltpu.VMEM(kv.shape, BF16),
        pltpu.VMEM(ffn.shape, BF16),
        pltpu.VMEM(kv.shape, BF16),
        pltpu.VMEM((tokens, 2 * cols), BF16),
        pltpu.VMEM((tokens, 2 * cols), BF16),
        pltpu.VMEM((tokens, 2 * cols), BF16),
        pltpu.VMEM((tokens, 2 * cols), BF16),
        pltpu.VMEM((tokens, cols), F32),
        pltpu.VMEM((tokens // rows, rows * cols // HD), F32),
        pltpu.VMEM((chunk, width), F32),
        pltpu.VMEM((chunk, width), BF16),
        dma((3,)),
        dma((3 * rows,)),
        dma((3 * rows,)),
    ]
    scratch += Scatter.scratch(chunk, width, RING_FIRST)
    return pl.pallas_call(
        functools.partial(back_kernel, rows),
        out_shape=out_shape,
        in_specs=[pl.BlockSpec(memory_space=pltpu.SMEM)]
        + [VMEM] * (len(rest) - 2)
        + [pl.BlockSpec(memory_space=pl.ANY)] * 3,
        out_specs=[VMEM] * len(out_shape),
        scratch_shapes=scratch,
        compiler_params=pltpu.CompilerParams(
            collective_id=2, has_side_effects=True, vmem_limit_bytes=ROOM
        ),
    )(lengths, q, *rest)


COMMON_FEED, OWN_FEED = 128, 32
COMMON_QKV, OWN_QKV = 48, 16


class Total:
    def __init__(self, place, common, scratch):
        self.p = p = place
        self.common = common
        (
            self.send_buf,
            self.land_row,
            self.by_row,
            self.land_seq,
            self.mine,
            self.across,
            self.held,
            *self.sems,
        ) = scratch
        self.rows = [(lax.rem(p.row + step, RING), p.seq, p.me) for step in range(1, RING)]
        self.seqs = [(p.row, lax.rem(p.seq + step, RING), p.me) for step in range(1, RING)]
        self.heads = [p.at(lax.rem(p.me + step, PARTS)) for step in range(1, PARTS)]

    @staticmethod
    def scratch(common, own):
        dma = pltpu.SemaphoreType.DMA
        piece = (common + own, 128)
        return [
            pltpu.VMEM((RING * RING, *piece), BF16),
            pltpu.VMEM((RING - 1, RING, *piece), BF16),
            pltpu.VMEM((RING, *piece), BF16),
            pltpu.VMEM((RING - 1, *piece), BF16),
            pltpu.VMEM(piece, BF16),
            pltpu.VMEM((PARTS - 1, common, 128), BF16),
            pltpu.VMEM((RING * RING, *piece), BF16),
        ] + [dma((n,)) for n in (3, 3, 3, 3, PARTS - 1, PARTS - 1, 3, 3, 3, 3)]

    def greet(self):
        barrier = pltpu.get_barrier_semaphore()
        for place in self.rows + self.seqs + self.heads:
            pl.semaphore_signal(barrier, inc=1, device_id=place, device_id_type=MESH)
        pl.semaphore_wait(barrier, 2 * (RING - 1) + PARTS - 1)

    def fill(self, rows, source):
        for piece in range(RING * RING):
            self.send_buf[piece, rows] = source[:, piece * 128 : (piece + 1) * 128].astype(BF16)

    def copies(self, source, target, ends, stage):
        made = []
        for step, place in enumerate(ends):
            made.append(
                pltpu.make_async_remote_copy(
                    src_ref=source(place),
                    dst_ref=target(step),
                    send_sem=self.sems[2 * stage].at[step],
                    recv_sem=self.sems[2 * stage + 1].at[step],
                    device_id=place,
                    device_id_type=MESH,
                )
            )
            made[-1].start()
        return made

    def start(self):
        self.wait = self.copies(
            lambda place: self.send_buf.at[rows_of(place[0], RING)],
            lambda step: self.land_row.at[step],
            self.rows,
            0,
        )

    def second(self):
        for copy in self.wait:
            copy.wait()
        for q in range(RING):
            total = self.send_buf[self.p.row * RING + q].astype(F32)
            for step in range(RING - 1):
                total += self.land_row[step, q].astype(F32)
            self.by_row[q] = total.astype(BF16)
        self.wait = self.copies(
            lambda place: self.by_row.at[place[1]], lambda step: self.land_seq.at[step], self.seqs, 1
        )

    def third(self):
        for copy in self.wait:
            copy.wait()
        total = self.by_row[self.p.seq].astype(F32)
        for step in range(RING - 1):
            total += self.land_seq[step].astype(F32)
        self.mine[...] = total.astype(BF16)
        self.wait = self.copies(
            lambda place: self.mine.at[: self.common],
            lambda step: self.across.at[step],
            self.heads,
            2,
        )

    def fourth(self):
        for copy in self.wait:
            copy.wait()
        shared = self.mine[: self.common].astype(F32)
        for step in range(PARTS - 1):
            shared += self.across[step].astype(F32)
        here = self.p.row * RING + self.p.seq
        self.held[here, : self.common] = shared.astype(BF16)
        self.held[here, self.common :] = self.mine[self.common :]
        view = self.held.at[here]
        self.wait = self.copies(lambda place: view, lambda step: view, self.seqs, 3)

    def fifth(self):
        for copy in self.wait:
            copy.wait()
        view = self.held.at[rows_of(self.p.row, RING)]
        self.wait = self.copies(lambda place: view, lambda step: view, self.rows, 4)

    def end(self, out):
        for copy in self.wait:
            copy.wait()
        for piece in range(RING * RING):
            out[:, piece * 128 : (piece + 1) * 128] = self.held[piece].astype(F32)


def close_kernel(
    cols,
    dqkv_ref,
    vqkv,
    xn1_hbm,
    x_hbm,
    gain,
    dh1_ref,
    b_raw,
    t_raw,
    e_qkv,
    n2_qkv,
    pack_feed,
    e_down,
    gx_ref,
    sum_feed,
    sum_qkv,
    part,
    pack,
    xn1,
    x_own,
    total_own,
    b_qkv,
    local_sems,
    gather_s,
    gather_r,
    *scratch,
):
    tokens, width = xn1.shape
    chunk = tokens // PARTS
    p = Place()
    own = rows_of(p.me, chunk)
    totals = Total(p, COMMON_QKV, scratch[:17])
    early = Total(p, COMMON_FEED, scratch[17:34])
    load = pltpu.make_async_copy(x_hbm.at[own], x_own, local_sems.at[0])
    load.start()
    load_xn1 = pltpu.make_async_copy(xn1_hbm, xn1, local_sems.at[1])
    load_xn1.start()
    early.fill(slice(None), pack_feed)
    row = 7 * RANK + 1
    early.fill(slice(row, row + 1), e_down)
    totals.greet()
    early.start()

    def back_part(first, last):
        @pl.loop(first // 256, last // 256)
        def _(n):
            at = rows_of(n, 256)
            part[:, at] = nt(dqkv_ref[...], vqkv[at, :]).astype(BF16)

    scatter = Scatter(p, part, total_own, chunk, EVEN, scratch[34:])
    back_part(1024, width)
    scatter.start_b()
    back_part(0, 1024)
    scatter.start_a(0)
    scatter.start_a(1)

    b_qkv[...] = jnp.zeros_like(b_qkv)
    for k in range(3):
        b_qkv[k * RANK : (k + 1) * RANK, k * cols : (k + 1) * cols] = b_raw[k].astype(BF16)
    t_qkv = t_raw[...].astype(BF16)
    ratio = e_qkv[...] / n2_qkv[...]
    back_qkv = (b_qkv[...].astype(F32) * ratio).astype(BF16)
    t_one = nt(b_qkv[...], dqkv_ref[...]).astype(BF16)
    load_xn1.wait()
    t_two = nt(t_qkv, xn1[...]).astype(BF16)
    scatter.first()
    early.second()
    for n in range(0, width, 512):
        at = slice(n, n + 512)
        pack[: 3 * RANK, at] = nn(t_one, xn1[:, at]) - nt(back_qkv, vqkv[at, :])
    gb = nn(t_two, dqkv_ref[...]) - nn(t_qkv, vqkv[...]) * ratio
    pack[COMMON_QKV:, :] = jnp.zeros((OWN_QKV, width), F32)
    for k in range(3):
        pack[COMMON_QKV:, k * cols : (k + 1) * cols] = gb[
            k * RANK : (k + 1) * RANK, k * cols : (k + 1) * cols
        ]
    pack[COMMON_QKV : COMMON_QKV + 1, 3 * cols : 6 * cols] = e_qkv[...]
    totals.fill(slice(None), pack)
    totals.start()
    scatter.middle()
    early.third()
    load.wait()
    x = x_own[...].astype(F32)
    inv1 = lax.rsqrt(jnp.mean(x * x, axis=-1, keepdims=True) + EPS)
    scatter.end()
    scaled = total_own[...] * gain[...]
    mean = jnp.mean(scaled * x, axis=-1, keepdims=True)
    grad = dh1_ref[...] + inv1 * (scaled - x * (inv1 * inv1 * mean))
    gx_ref[own, :] = grad.astype(BF16)
    gather = Gather(p, gx_ref, chunk, (gather_s, gather_r), EVEN)
    gather.start()
    totals.second()
    early.fourth()
    gather.first()
    totals.third()
    early.fifth()
    gather.middle()
    totals.fourth()
    gather.late()
    totals.fifth()
    early.end(sum_feed)
    gather.end()
    totals.end(sum_qkv)


def close(cols, dqkv, vqkv, xn1, x, *rest):
    tokens, width = xn1.shape
    chunk = tokens // PARTS
    shape = jax.ShapeDtypeStruct
    dma = pltpu.SemaphoreType.DMA
    out_shape = (
        shape((tokens, width), BF16),
        shape((COMMON_FEED + OWN_FEED, width), F32),
        shape((COMMON_QKV + OWN_QKV, width), F32),
    )
    scratch = [
        pltpu.VMEM((tokens, width), BF16),
        pltpu.VMEM((COMMON_QKV + OWN_QKV, width), F32),
        pltpu.VMEM((tokens, width), BF16),
        pltpu.VMEM((chunk, width), BF16),
        pltpu.VMEM((chunk, width), F32),
        pltpu.VMEM((3 * RANK, 3 * cols), BF16),
        dma((2,)),
        dma((GATHER_SEMS,)),
        dma((GATHER_SEMS,)),
    ]
    scratch += Total.scratch(COMMON_QKV, OWN_QKV) + Total.scratch(COMMON_FEED, OWN_FEED)
    scratch += Scatter.scratch(chunk, width, EVEN)
    return pl.pallas_call(
        functools.partial(close_kernel, cols),
        out_shape=out_shape,
        in_specs=[VMEM] * 2 + [pl.BlockSpec(memory_space=pl.ANY)] * 2 + [VMEM] * len(rest),
        out_specs=[VMEM] * 3,
        scratch_shapes=scratch,
        compiler_params=pltpu.CompilerParams(
            collective_id=3, has_side_effects=True, vmem_limit_bytes=ROOM
        ),
    )(dqkv, vqkv, xn1, x, *rest)


def three_terms(left, right):
    def split(a):
        high = a.astype(BF16)
        return high, (a - high.astype(F32)).astype(BF16)

    left_high, left_low = split(left)
    right_high, right_low = split(right)
    return (
        jnp.concatenate([left_high, left_low, left_high], axis=0),
        jnp.concatenate([right_high, right_high, right_low], axis=0),
    )


def front_kernel(
    rows,
    spread,
    lengths,
    gain,
    m_qkv,
    m_out,
    m_gu,
    m_down,
    t_qkv,
    b_qkv,
    t_out,
    b_out,
    t_gu,
    b_gu,
    t_down,
    b_down,
    cosines,
    sines,
    x_hbm,
    wqkv_hbm,
    wout_hbm,
    wgu_hbm,
    wdown_hbm,
    q_ref,
    kept_ref,
    mixed_ref,
    lse_ref,
    n2_qkv,
    n2_gu,
    n2_model,
    s_qkv,
    s_gu,
    s_out,
    s_down,
    at_out,
    av_out,
    av_down,
    xn1_hbm,
    vqkv_hbm,
    vout_hbm,
    vgu_hbm,
    vdown_hbm,
    kv_hbm,
    x_ref,
    wqkv,
    wout,
    wgu,
    wdown,
    xn1,
    vqkv,
    vfull,
    vgu,
    vdown,
    kv,
    acc,
    top,
    weight,
    squares,
    land_squares,
    at_mine,
    load_sems,
    store_sems,
    gather_s,
    gather_r,
    share_s,
    share_r,
    kv_s,
    kv_r,
    square_s,
    square_r,
    at_s,
    at_r,
):
    tokens, width = x_ref.shape
    span = tokens // rows
    cols = q_ref.shape[1]
    heads = cols // HD
    hidden = wdown.shape[0]
    hpad = vdown.shape[0]
    p = Place()
    core = lax.rem(p.seq, 2)
    upper = p.seq // 2
    sibling = upper * 2 + 1 - core
    loads = []
    pairs = [(wout_hbm, wout), (wqkv_hbm, wqkv), (x_hbm, x_ref), (wdown_hbm, wdown), (wgu_hbm, wgu)]
    for i, (src, dst) in enumerate(pairs):
        loads.append(pltpu.make_async_copy(src, dst, load_sems.at[i]))
        loads[-1].start()
    barrier = pltpu.get_barrier_semaphore()
    for step in range(1, PARTS):
        place = p.at(lax.rem(p.me + step, PARTS))
        pl.semaphore_signal(barrier, inc=1, device_id=place, device_id_type=MESH)
    for seq in (sibling, (1 - upper) * 2 + core):
        pl.semaphore_signal(barrier, inc=1, device_id=(p.row, seq, p.me), device_id_type=MESH)

    left, right = three_terms(t_out[...], b_out[...])
    my_cols = rows_of(p.me, cols)
    loads[0].wait()
    squares[...] = jnp.zeros_like(squares)
    for n in range(0, width, 512):
        at = slice(n, n + 512)
        v = wout[:, at].astype(F32) + SCALE * tn(left, right[:, at])
        vfull[my_cols, at] = v.astype(BF16)
        squares[0:1, at] = jnp.sum(v * v, axis=0, keepdims=True)
    at_mine[...] = t_out[...].astype(BF16)
    at_out[:, my_cols] = t_out[...].astype(BF16)
    pl.semaphore_wait(barrier, PARTS + 1)
    gather = Gather(p, vfull, cols // 2, (gather_s, gather_r), RING_FIRST, cols, core)
    gather.start()
    at_copies = []
    for step in range(1, PARTS):
        to = lax.rem(p.me + step, PARTS)
        at_copies.append(p.send(at_mine, at_out.at[:, my_cols], (at_s, at_r), step - 1, to))

    loads[1].wait()

    def direct(k):
        left, right = three_terms(t_qkv[k], b_qkv[k])
        at = slice(k * cols, (k + 1) * cols)
        total = jnp.zeros((1, cols), F32)
        for n in range(0, width, 512):
            part = slice(n, n + 512)
            v = wqkv[k, part, :].astype(F32) + SCALE * tn(left[:, part], right)
            vqkv[part, at] = v.astype(BF16)
            total += jnp.sum(v * v, axis=0, keepdims=True)
        n2_qkv[:, at] = total
        s_qkv[:, at] = m_qkv[k : k + 1, :] * lax.rsqrt(total)

    def project(r, k):
        part = slice(r * span, (r + 1) * span)
        at = slice(k * cols, (k + 1) * cols)
        y = nn(xn1[part, :], vqkv[:, at]) * s_qkv[:, at]
        kept_ref[part, at] = y.astype(BF16)
        if k < 2:
            y = jnp.concatenate(
                [turn(y[:, h * HD : (h + 1) * HD], cosines[...], sines[...]) for h in range(heads)],
                axis=1,
            )
        if k == 0:
            q_ref[part, :] = y.astype(BF16)
        else:
            kv[p.seq, part, (k - 1) * cols : k * cols] = y.astype(BF16)

    def over(source, index, seq):
        return pltpu.make_async_remote_copy(
            src_ref=source,
            dst_ref=source,
            send_sem=kv_s.at[index],
            recv_sem=kv_r.at[index],
            device_id=(p.row, seq, p.me),
            device_id_type=MESH,
        )

    direct(1)
    direct(2)
    loads[2].wait()
    to_sib, to_far, onward = [], [], []
    for r in range(rows):
        part = slice(r * span, (r + 1) * span)
        to_sib.append(over(kv.at[p.seq, part], r, sibling))
        to_far.append(over(kv.at[p.seq, part], rows + r, 2 + core))
        onward.append(over(kv.at[core, part], 2 * rows + r, sibling))

        @pl.loop(0, span // 128)
        def _(i, r=r):
            piece = pl.ds(pl.multiple_of(r * span + i * 128, 128), 128)
            x = x_ref[piece, :].astype(F32)
            inv = lax.rsqrt(jnp.mean(x * x, axis=-1, keepdims=True) + EPS)
            xn1[piece, :] = (x * inv * gain[...]).astype(BF16)

        project(r, 1)
        project(r, 2)

        @pl.when(upper == 0)
        def _(r=r):
            to_far[r].start()

        @pl.when(core == 0)
        def _(r=r):
            to_sib[r].start()

    direct(0)
    for r in range(rows):
        project(r, 0)
    stores = [
        pltpu.make_async_copy(vqkv, vqkv_hbm, store_sems.at[1]),
        pltpu.make_async_copy(xn1, xn1_hbm, store_sems.at[2]),
    ]
    for copy in stores:
        copy.start()

    query_pos = p.seq * span + lax.broadcasted_iota(jnp.int32, (span, span), 0)
    key_pos = lax.broadcasted_iota(jnp.int32, (span, span), 1)

    def absorb(r, j, fresh=False):
        part = slice(r * span, (r + 1) * span)
        for head in range(heads):
            at = slice(head * HD, (head + 1) * HD)
            to = slice(cols + head * HD, cols + (head + 1) * HD)
            one = (slice(None), slice(r * heads + head, r * heads + head + 1))
            scores = scores_of(
                q_ref[part, at], kv[j, part, at], query_pos, key_pos, j * span, lengths[r]
            )
            best = jnp.max(scores, axis=-1, keepdims=True)
            if not fresh:
                best = jnp.maximum(best, top[one])
            expo = jnp.exp(scores - best)
            summed = jnp.sum(expo, axis=-1, keepdims=True)
            mixed = nn(expo.astype(BF16), kv[j, part, to])
            if not fresh:
                fade = jnp.exp(top[one] - best)
                summed += weight[one] * fade
                mixed += acc[part, at] * fade
            top[one] = best
            weight[one] = summed
            acc[part, at] = mixed

    gather.first()
    for r in range(rows):
        absorb(r, p.seq, True)
    gather.middle()

    loads[3].wait()
    vdown[hidden:, :] = jnp.zeros((hpad - hidden, width), BF16)
    left, right = three_terms(t_down[...], b_down[...])
    for n in range(0, width, 512):
        at = slice(n, n + 512)
        v = wdown[:, at].astype(F32) + SCALE * tn(left, right[:, at])
        vdown[:hidden, at] = v.astype(BF16)
        squares[1:2, at] = jnp.sum(v * v, axis=0, keepdims=True)
    square_copies = []
    for step in range(1, PARTS):
        to = lax.rem(p.me + step, PARTS)
        square_copies.append(
            p.send(squares, land_squares.at[step - 1], (square_s, square_r), step - 1, to)
        )
    stores.append(pltpu.make_async_copy(vdown, vdown_hbm, store_sems.at[3]))
    stores[-1].start()
    shares = []

    def share(plane, steps):
        for step in steps:
            view = gather.view(plane * RING + p.side(step))
            index = len(shares)
            shares.append(
                pltpu.make_async_remote_copy(
                    src_ref=view,
                    dst_ref=view,
                    send_sem=share_s.at[index],
                    recv_sem=share_r.at[index],
                    device_id=(p.row, sibling, p.me),
                    device_id_type=MESH,
                )
            )

            shares[-1].start()

    share(p.z, (1, 2, 3))

    loads[4].wait()
    ones = jnp.ones((8, width), BF16)
    for k in range(2):
        left, right = three_terms(b_gu[k], t_gu[k])
        base = k * hpad
        vgu[base + hidden : base + hpad, :] = jnp.zeros((hpad - hidden, width), BF16)
        n2_gu[:, base + hidden : base + hpad] = jnp.ones((1, hpad - hidden), F32)
        for n in range(0, hidden, 128):
            size = min(128, hidden - n)
            v = wgu[k, n : n + size, :].astype(F32) + SCALE * tn(left[:, n : n + size], right)
            vgu[base + n : base + n + size, :] = v.astype(BF16)
            n2_gu[:, base + n : base + n + size] = nt(ones, (v * v).astype(BF16))[:1]
        units = slice(base, base + hidden)
        s_gu[:, base : base + hpad] = jnp.zeros((1, hpad), F32)
        s_gu[:, units] = m_gu[k : k + 1, :] * lax.rsqrt(n2_gu[:, units])
    stores.append(pltpu.make_async_copy(vgu, vgu_hbm, store_sems.at[4]))
    stores[-1].start()
    gather.late()

    @pl.when(core == 1)
    def _():
        for r in range(rows):
            to_sib[r].wait_recv()
            absorb(r, p.seq - 1)

    for copy in shares:
        copy.wait_recv()
    half = rows_of(p.z, RING * cols)
    stores.append(pltpu.make_async_copy(vfull.at[half], vout_hbm.at[half], store_sems.at[0]))
    stores[-1].start()

    def from_far(r):
        @pl.when(upper == 1)
        def _():
            to_far[r].wait_recv()
            onward[r].start()
            absorb(r, core)
            onward[r].wait_recv()
            absorb(r, 1 - core)

    from_far(0)
    gather.end()
    share(p.far, (0, 1, 2, 3))
    for r in range(1, rows):
        from_far(r)

    @pl.loop(p.seq + 1, kv.shape[0])
    def _(j):
        kv[j] = jnp.zeros(kv.shape[1:], BF16)

    stores.append(pltpu.make_async_copy(kv, kv_hbm, store_sems.at[5]))
    stores[-1].start()
    for r in range(rows):
        part = slice(r * span, (r + 1) * span)
        for head in range(heads):
            at = slice(head * HD, (head + 1) * HD)
            one = (slice(None), slice(r * heads + head, r * heads + head + 1))
            mixed_ref[part, at] = (acc[part, at] / weight[one]).astype(BF16)
            lse_ref[part, at] = jnp.broadcast_to(top[one] + jnp.log(weight[one]), (span, HD))
    av_out[...] = nn(at_mine[...], vfull[my_cols, :]) / spread
    at_down = t_down[...].astype(BF16)
    av_down[...] = nn(at_down, vdown[:hidden, :]) / spread
    for copy in square_copies:
        copy.wait_recv()
    total = squares[...]
    for step in range(PARTS - 1):
        total += land_squares[step]
    n2_model[...] = total
    s_out[...] = m_out[...] * lax.rsqrt(total[0:1])
    s_down[...] = m_down[...] * lax.rsqrt(total[1:2])
    for copy in at_copies + shares[RING - 1 :]:
        copy.wait_recv()
    half = rows_of(p.far, RING * cols)
    stores.append(pltpu.make_async_copy(vfull.at[half], vout_hbm.at[half], store_sems.at[6]))
    stores[-1].start()
    for copy in at_copies + square_copies + shares:
        copy.wait_send()
    for copy in stores:
        copy.wait()

    @pl.when(upper == 0)
    def _():
        for r in range(rows):
            to_far[r].wait_send()

    @pl.when(core == 0)
    def _():
        for r in range(rows):
            to_sib[r].wait_send()

    @pl.when(upper == 1)
    def _():
        for r in range(rows):
            onward[r].wait_send()


def front(rows, seqs, spread, lengths, *rest):
    x, w_qkv, _, _, w_down = rest[-5:]
    tokens, width = x.shape
    cols = w_qkv.shape[2]
    heads = cols // HD
    hidden = w_down.shape[0]
    hpad = pad_to(hidden)
    span = tokens // rows
    shape = jax.ShapeDtypeStruct
    dma = pltpu.SemaphoreType.DMA
    vmem = pltpu.VMEM
    out_shape = (
        shape((tokens, cols), BF16),
        shape((tokens, 3 * cols), BF16),
        shape((tokens, cols), BF16),
        shape((tokens, cols), F32),
        shape((1, 3 * cols), F32),
        shape((1, 2 * hpad), F32),
        shape((8, width), F32),
        shape((1, 3 * cols), F32),
        shape((1, 2 * hpad), F32),
        shape((1, width), F32),
        shape((1, width), F32),
        shape((RANK, width), BF16),
        shape((RANK, width), F32),
        shape((RANK, width), F32),
        shape((tokens, width), BF16),
        shape((width, 3 * cols), BF16),
        shape((PARTS * cols, width), BF16),
        shape((2 * hpad, width), BF16),
        shape((hpad, width), BF16),
        shape((seqs, tokens, 2 * cols), BF16),
    )
    scratch = [
        vmem((tokens, width), BF16),
        vmem((3, width, cols), BF16),
        vmem((cols, width), BF16),
        vmem((2, hidden, width), BF16),
        vmem((hidden, width), BF16),
        vmem((tokens, width), BF16),
        vmem((width, 3 * cols), BF16),
        vmem((PARTS * cols, width), BF16),
        vmem((2 * hpad, width), BF16),
        vmem((hpad, width), BF16),
        vmem((seqs, tokens, 2 * cols), BF16),
        vmem((tokens, cols), F32),
        vmem((span, rows * heads), F32),
        vmem((span, rows * heads), F32),
        vmem((8, width), F32),
        vmem((PARTS - 1, 8, width), F32),
        vmem((RANK, cols), BF16),
        dma((5,)),
        dma((7,)),
        dma((GATHER_SEMS,)),
        dma((GATHER_SEMS,)),
        dma((PARTS,)),
        dma((PARTS,)),
        dma((3 * rows,)),
        dma((3 * rows,)),
    ] + [dma((PARTS - 1,))] * 4
    anywhere = pl.BlockSpec(memory_space=pl.ANY)
    return pl.pallas_call(
        functools.partial(front_kernel, rows, spread),
        out_shape=out_shape,
        in_specs=[pl.BlockSpec(memory_space=pltpu.SMEM)] + [VMEM] * 15 + [anywhere] * 5,
        out_specs=[VMEM] * 14 + [anywhere] * 6,
        scratch_shapes=scratch,
        compiler_params=pltpu.CompilerParams(
            collective_id=4, has_side_effects=True, vmem_limit_bytes=ROOM
        ),
    )(lengths, *rest)


def finish_kernel(
    hidden,
    summed,
    summed_qkv,
    m_qkv,
    m_out,
    m_gu,
    m_down,
    n2_model,
    b_out,
    b_down,
    vdown_hbm,
    vout_hbm,
    out_hbm,
    gx_hbm,
    output,
    grad_x,
    gm_qkv,
    ga_qkv,
    gb_qkv,
    gm_out,
    ga_out,
    gb_out,
    gm_gu,
    ga_gu,
    gb_gu,
    gm_down,
    ga_down,
    gb_down,
    vout,
    vdown,
    held,
    sems,
):
    cols, width = vout.shape
    hpad = vdown.shape[0]
    load = pltpu.make_async_copy(vout_hbm.at[rows_of(lax.axis_index("head"), cols)], vout, sems.at[0])
    load.start()
    load_down = pltpu.make_async_copy(vdown_hbm, vdown, sems.at[17])
    load_down.start()
    moves = []
    tokens = output.shape[0]
    for i in range(4):
        part = pl.ds(i * tokens // 4, tokens // 4)
        for k, src in enumerate((out_hbm, gx_hbm)):
            moves.append(pltpu.make_async_copy(src.at[part], held.at[k, part], sems.at[1 + 2 * i + k]))
            moves[-1].start()
    for i in range(4):
        part = pl.ds(i * tokens // 4, tokens // 4)
        for k, dst in enumerate((output, grad_x)):
            moves[2 * i + k].wait()
            moves.append(pltpu.make_async_copy(held.at[k, part], dst.at[part], sems.at[9 + 2 * i + k]))
            moves[-1].start()

    def block(first):
        return summed[first * RANK : (first + 1) * RANK, :]

    own_qkv = slice(COMMON_QKV, COMMON_QKV + RANK)
    for k in range(3):
        at = slice(k * cols, (k + 1) * cols)
        ga_qkv[k] = SCALE * summed_qkv[k * RANK : (k + 1) * RANK, :]
        gb_qkv[k] = SCALE * summed_qkv[own_qkv, at]
        e_one = summed_qkv[COMMON_QKV : COMMON_QKV + 1, (3 + k) * cols : (4 + k) * cols]
        gm_qkv[k : k + 1, :] = e_one / m_qkv[k : k + 1, :]
    for k in range(2):
        ga_gu[k] = SCALE * block(k)
    e_out = summed[7 * RANK : 7 * RANK + 1, :]
    e_down = summed[7 * RANK + 1 : 7 * RANK + 2, :]
    ratio_out = e_out / n2_model[0:1, :]
    ratio_down = e_down / n2_model[1:2, :]
    gm_out[...] = e_out / m_out[...]
    gm_down[...] = e_down / m_down[...]
    gb_out[...] = SCALE * (block(2) - block(5) * ratio_out)
    gb_down[...] = SCALE * (block(3) - block(6) * ratio_down)
    own_rows = slice(COMMON_FEED, COMMON_FEED + RANK)
    fold_rows = slice(COMMON_FEED + RANK, COMMON_FEED + OWN_FEED)
    fits = width - 2 * hpad
    gb = summed[own_rows, : 2 * hpad]
    e_gu = summed[COMMON_FEED + RANK : COMMON_FEED + RANK + 1, fits:]
    for k in range(2):
        at = slice(k * hpad, k * hpad + hidden)
        gb_gu[k] = SCALE * gb[:, at]
        gm_gu[k : k + 1, :] = e_gu[:, at] / m_gu[k : k + 1, :]
    back_down = (b_down[...] * ratio_down).astype(BF16)
    load_down.wait()
    down = jnp.concatenate([summed[own_rows, 2 * hpad :], summed[fold_rows, : hpad - fits]], axis=1)
    down = down - nt(back_down, vdown[...])
    ga_down[...] = SCALE * down[:, :hidden]
    load.wait()
    back_out = (b_out[...] * ratio_out).astype(BF16)
    at = rows_of(lax.axis_index("head"), cols)
    ga_out[...] = SCALE * (summed[4 * RANK : 5 * RANK, at] - nt(back_out, vout[...]))
    for move in moves[8:]:
        move.wait()


def finish(hidden, cols, summed, *rest):
    width = summed.shape[1]
    tokens = rest[-1].shape[0]
    shape = jax.ShapeDtypeStruct
    out_shape = (
        shape((tokens, width), BF16),
        shape((tokens, width), BF16),
        shape((3, cols), F32),
        shape((3, RANK, width), F32),
        shape((3, RANK, cols), F32),
        shape((1, width), F32),
        shape((RANK, cols), F32),
        shape((RANK, width), F32),
        shape((2, hidden), F32),
        shape((2, RANK, width), F32),
        shape((2, RANK, hidden), F32),
        shape((1, width), F32),
        shape((RANK, hidden), F32),
        shape((RANK, width), F32),
    )
    anywhere = pl.BlockSpec(memory_space=pl.ANY)
    return pl.pallas_call(
        functools.partial(finish_kernel, hidden),
        out_shape=out_shape,
        in_specs=[VMEM] * 9 + [anywhere] * 4,
        out_specs=[anywhere] * 2 + [VMEM] * 12,
        scratch_shapes=[
            pltpu.VMEM((cols, width), BF16),
            pltpu.VMEM(rest[-4].shape, BF16),
            pltpu.VMEM((2, tokens, width), BF16),
            pltpu.SemaphoreType.DMA((18,)),
        ],
        compiler_params=pltpu.CompilerParams(vmem_limit_bytes=ROOM),
    )(summed, *rest)


def shards(
    layer_input,
    cotangent,
    lengths,
    gain_attn,
    gain_ffn,
    w_qkv,
    m_qkv,
    a_qkv,
    b_qkv,
    w_out,
    m_out,
    a_out,
    b_out,
    w_gu,
    m_gu,
    a_gu,
    b_gu,
    w_down,
    m_down,
    a_down,
    b_down,
):
    rows, span, width = layer_input.shape
    seqs = lax.axis_size("seq")
    tokens = rows * span
    cols = w_qkv.shape[2]
    hidden = w_gu.shape[2]
    hpad = pad_to(hidden)

    positions = lax.axis_index("seq") * span + jnp.arange(span, dtype=jnp.int32)
    freqs = ROPE_BASE ** (-jnp.arange(HD // 2, dtype=F32) * 2.0 / HD)
    turned = positions.astype(F32)[:, None] * freqs[None, :]
    cosines = jnp.concatenate([jnp.cos(turned)] * 2, axis=1)
    sines = jnp.concatenate([-jnp.sin(turned), jnp.sin(turned)], axis=1)
    x = layer_input.reshape(tokens, width)
    t_qkv, t_gu = a_qkv.transpose(0, 2, 1), a_gu.transpose(0, 2, 1)
    t_out, t_down = a_out.T, a_down.T
    (
        query,
        kept,
        mixed,
        lse,
        n2_qkv,
        n2_gu,
        n2_model,
        s_qkv,
        s_gu,
        s_out,
        s_down,
        full_t_out,
        av_out,
        av_down,
        normed1,
        vb_qkv,
        full_out,
        vb_gu,
        vb_down,
        pairs,
    ) = front(
        rows,
        seqs,
        float(lax.axis_size("row") * seqs),
        lengths,
        gain_attn[None],
        m_qkv,
        m_out[None],
        m_gu,
        m_down[None],
        t_qkv,
        b_qkv,
        t_out,
        b_out,
        t_gu,
        b_gu,
        t_down,
        b_down,
        cosines,
        sines,
        x,
        w_qkv,
        w_out,
        w_gu.transpose(0, 2, 1),
        w_down,
    )
    cot = cotangent.reshape(tokens, width)
    (
        hidden1,
        grad_h1,
        grad_mixed,
        pack,
        ffn_part,
    ) = feed(
        span,
        lengths,
        mixed,
        s_out,
        gain_ffn[None],
        s_gu,
        s_down,
        n2_gu,
        b_gu,
        t_gu.reshape(2 * RANK, width),
        t_down,
        b_down,
        b_out,
        full_t_out,
        av_out,
        av_down,
        x,
        cot,
        full_out,
        vb_gu,
        vb_down,
    )
    dqkv, e_qkv, output, e_down = back(
        rows,
        lengths,
        query,
        mixed,
        lse,
        grad_mixed,
        kept,
        cosines,
        sines,
        s_qkv,
        s_down,
        hidden1,
        cot,
        pairs,
        ffn_part,
    )
    grad_x, summed, summed_qkv = close(
        cols,
        dqkv,
        vb_qkv,
        normed1,
        x,
        gain_attn[None],
        grad_h1,
        b_qkv,
        t_qkv.reshape(3 * RANK, width),
        e_qkv,
        n2_qkv,
        pack,
        e_down,
    )
    (
        output,
        grad_x,
        gm_qkv,
        ga_qkv,
        gb_qkv,
        gm_out,
        ga_out,
        gb_out,
        gm_gu,
        ga_gu,
        gb_gu,
        gm_down,
        ga_down,
        gb_down,
    ) = finish(
        hidden,
        cols,
        summed,
        summed_qkv,
        m_qkv,
        m_out[None],
        m_gu,
        m_down[None],
        n2_model,
        b_out,
        b_down,
        vb_down,
        full_out,
        output,
        grad_x,
    )
    return (
        output.reshape(rows, span, width),
        grad_x.reshape(rows, span, width),
        gm_qkv,
        ga_qkv.transpose(0, 2, 1),
        gb_qkv,
        gm_out[0],
        ga_out.T,
        gb_out,
        gm_gu,
        ga_gu.transpose(0, 2, 1),
        gb_gu,
        gm_down[0],
        ga_down.T,
        gb_down,
    )


def solution(mesh):
    placed = (
        P("row", "seq", None),
        P("row", "seq", None),
        P("row"),
        P(),
        P(),
        P(None, None, "head"),
        P(None, "head"),
        P(),
        P(None, None, "head"),
        P("head", None),
        P(),
        P("head", None),
        P(),
        P(None, None, "head"),
        P(None, "head"),
        P(),
        P(None, None, "head"),
        P("head", None),
        P(),
        P("head", None),
        P(),
    )
    return jax.shard_map(
        shards,
        mesh=mesh,
        in_specs=placed,
        out_specs=(
            P("row", "seq", None),
            P("row", "seq", None),
            P(None, "head"),
            P(),
            P(None, None, "head"),
            P(),
            P("head", None),
            P(),
            P(None, "head"),
            P(),
            P(None, None, "head"),
            P(),
            P("head", None),
            P(),
        ),
        check_vma=False,
    )
```

```python
import functools

import jax
import jax.numpy as jnp
from jax import lax
from jax.experimental import pallas as pl
from jax.experimental.pallas import tpu as pltpu
from jax.sharding import PartitionSpec as P

HD = 128
RANK = 16
SCALE = 2.0
EPS = 1e-05
ROPE_BASE = 10000.0
MASKED = -1000000000.0
F32 = jnp.float32
BF16 = jnp.bfloat16


def pad_to(n, m=256):
    return -(-n // m) * m


def mm(a, b, dims):
    return lax.dot_general(a, b, (dims, ((), ())), preferred_element_type=F32)


def nn(a, b):
    return mm(a, b, ((1,), (0,)))


def nt(a, b):
    return mm(a, b, ((1,), (1,)))


def tn(a, b):
    return mm(a, b, ((0,), (0,)))


MESH = pl.DeviceIdType.MESH
VMEM = pl.BlockSpec(memory_space=pltpu.VMEM)
ROOM = 60 * 2**20
RING = 4
PARTS = 8


class Place:
    def __init__(self):
        self.row, self.seq, self.me = (lax.axis_index(n) for n in ("row", "seq", "head"))
        self.y = lax.rem(self.me, RING)
        self.z = self.me // RING
        self.far = 1 - self.z
        self.cross = self.far * RING + self.y

    def side(self, step):
        return lax.rem(self.y + step + RING, RING)

    def at(self, head):
        return (self.row, self.seq, head)

    def greet(self):
        barrier = pltpu.get_barrier_semaphore()
        for step in range(1, PARTS):
            pl.semaphore_signal(
                barrier, inc=1, device_id=self.at(lax.rem(self.me + step, PARTS)), device_id_type=MESH
            )
        pl.semaphore_wait(barrier, PARTS - 1)

    def send(self, source, target, sems, index, head):
        copy = pltpu.make_async_remote_copy(
            src_ref=source,
            dst_ref=target,
            send_sem=sems[0].at[index],
            recv_sem=sems[1].at[index],
            device_id=self.at(head),
            device_id_type=MESH,
        )
        copy.start()
        return copy


def rows_of(index, count):
    return pl.ds(pl.multiple_of(index * count, count), count)


EVEN = {"a": (0, 640, 1152), "b": (1152, 1536, 2048)}
RING_FIRST = {"a": (0, 768, 1536), "b": (1536, 1792, 2048)}
RING_MOST = {"a": (0, 896, 1792), "b": (1792, 1920, 2048)}
UP, DOWN = 1, -1


def span_of(spans, which, half=None):
    first, split, last = spans[which]
    if half == UP:
        last = split
    if half == DOWN:
        first = split
    return first, last


class Gather:
    def __init__(self, place, buf, chunk, sems, spans, stride=None, offset=0):
        self.place, self.buf, self.chunk, self.sems, self.spans = place, buf, chunk, sems, spans
        self.stride, self.offset = stride or chunk, offset
        self.sent = []

    def view(self, head, which=None, half=None):
        first = head * self.stride + self.offset * self.chunk
        rows = pl.ds(pl.multiple_of(first, self.chunk), self.chunk)
        if which is None:
            return self.buf.at[rows]
        first, last = span_of(self.spans, which, half)
        return self.buf.at[rows, first:last]

    def pass_on(self, head, which, half, index, to):
        view = self.view(head, which, half)
        copy = self.place.send(view, view, self.sems, index, to)
        self.sent.append(copy)
        return copy

    def ring(self, head, which, index):
        p = self.place
        return {
            way: self.pass_on(head, which, None, index + i, p.z * RING + p.side(way))
            for i, way in enumerate((UP, DOWN))
        }

    def relay(self, copies, plane, which, index, then=None):
        p = self.place
        made = []
        for i, way in enumerate((UP, DOWN)):
            copies[way].wait_recv()
            head = plane * RING + p.side(-way)
            made.append(self.pass_on(head, which, way, index + i, p.z * RING + p.side(way)))
            if then is not None:
                then(head, i)
        return made

    def start(self):
        p = self.place
        self.rest = []
        self.a_cross = self.pass_on(p.me, "a", None, 0, p.cross)
        self.b_ring = self.ring(p.me, "b", 6)
        self.a_ring = self.ring(p.me, "a", 8)
        self.rest.append(self.pass_on(p.me, "b", None, 1, p.cross))

    def first(self):
        p = self.place

        def across(head, i):
            self.rest.append(self.pass_on(head, "b", None, 2 + i, p.cross))

        self.b_relay = self.relay(self.b_ring, p.z, "b", 10, across)
        self.a_cross.wait_recv()
        self.far_ring = self.ring(p.cross, "a", 14)
        self.a_relay = self.relay(self.a_ring, p.z, "a", 12)

    def middle(self):
        p = self.place
        opposite = p.z * RING + p.side(2)
        for i, way in enumerate((UP, DOWN)):
            self.b_relay[i].wait_recv()
            self.rest.append(self.pass_on(opposite, "b", way, 4 + i, p.cross))
        for copy in self.a_relay:
            copy.wait_recv()

    def late(self):
        self.rest += self.relay(self.far_ring, self.place.far, "a", 16)

    def end(self):
        for copy in self.rest:
            copy.wait_recv()
        for copy in self.sent:
            copy.wait_send()


GATHER_SEMS = 18


class Scatter:
    def __init__(self, place, src, out, chunk, spans, scratch):
        self.place, self.src, self.out, self.chunk = place, src, out, chunk
        self.spans = spans
        self.cut = spans["a"][2]
        (
            self.far_b,
            self.hold_b,
            self.relay_b,
            self.land_b,
            self.hold_a,
            self.relay_a,
            self.land_a,
            self.hold_far,
            self.land_far,
            s,
            r,
        ) = scratch
        self.sems = (s, r)
        self.sent = []
        self.a_relay = [None, None]

    @staticmethod
    def scratch(chunk, width, spans):
        a = spans["a"][2]
        b = width - a
        return [
            pltpu.VMEM((RING, chunk, b), BF16),
            pltpu.VMEM((3, chunk, b), BF16),
            pltpu.VMEM((chunk, b), BF16),
            pltpu.VMEM((2, chunk, b), BF16),
            pltpu.VMEM((2, 2, chunk, a), BF16),
            pltpu.VMEM((2, chunk, a), BF16),
            pltpu.VMEM((2, 2, chunk, a), BF16),
            pltpu.VMEM((chunk, a), BF16),
            pltpu.VMEM((chunk, a), BF16),
            pltpu.SemaphoreType.DMA((17,)),
            pltpu.SemaphoreType.DMA((17,)),
        ]

    def send(self, source, target, index, head):
        copy = self.place.send(source, target, self.sems, index, head)
        self.sent.append(copy)
        return copy

    def mine(self, plane, y, which):
        first, last = span_of(self.spans, which)
        return self.src[rows_of(plane * RING + y, self.chunk), first:last].astype(F32)

    def within(self, which, half):
        base = self.spans[which][0]
        first, last = span_of(self.spans, which, half)
        return slice(first - base, last - base)

    def opposite(self, source, target, which, index):
        p = self.place
        made = {}
        for i, half in enumerate((UP, DOWN)):
            part = self.within(which, half)
            made[half] = self.send(
                source(half, part), target.at[:, part], index + i, p.z * RING + p.side(-half)
            )
        return made

    def start_b(self):
        p = self.place
        self.across = []
        for i, step in enumerate((2, DOWN, UP, 0)):
            view = self.src.at[rows_of(p.far * RING + p.side(step), self.chunk), self.cut :]
            self.across.append(self.send(view, self.far_b.at[i], i, p.cross))

    def start_a(self, k):
        p = self.place
        plane = p.z if k else p.far
        rows = rows_of(plane * RING + p.side(2), self.chunk)

        def source(half, part):
            return self.src.at[rows, part]

        self.a_relay[k] = self.opposite(source, self.relay_a.at[k], "a", 5 + 2 * k)

    def first(self):
        p = self.place
        self.a_direct = []
        for k, plane in enumerate((p.far, p.z)):
            made = {}
            for i, way in enumerate((DOWN, UP)):
                half = -way
                part = self.within("a", half)
                self.a_relay[k][half].wait_recv()
                self.hold_a[k, i] = self.mine(plane, p.side(way), "a").astype(BF16)
                self.hold_a[k, i, :, part] = (
                    self.hold_a[k, i, :, part].astype(F32) + self.relay_a[k, :, part].astype(F32)
                ).astype(BF16)
                made[way] = self.send(
                    self.hold_a.at[k, i],
                    self.land_a.at[k, i],
                    9 + 2 * k + i,
                    p.z * RING + p.side(way),
                )
            self.a_direct.append(made)
        self.across[0].wait_recv()
        total = self.mine(p.z, p.side(2), "b") + self.far_b[0].astype(F32)
        self.hold_b[2] = total.astype(BF16)

        def source(half, part):
            return self.hold_b.at[2, :, part]

        self.b_relay = self.opposite(source, self.relay_b, "b", 13)

    def middle(self):
        p = self.place
        total = self.mine(p.far, p.y, "a")
        for i, way in enumerate((DOWN, UP)):
            self.a_direct[0][way].wait_recv()
            total += self.land_a[0, i].astype(F32)
        self.hold_far[...] = total.astype(BF16)
        self.last = self.send(self.hold_far, self.land_far, 4, p.cross)

    def late(self):
        p = self.place
        self.b_direct = []
        for i, way in enumerate((DOWN, UP)):
            half = -way
            part = self.within("b", half)
            self.across[1 + i].wait_recv()
            total = self.mine(p.z, p.side(way), "b") + self.far_b[1 + i].astype(F32)
            self.b_relay[half].wait_recv()
            self.hold_b[i] = total.astype(BF16)
            self.hold_b[i, :, part] = (
                total[:, part] + self.relay_b[:, part].astype(F32)
            ).astype(BF16)
            self.b_direct.append(
                self.send(
                    self.hold_b.at[i], self.land_b.at[i], 15 + i, p.z * RING + p.side(way)
                )
            )

    def end(self):
        p = self.place
        total = self.mine(p.z, p.y, "a")
        for i, way in enumerate((DOWN, UP)):
            self.a_direct[1][way].wait_recv()
            total += self.land_a[1, i].astype(F32)
        self.across[3].wait_recv()
        rest = self.mine(p.z, p.y, "b") + self.far_b[3].astype(F32)
        for i in range(2):
            self.b_direct[i].wait_recv()
            rest += self.land_b[i].astype(F32)
        self.out[:, self.cut :] = rest
        self.last.wait_recv()
        self.out[:, : self.cut] = total + self.land_far[...].astype(F32)
        for copy in self.sent:
            copy.wait_send()


def feed_kernel(
    span,
    lengths,
    mixed_ref,
    s_out,
    gain,
    s_gu,
    s_down,
    n2_gu,
    b_gu_raw,
    t_gu,
    t_down,
    b_down,
    b_out,
    at_out,
    av_out,
    av_down,
    x_hbm,
    cot_hbm,
    vout_hbm,
    vgu_hbm,
    vdown_hbm,
    h1_ref,
    dh1_ref,
    dmix_ref,
    pack,
    ffn_hbm,
    ffn_ref,
    vout,
    vgu,
    vdown,
    dys,
    xn2,
    part,
    dhid,
    hid,
    dgu,
    x_own,
    mixed_own,
    dmix_own,
    attn,
    sum_own,
    b_gu,
    at_down,
    local_sems,
    swap_s,
    swap_r,
    back_s,
    back_r,
    gather_s,
    gather_r,
    *scatter_scratch,
):
    tokens, width = xn2.shape
    chunk = tokens // PARTS
    block = tokens // 2
    cols = mixed_ref.shape[1]
    hpad = hid.shape[1]
    tile = 256
    p = Place()
    own = rows_of(p.me, chunk)
    loads = []
    for i, (src, dst) in enumerate(
        [
            (x_hbm.at[own], x_own),
            (vout_hbm, vout),
            (cot_hbm, dys),
            (vdown_hbm, vdown),
            (vgu_hbm, vgu),
        ]
    ):
        loads.append(pltpu.make_async_copy(src, dst, local_sems.at[i]))
        loads[-1].start()
    p.greet()

    my_cols = rows_of(p.me, cols)
    swaps = []
    for step in range(1, PARTS):
        to = lax.rem(p.me + step, PARTS)
        swaps.append(
            p.send(
                mixed_ref.at[rows_of(to, chunk)],
                mixed_own.at[:, my_cols],
                (swap_s, swap_r),
                step - 1,
                to,
            )
        )
    mixed_own[:, my_cols] = mixed_ref[own, :]

    hidden = t_down.shape[1]
    b_gu[...] = jnp.zeros_like(b_gu)
    at_down[...] = jnp.zeros_like(at_down)
    for k in range(2):
        b_gu[:, k * hpad : k * hpad + hidden] = b_gu_raw[k].astype(BF16)
    at_down[:, :hidden] = t_down[...].astype(BF16)
    def back_hidden(half):
        rows = slice(half * block, (half + 1) * block)

        @pl.loop(0, hpad // tile)
        def _(n):
            units = rows_of(n, tile)
            dhid[rows, units] = nt(dys[rows, :], vdown[units, :]).astype(BF16)


    for copy in swaps:
        copy.wait_recv()
    loads[0].wait()
    loads[1].wait()

    @pl.loop(0, width // 512)
    def _(n):
        part_cols = rows_of(n, 512)
        attn[:, part_cols] = nn(mixed_own[...], vout[:, part_cols]) * s_out[:, part_cols]

    h1_ref[...] = x_own[...].astype(F32) + attn[...]
    inv2 = lax.rsqrt(jnp.mean(h1_ref[...] * h1_ref[...], axis=-1, keepdims=True) + EPS)
    xn2[own, :] = (h1_ref[...] * inv2 * gain[...]).astype(BF16)
    gather = Gather(p, xn2, chunk, (gather_s, gather_r), EVEN)
    gather.start()
    own_rows = slice(COMMON_FEED, COMMON_FEED + RANK)
    fold_rows = slice(COMMON_FEED + RANK, COMMON_FEED + OWN_FEED)
    e_row = slice(COMMON_FEED + RANK, COMMON_FEED + RANK + 1)
    e_first = width - 2 * hpad
    pack[...] = jnp.zeros_like(pack)
    at = 5 * RANK
    for piece in (av_out, av_down):
        pack[at : at + RANK, :] = piece[...]
        at += RANK
    loads[2].wait()
    loads[3].wait()
    seq = lax.axis_index("seq")

    @pl.loop(0, PARTS)
    def _(i):
        rows = rows_of(i, chunk)
        base = lax.rem(i * chunk, span)
        length = lengths[0]
        for r in range(1, tokens // span):
            length = jnp.where(i * chunk >= r * span, lengths[r], length)
        pos = seq * span + base + lax.broadcasted_iota(jnp.int32, (chunk, 1), 0)
        live = (pos < length).astype(F32)
        dys[rows, :] = (dys[rows, :].astype(F32) * live * s_down[...]).astype(BF16)

    back_hidden(0)
    back_hidden(1)
    loads[4].wait()

    def hidden_units(plane):
        rows = rows_of(plane, block)

        @pl.loop(0, hpad // tile)
        def _(n):
            at_gate = rows_of(n, tile)
            at_up = rows_of(n + hpad // tile, tile)
            of_gate = rows_of(n + e_first // tile, tile)
            of_up = rows_of(n + (e_first + hpad) // tile, tile)
            gate = nt(xn2[rows, :], vgu[at_gate, :]) * s_gu[:, at_gate]
            up = nt(xn2[rows, :], vgu[at_up, :]) * s_gu[:, at_up]
            sigma = jax.nn.sigmoid(gate)
            active = gate * sigma
            hid[rows, at_gate] = (active * up).astype(BF16)
            back = dhid[rows, at_gate].astype(F32)
            grad_gate = back * up * sigma * (1.0 + gate * (1.0 - sigma))
            grad_up = back * active
            pack[e_row, of_gate] += jnp.sum(grad_gate * gate, axis=0, keepdims=True)
            pack[e_row, of_up] += jnp.sum(grad_up * up, axis=0, keepdims=True)
            dgu[rows, at_gate] = (grad_gate * s_gu[:, at_gate]).astype(BF16)
            dgu[rows, at_up] = (grad_up * s_gu[:, at_up]).astype(BF16)

    def back_part(plane, first, last):
        rows = rows_of(plane, block)

        @pl.loop(first // 512, last // 512)
        def _(n):
            part_cols = rows_of(n, 512)
            part[rows, part_cols] = nn(dgu[rows, :], vgu[:, part_cols]).astype(BF16)

    scatter = Scatter(p, part, sum_own, chunk, EVEN, scatter_scratch)
    gather.first()
    gather.middle()
    hidden_units(p.z)
    gather.late()
    back_part(p.z, 0, width)
    scatter.start_a(1)
    gather.end()
    hidden_units(p.far)
    back_part(p.far, 1024, width)
    scatter.start_b()
    back_part(p.far, 0, 1024)
    scatter.start_a(0)

    def forward_part(half):
        rows = slice(half * block, (half + 1) * block)

        @pl.loop(0, width // 512)
        def _(n):
            part_cols = rows_of(n, 512)
            ffn_ref[rows, part_cols] = nn(hid[rows, :], vdown[:, part_cols]).astype(BF16)

    t_one = []
    for k in range(2):
        part_cols = slice(k * hpad, (k + 1) * hpad)
        t_one.append(nt(b_gu[:, part_cols], dgu[:, part_cols]).astype(BF16))
    t_one = jnp.concatenate(t_one, axis=0)
    left_gu = t_gu[...].astype(BF16)
    x_gu = nt(left_gu, xn2[...]).astype(BF16)
    scatter.first()
    ratio = pack[e_row, e_first:] / n2_gu[...]
    back_gu = (b_gu[...].astype(F32) * ratio).astype(BF16)
    for n in range(0, width, 512):
        at = slice(n, n + 512)
        first = nn(t_one, xn2[:, at])
        for k in range(2):
            units = slice(k * hpad, (k + 1) * hpad)
            pack[k * RANK : (k + 1) * RANK, at] = first[k * RANK : (k + 1) * RANK] - nn(
                back_gu[:, units], vgu[units, at]
            )
    forward_part(0)
    forward_part(1)
    store = pltpu.make_async_copy(ffn_ref, ffn_hbm, local_sems.at[6])
    store.start()
    scatter.middle()
    scatter.late()
    for k in range(2):
        part_cols = slice(k * hpad, (k + 1) * hpad)
        both = slice(k * RANK, (k + 1) * RANK)
        pack[own_rows, part_cols] = (
            nn(x_gu[both], dgu[:, part_cols])
            - nt(left_gu[both], vgu[part_cols, :]) * ratio[:, part_cols]
        )
    back_down = nt(b_down[...].astype(BF16), dys[...]).astype(BF16)
    ga_down = nn(back_down, hid[...])
    fits = width - 2 * hpad
    pack[own_rows, 2 * hpad :] = ga_down[:, :fits]
    pack[fold_rows, : hpad - fits] = ga_down[:, fits:]
    x_down = nt(at_down[...], hid[...]).astype(BF16)
    for n in range(0, width, 512):
        pack[3 * RANK : 4 * RANK, n : n + 512] = nn(x_down, dys[:, n : n + 512])
    scatter.end()

    length = lengths[0]
    for r in range(1, tokens // span):
        length = jnp.where(p.me * chunk >= r * span, lengths[r], length)
    pos = seq * span + lax.rem(p.me * chunk, span) + lax.broadcasted_iota(jnp.int32, (chunk, 1), 0)
    live = (pos < length).astype(F32)
    dy_copy = pltpu.make_async_copy(cot_hbm.at[own], x_own, local_sems.at[5])
    dy_copy.start()
    scaled = sum_own[...] * gain[...]
    h1 = h1_ref[...]
    mean = jnp.mean(scaled * h1, axis=-1, keepdims=True)
    dy_copy.wait()
    grad = x_own[...].astype(F32) * live + inv2 * (scaled - h1 * (inv2 * inv2 * mean))
    dh1_ref[...] = grad
    low = grad.astype(BF16).astype(F32)
    pack[7 * RANK : 7 * RANK + 1, :] = jnp.sum(low * attn[...], axis=0, keepdims=True)
    das = (low * s_out[...]).astype(BF16)

    @pl.loop(0, width // 512)
    def _(n):
        part_cols = rows_of(n, 512)
        dmix_own[:, part_cols] = nt(das, vout[part_cols, :]).astype(BF16)

    backs = []
    for step in range(1, PARTS):
        to = lax.rem(p.me + step, PARTS)
        backs.append(
            p.send(
                dmix_own.at[:, rows_of(to, cols)],
                dmix_ref.at[own],
                (back_s, back_r),
                step - 1,
                to,
            )
        )
    dmix_ref[own, :] = dmix_own[:, my_cols]
    t_out = nt(b_out[...].astype(BF16), das).astype(BF16)
    pack[4 * RANK : 5 * RANK, :] = nn(t_out, mixed_own[...])
    x_out = nt(at_out[...], mixed_own[...]).astype(BF16)
    pack[2 * RANK : 3 * RANK, :] = nn(x_out, das)
    for copy in backs:
        copy.wait_recv()
    for copy in swaps + backs:
        copy.wait_send()
    store.wait()


def feed(span, lengths, mixed, *rest):
    tokens, cols = mixed.shape
    hpad, width = rest[-1].shape
    chunk = tokens // PARTS
    shape = jax.ShapeDtypeStruct
    out_shape = (
        shape((chunk, width), F32),
        shape((chunk, width), F32),
        shape((tokens, cols), BF16),
        shape((COMMON_FEED + OWN_FEED, width), F32),
        shape((tokens, width), BF16),
    )
    dma = pltpu.SemaphoreType.DMA
    scratch = [
        pltpu.VMEM((tokens, width), BF16),
        pltpu.VMEM((width, width), BF16),
        pltpu.VMEM((2 * hpad, width), BF16),
        pltpu.VMEM((hpad, width), BF16),
        pltpu.VMEM((tokens, width), BF16),
        pltpu.VMEM((tokens, width), BF16),
        pltpu.VMEM((tokens, width), BF16),
        pltpu.VMEM((tokens, hpad), BF16),
        pltpu.VMEM((tokens, hpad), BF16),
        pltpu.VMEM((tokens, 2 * hpad), BF16),
        pltpu.VMEM((chunk, width), BF16),
        pltpu.VMEM((chunk, width), BF16),
        pltpu.VMEM((chunk, width), BF16),
        pltpu.VMEM((chunk, width), F32),
        pltpu.VMEM((chunk, width), F32),
        pltpu.VMEM((RANK, 2 * hpad), BF16),
        pltpu.VMEM((RANK, hpad), BF16),
        dma((7,)),
        dma((PARTS - 1,)),
        dma((PARTS - 1,)),
        dma((PARTS - 1,)),
        dma((PARTS - 1,)),
        dma((GATHER_SEMS,)),
        dma((GATHER_SEMS,)),
    ]
    scratch += Scatter.scratch(chunk, width, EVEN)
    anywhere = pl.BlockSpec(memory_space=pl.ANY)
    return pl.pallas_call(
        functools.partial(feed_kernel, span),
        out_shape=out_shape,
        in_specs=[pl.BlockSpec(memory_space=pltpu.SMEM)] + [VMEM] * 14 + [anywhere] * 5,
        out_specs=[VMEM] * 4 + [anywhere],
        scratch_shapes=scratch,
        compiler_params=pltpu.CompilerParams(
            collective_id=1, has_side_effects=True, vmem_limit_bytes=ROOM
        ),
    )(lengths, mixed, *rest)


def turn(values, cosines, sines):
    return values * cosines + pltpu.roll(values, HD // 2, 1) * sines


def scores_of(q, keys, query_pos, key_pos, first, length):
    scores = nt(q, keys) * HD ** (-0.5)
    at = key_pos + first
    return jnp.where((at <= query_pos) & (at < length), scores, MASKED)


def back_kernel(
    rows,
    lengths,
    cosines,
    sines,
    s_qkv,
    s_down,
    q_hbm,
    mixed_hbm,
    lse_hbm,
    dmix_hbm,
    kept_hbm,
    h1_hbm,
    cot_hbm,
    kv_hbm,
    ffn_hbm,
    dqkv_ref,
    e_qkv,
    out_ref,
    e_down,
    gather_s,
    gather_r,
    q_ref,
    mixed_ref,
    lse_ref,
    dmix_ref,
    kept_ref,
    h1_ref,
    kv_ref,
    ffn_ref,
    dkv,
    sib_far,
    hold,
    far,
    sib,
    dq,
    inner,
    total_own,
    dy_own,
    local_sems,
    send_sems,
    recv_sems,
    *scratch,
):
    tokens, cols = q_ref.shape
    span = tokens // rows
    heads = cols // HD
    chunk = tokens // PARTS
    p = Place()
    core = lax.rem(p.seq, 2)
    upper = p.seq // 2
    sibling = upper * 2 + 1 - core
    loads = []
    for i, (src, dst) in enumerate(
        [
            (ffn_hbm, ffn_ref),
            (kv_hbm, kv_ref),
            (q_hbm, q_ref),
            (dmix_hbm, dmix_ref),
            (mixed_hbm, mixed_ref),
            (lse_hbm, lse_ref),
            (kept_hbm, kept_ref),
            (h1_hbm, h1_ref),
            (cot_hbm.at[rows_of(p.me, chunk)], dy_own),
        ]
    ):
        loads.append(pltpu.make_async_copy(src, dst, local_sems.at[i]))
        loads[-1].start()
    barrier = pltpu.get_barrier_semaphore()
    for step in range(1, PARTS):
        place = p.at(lax.rem(p.me + step, PARTS))
        pl.semaphore_signal(barrier, inc=1, device_id=place, device_id_type=MESH)
    for seq in (sibling, (1 - upper) * 2 + core):
        pl.semaphore_signal(barrier, inc=1, device_id=(p.row, seq, p.me), device_id_type=MESH)
    e_qkv[...] = jnp.zeros_like(e_qkv)
    dq[...] = jnp.zeros_like(dq)
    pl.semaphore_wait(barrier, PARTS + 1)
    loads[0].wait()
    scatter = Scatter(p, ffn_ref, total_own, chunk, RING_FIRST, scratch)
    scatter.start_b()
    scatter.start_a(0)
    scatter.start_a(1)

    def over(source, target, index, seq):
        return pltpu.make_async_remote_copy(
            src_ref=source,
            dst_ref=target,
            send_sem=send_sems.at[index],
            recv_sem=recv_sems.at[index],
            device_id=(p.row, seq, p.me),
            device_id_type=MESH,
        )

    to_sib_far = []
    to_sib = []
    to_far = []
    for r in range(rows):
        part = slice(r * span, (r + 1) * span)
        to_sib_far.append(over(dkv.at[1 - core, part], sib_far.at[part], r, sibling))
        to_sib.append(over(dkv.at[upper * 2, part], sib.at[part], rows + r, sibling))
        to_far.append(over(hold.at[part], far.at[part], 2 * rows + r, core))

    for load in loads[1:7]:
        load.wait()
    query_pos = p.seq * span + lax.broadcasted_iota(jnp.int32, (span, span), 0)
    key_pos = lax.broadcasted_iota(jnp.int32, (span, span), 1)

    for r in range(rows):
        part = slice(r * span, (r + 1) * span)
        for head in range(heads):
            at = slice(head * HD, (head + 1) * HD)
            i = r * heads + head
            inner[:, i : i + 1] = jnp.sum(
                dmix_ref[part, at].astype(F32) * mixed_ref[part, at].astype(F32),
                axis=-1,
                keepdims=True,
            )

    def blocks(r, head, first, last):
        part = slice(r * span, (r + 1) * span)
        kcols = slice(head * HD, (head + 1) * HD)
        vcols = slice(cols + head * HD, cols + (head + 1) * HD)
        i = r * heads + head

        @pl.loop(first, last)
        def _(j):
            q = q_ref[part, kcols]
            do = dmix_ref[part, kcols]
            lse = lse_ref[part, head * HD : head * HD + 1]
            scores = scores_of(q, kv_ref[j, part, kcols], query_pos, key_pos, j * span, lengths[r])
            probs = jnp.exp(scores - lse)
            dkv[j, part, vcols] = tn(probs.astype(BF16), do).astype(BF16)
            grad = (probs * (nt(do, kv_ref[j, part, vcols]) - inner[:, i : i + 1])).astype(BF16)
            dq[part, kcols] += nn(grad, kv_ref[j, part, kcols])
            dkv[j, part, kcols] = (tn(grad, q) * HD ** (-0.5)).astype(BF16)

    def onward(r):
        part = slice(r * span, (r + 1) * span)

        @pl.when(upper == 1)
        def _():
            to_sib_far[r].wait_recv()
            hold[part] = (dkv[core, part].astype(F32) + sib_far[part].astype(F32)).astype(BF16)
            to_far[r].start()

    def emit(part, at, grad):
        held = kept_ref[part, at].astype(F32)
        e_qkv[:, at] += jnp.sum(grad * held, axis=0, keepdims=True)
        dqkv_ref[part, at] = (grad * s_qkv[:, at]).astype(BF16)

    def results():
        loads[7].wait()
        loads[8].wait()
        length = lengths[0]
        for r in range(1, rows):
            length = jnp.where(p.me * chunk >= r * span, lengths[r], length)
        first = p.seq * span + lax.rem(p.me * chunk, span)
        pos = first + lax.broadcasted_iota(jnp.int32, (chunk, 1), 0)
        live = (pos < length).astype(F32)
        ffn = total_own[...] * s_down[...]
        out_ref[rows_of(p.me, chunk), :] = ((h1_ref[...] + ffn) * live).astype(BF16)
        e_down[...] = jnp.sum(dy_own[...].astype(F32) * live * ffn, axis=0, keepdims=True)

    for r in range(rows):
        for head in range(heads):
            blocks(r, head, 0, 2 * upper)

        @pl.when(upper == 1)
        def _(r=r):
            to_sib_far[r].start()

        if r == 0:
            scatter.first()
        else:
            onward(r - 1)
    for r in range(rows):
        for head in range(heads):
            blocks(r, head, 2 * upper, p.seq + 1)
            if r == 0 and head == 0:
                scatter.middle()
                scatter.late()
                onward(rows - 1)
            if r == 1 and head == 0:
                scatter.end()
                results()
                gather = Gather(p, out_ref, chunk, (gather_s, gather_r), RING_FIRST)
                gather.start()

        @pl.when(core == 1)
        def _(r=r):
            to_sib[r].start()

    gather.first()
    for r in range(rows):
        part = slice(r * span, (r + 1) * span)
        for head in range(heads):
            at = slice(head * HD, (head + 1) * HD)
            emit(part, at, turn(dq[part, at] * HD ** (-0.5), cosines[...], -sines[...]))
    gather.middle()

    for r in range(rows):
        part = slice(r * span, (r + 1) * span)

        @pl.when(core == 0)
        def _(r=r):
            to_sib[r].wait_recv()

        @pl.when(upper == 0)
        def _(r=r):
            to_far[r].wait_recv()

        for head in range(2 * heads):
            at = slice(head * HD, (head + 1) * HD)
            grad = dkv[p.seq, part, at].astype(F32)
            grad = grad + jnp.where(core == 0, sib[part, at].astype(F32), 0.0)
            grad = grad + jnp.where(upper == 0, far[part, at].astype(F32), 0.0)
            if head < heads:
                grad = turn(grad, cosines[...], -sines[...])
            emit(part, slice(cols + head * HD, cols + (head + 1) * HD), grad)
        if r == 0:
            gather.late()
    gather.end()

    for r in range(rows):

        @pl.when(upper == 1)
        def _(r=r):
            to_sib_far[r].wait_send()
            to_far[r].wait_send()

        @pl.when(core == 1)
        def _(r=r):
            to_sib[r].wait_send()


def back(rows, lengths, *rest):
    q, mixed, lse, dmix, kept, h1, _, kv, ffn = rest[-9:]
    tokens, cols = q.shape
    width = ffn.shape[1]
    chunk = tokens // PARTS
    shape = jax.ShapeDtypeStruct
    dma = pltpu.SemaphoreType.DMA
    out_shape = (
        shape((tokens, 3 * cols), BF16),
        shape((1, 3 * cols), F32),
        shape((tokens, width), BF16),
        shape((1, width), F32),
    )
    scratch = [
        dma((GATHER_SEMS,)),
        dma((GATHER_SEMS,)),
        pltpu.VMEM(q.shape, BF16),
        pltpu.VMEM(mixed.shape, BF16),
        pltpu.VMEM(lse.shape, F32),
        pltpu.VMEM(dmix.shape, BF16),
        pltpu.VMEM(kept.shape, BF16),
        pltpu.VMEM(h1.shape, F32),
        pltpu.VMEM(kv.shape, BF16),
        pltpu.VMEM(ffn.shape, BF16),
        pltpu.VMEM(kv.shape, BF16),
        pltpu.VMEM((tokens, 2 * cols), BF16),
        pltpu.VMEM((tokens, 2 * cols), BF16),
        pltpu.VMEM((tokens, 2 * cols), BF16),
        pltpu.VMEM((tokens, 2 * cols), BF16),
        pltpu.VMEM((tokens, cols), F32),
        pltpu.VMEM((tokens // rows, rows * cols // HD), F32),
        pltpu.VMEM((chunk, width), F32),
        pltpu.VMEM((chunk, width), BF16),
        dma((9,)),
        dma((3 * rows,)),
        dma((3 * rows,)),
    ]
    scratch += Scatter.scratch(chunk, width, RING_FIRST)
    return pl.pallas_call(
        functools.partial(back_kernel, rows),
        out_shape=out_shape,
        in_specs=[pl.BlockSpec(memory_space=pltpu.SMEM)]
        + [VMEM] * 4
        + [pl.BlockSpec(memory_space=pl.ANY)] * 9,
        out_specs=[VMEM] * len(out_shape),
        scratch_shapes=scratch,
        compiler_params=pltpu.CompilerParams(
            collective_id=2, has_side_effects=True, vmem_limit_bytes=ROOM
        ),
    )(lengths, *rest)


COMMON_FEED, OWN_FEED = 128, 32
COMMON_QKV, OWN_QKV = 48, 16


class Total:
    def __init__(self, place, common, scratch):
        self.p = p = place
        self.common = common
        (
            self.send_buf,
            self.land_row,
            self.by_row,
            self.land_seq,
            self.mine,
            self.across,
            self.held,
            *self.sems,
        ) = scratch
        self.rows = [(lax.rem(p.row + step, RING), p.seq, p.me) for step in range(1, RING)]
        self.seqs = [(p.row, lax.rem(p.seq + step, RING), p.me) for step in range(1, RING)]
        self.heads = [p.at(lax.rem(p.me + step, PARTS)) for step in range(1, PARTS)]

    @staticmethod
    def scratch(common, own):
        dma = pltpu.SemaphoreType.DMA
        piece = (common + own, 128)
        return [
            pltpu.VMEM((RING * RING, *piece), BF16),
            pltpu.VMEM((RING - 1, RING, *piece), BF16),
            pltpu.VMEM((RING, *piece), BF16),
            pltpu.VMEM((RING - 1, *piece), BF16),
            pltpu.VMEM(piece, BF16),
            pltpu.VMEM((PARTS - 1, common, 128), BF16),
            pltpu.VMEM((RING * RING, *piece), BF16),
        ] + [dma((n,)) for n in (3, 3, 3, 3, PARTS - 1, PARTS - 1, 3, 3, 3, 3)]

    def greet(self):
        barrier = pltpu.get_barrier_semaphore()
        for place in self.rows + self.seqs + self.heads:
            pl.semaphore_signal(barrier, inc=1, device_id=place, device_id_type=MESH)
        pl.semaphore_wait(barrier, 2 * (RING - 1) + PARTS - 1)

    def fill(self, rows, source):
        for piece in range(RING * RING):
            self.send_buf[piece, rows] = source[:, piece * 128 : (piece + 1) * 128].astype(BF16)

    def copies(self, source, target, ends, stage):
        made = []
        for step, place in enumerate(ends):
            made.append(
                pltpu.make_async_remote_copy(
                    src_ref=source(place),
                    dst_ref=target(step),
                    send_sem=self.sems[2 * stage].at[step],
                    recv_sem=self.sems[2 * stage + 1].at[step],
                    device_id=place,
                    device_id_type=MESH,
                )
            )
            made[-1].start()
        return made

    def start(self):
        self.wait = self.copies(
            lambda place: self.send_buf.at[rows_of(place[0], RING)],
            lambda step: self.land_row.at[step],
            self.rows,
            0,
        )

    def second(self):
        for copy in self.wait:
            copy.wait()
        for q in range(RING):
            total = self.send_buf[self.p.row * RING + q].astype(F32)
            for step in range(RING - 1):
                total += self.land_row[step, q].astype(F32)
            self.by_row[q] = total.astype(BF16)
        self.wait = self.copies(
            lambda place: self.by_row.at[place[1]], lambda step: self.land_seq.at[step], self.seqs, 1
        )

    def third(self):
        for copy in self.wait:
            copy.wait()
        total = self.by_row[self.p.seq].astype(F32)
        for step in range(RING - 1):
            total += self.land_seq[step].astype(F32)
        self.mine[...] = total.astype(BF16)
        self.wait = self.copies(
            lambda place: self.mine.at[: self.common],
            lambda step: self.across.at[step],
            self.heads,
            2,
        )

    def fourth(self):
        for copy in self.wait:
            copy.wait()
        shared = self.mine[: self.common].astype(F32)
        for step in range(PARTS - 1):
            shared += self.across[step].astype(F32)
        here = self.p.row * RING + self.p.seq
        self.held[here, : self.common] = shared.astype(BF16)
        self.held[here, self.common :] = self.mine[self.common :]
        view = self.held.at[here]
        self.wait = self.copies(lambda place: view, lambda step: view, self.seqs, 3)

    def fifth(self):
        for copy in self.wait:
            copy.wait()
        view = self.held.at[rows_of(self.p.row, RING)]
        self.wait = self.copies(lambda place: view, lambda step: view, self.rows, 4)

    def end(self, out):
        for copy in self.wait:
            copy.wait()
        for piece in range(RING * RING):
            out[:, piece * 128 : (piece + 1) * 128] = self.held[piece].astype(F32)


def close_kernel(
    cols,
    dqkv_hbm,
    vqkv_hbm,
    xn1_hbm,
    x_hbm,
    dh1_hbm,
    pack_hbm,
    gain,
    b_raw,
    t_raw,
    e_qkv,
    n2_qkv,
    e_down,
    gx_ref,
    sum_feed,
    sum_qkv,
    part,
    pack,
    dqkv_ref,
    vqkv,
    dh1_ref,
    pack_feed,
    xn1,
    x_own,
    total_own,
    b_qkv,
    local_sems,
    gather_s,
    gather_r,
    *scratch,
):
    tokens, width = xn1_hbm.shape
    chunk = tokens // PARTS
    p = Place()
    own = rows_of(p.me, chunk)
    totals = Total(p, COMMON_QKV, scratch[:17])
    early = Total(p, COMMON_FEED, scratch[17:34])
    loads = []
    for i, (src, dst) in enumerate(
        [
            (dqkv_hbm, dqkv_ref),
            (vqkv_hbm, vqkv),
            (pack_hbm, pack_feed),
            (xn1_hbm, xn1),
            (x_hbm.at[own], x_own),
            (dh1_hbm, dh1_ref),
        ]
    ):
        loads.append(pltpu.make_async_copy(src, dst, local_sems.at[i]))
        loads[-1].start()
    totals.greet()
    loads[0].wait()
    loads[1].wait()

    def back_part(first, last):
        @pl.loop(first // 256, last // 256)
        def _(n):
            at = rows_of(n, 256)
            part[:, at] = nt(dqkv_ref[...], vqkv[at, :]).astype(BF16)

    scatter = Scatter(p, part, total_own, chunk, EVEN, scratch[34:])
    back_part(1024, width)
    scatter.start_b()
    back_part(0, 1024)
    scatter.start_a(0)
    scatter.start_a(1)
    loads[2].wait()
    early.fill(slice(None), pack_feed)
    row = 7 * RANK + 1
    early.fill(slice(row, row + 1), e_down)
    early.start()

    b_qkv[...] = jnp.zeros_like(b_qkv)
    for k in range(3):
        b_qkv[k * RANK : (k + 1) * RANK, k * cols : (k + 1) * cols] = b_raw[k].astype(BF16)
    t_qkv = t_raw[...].astype(BF16)
    ratio = e_qkv[...] / n2_qkv[...]
    back_qkv = (b_qkv[...].astype(F32) * ratio).astype(BF16)
    t_one = nt(b_qkv[...], dqkv_ref[...]).astype(BF16)
    loads[3].wait()
    t_two = nt(t_qkv, xn1[...]).astype(BF16)
    scatter.first()
    early.second()
    for n in range(0, width, 512):
        at = slice(n, n + 512)
        pack[: 3 * RANK, at] = nn(t_one, xn1[:, at]) - nt(back_qkv, vqkv[at, :])
        if n == width // 2:
            scatter.middle()
    gb = nn(t_two, dqkv_ref[...]) - nn(t_qkv, vqkv[...]) * ratio
    pack[COMMON_QKV:, :] = jnp.zeros((OWN_QKV, width), F32)
    for k in range(3):
        pack[COMMON_QKV:, k * cols : (k + 1) * cols] = gb[
            k * RANK : (k + 1) * RANK, k * cols : (k + 1) * cols
        ]
    pack[COMMON_QKV : COMMON_QKV + 1, 3 * cols : 6 * cols] = e_qkv[...]
    totals.fill(slice(None), pack)
    totals.start()
    scatter.late()
    early.third()
    loads[4].wait()
    loads[5].wait()
    x = x_own[...].astype(F32)
    inv1 = lax.rsqrt(jnp.mean(x * x, axis=-1, keepdims=True) + EPS)
    scatter.end()
    scaled = total_own[...] * gain[...]
    mean = jnp.mean(scaled * x, axis=-1, keepdims=True)
    grad = dh1_ref[...] + inv1 * (scaled - x * (inv1 * inv1 * mean))
    gx_ref[own, :] = grad.astype(BF16)
    gather = Gather(p, gx_ref, chunk, (gather_s, gather_r), EVEN)
    gather.start()
    totals.second()
    early.fourth()
    gather.first()
    totals.third()
    early.fifth()
    gather.middle()
    totals.fourth()
    gather.late()
    totals.fifth()
    early.end(sum_feed)
    gather.end()
    totals.end(sum_qkv)


def close(cols, dqkv, vqkv, xn1, x, dh1, pack, *rest):
    tokens, width = xn1.shape
    chunk = tokens // PARTS
    shape = jax.ShapeDtypeStruct
    dma = pltpu.SemaphoreType.DMA
    out_shape = (
        shape((tokens, width), BF16),
        shape((COMMON_FEED + OWN_FEED, width), F32),
        shape((COMMON_QKV + OWN_QKV, width), F32),
    )
    scratch = [
        pltpu.VMEM((tokens, width), BF16),
        pltpu.VMEM((COMMON_QKV + OWN_QKV, width), F32),
        pltpu.VMEM(dqkv.shape, BF16),
        pltpu.VMEM(vqkv.shape, BF16),
        pltpu.VMEM(dh1.shape, F32),
        pltpu.VMEM(pack.shape, F32),
        pltpu.VMEM((tokens, width), BF16),
        pltpu.VMEM((chunk, width), BF16),
        pltpu.VMEM((chunk, width), F32),
        pltpu.VMEM((3 * RANK, 3 * cols), BF16),
        dma((6,)),
        dma((GATHER_SEMS,)),
        dma((GATHER_SEMS,)),
    ]
    scratch += Total.scratch(COMMON_QKV, OWN_QKV) + Total.scratch(COMMON_FEED, OWN_FEED)
    scratch += Scatter.scratch(chunk, width, EVEN)
    return pl.pallas_call(
        functools.partial(close_kernel, cols),
        out_shape=out_shape,
        in_specs=[pl.BlockSpec(memory_space=pl.ANY)] * 6 + [VMEM] * len(rest),
        out_specs=[VMEM] * 3,
        scratch_shapes=scratch,
        compiler_params=pltpu.CompilerParams(
            collective_id=3, has_side_effects=True, vmem_limit_bytes=ROOM
        ),
    )(dqkv, vqkv, xn1, x, dh1, pack, *rest)


def three_terms(left, right):
    def split(a):
        high = a.astype(BF16)
        return high, (a - high.astype(F32)).astype(BF16)

    left_high, left_low = split(left)
    right_high, right_low = split(right)
    return (
        jnp.concatenate([left_high, left_low, left_high], axis=0),
        jnp.concatenate([right_high, right_high, right_low], axis=0),
    )


def front_kernel(
    rows,
    spread,
    lengths,
    gain,
    m_qkv,
    m_out,
    m_gu,
    m_down,
    t_qkv,
    b_qkv,
    t_out,
    b_out,
    t_gu,
    b_gu,
    t_down,
    b_down,
    cosines,
    sines,
    x_hbm,
    wqkv_hbm,
    wout_hbm,
    wgu_hbm,
    wdown_hbm,
    q_ref,
    kept_ref,
    mixed_ref,
    lse_ref,
    n2_qkv,
    n2_gu,
    n2_model,
    s_qkv,
    s_gu,
    s_out,
    s_down,
    at_out,
    av_out,
    av_down,
    xn1_hbm,
    vqkv_hbm,
    vout_hbm,
    vgu_hbm,
    vdown_hbm,
    kv_hbm,
    x_ref,
    wqkv,
    wout,
    wgu,
    wdown,
    xn1,
    vqkv,
    vfull,
    vgu,
    vdown,
    kv,
    acc,
    top,
    weight,
    squares,
    land_squares,
    at_mine,
    load_sems,
    store_sems,
    gather_s,
    gather_r,
    share_s,
    share_r,
    kv_s,
    kv_r,
    square_s,
    square_r,
    at_s,
    at_r,
):
    tokens, width = x_ref.shape
    span = tokens // rows
    cols = q_ref.shape[1]
    heads = cols // HD
    hidden = wdown.shape[0]
    hpad = vdown.shape[0]
    p = Place()
    core = lax.rem(p.seq, 2)
    upper = p.seq // 2
    sibling = upper * 2 + 1 - core
    loads = []
    pairs = [(wout_hbm, wout), (wqkv_hbm, wqkv), (x_hbm, x_ref), (wdown_hbm, wdown), (wgu_hbm, wgu)]
    for i, (src, dst) in enumerate(pairs):
        loads.append(pltpu.make_async_copy(src, dst, load_sems.at[i]))
        loads[-1].start()
    barrier = pltpu.get_barrier_semaphore()
    for step in range(1, PARTS):
        place = p.at(lax.rem(p.me + step, PARTS))
        pl.semaphore_signal(barrier, inc=1, device_id=place, device_id_type=MESH)
    for seq in (sibling, (1 - upper) * 2 + core):
        pl.semaphore_signal(barrier, inc=1, device_id=(p.row, seq, p.me), device_id_type=MESH)

    left, right = three_terms(t_out[...], b_out[...])
    my_cols = rows_of(p.me, cols)
    loads[0].wait()
    squares[...] = jnp.zeros_like(squares)
    for n in range(0, width, 512):
        at = slice(n, n + 512)
        v = wout[:, at].astype(F32) + SCALE * tn(left, right[:, at])
        vfull[my_cols, at] = v.astype(BF16)
        squares[0:1, at] = jnp.sum(v * v, axis=0, keepdims=True)
    at_mine[...] = t_out[...].astype(BF16)
    at_out[:, my_cols] = t_out[...].astype(BF16)
    pl.semaphore_wait(barrier, PARTS + 1)
    gather = Gather(p, vfull, cols // 2, (gather_s, gather_r), RING_MOST, cols, core)
    gather.start()
    at_copies = []
    for step in range(1, PARTS):
        to = lax.rem(p.me + step, PARTS)
        at_copies.append(p.send(at_mine, at_out.at[:, my_cols], (at_s, at_r), step - 1, to))

    loads[1].wait()

    def direct(k):
        left, right = three_terms(t_qkv[k], b_qkv[k])
        at = slice(k * cols, (k + 1) * cols)
        total = jnp.zeros((1, cols), F32)
        for n in range(0, width, 512):
            part = slice(n, n + 512)
            v = wqkv[k, part, :].astype(F32) + SCALE * tn(left[:, part], right)
            vqkv[part, at] = v.astype(BF16)
            total += jnp.sum(v * v, axis=0, keepdims=True)
        n2_qkv[:, at] = total
        s_qkv[:, at] = m_qkv[k : k + 1, :] * lax.rsqrt(total)

    def project(r, k):
        part = slice(r * span, (r + 1) * span)
        at = slice(k * cols, (k + 1) * cols)
        y = nn(xn1[part, :], vqkv[:, at]) * s_qkv[:, at]
        kept_ref[part, at] = y.astype(BF16)
        if k < 2:
            y = jnp.concatenate(
                [turn(y[:, h * HD : (h + 1) * HD], cosines[...], sines[...]) for h in range(heads)],
                axis=1,
            )
        if k == 0:
            q_ref[part, :] = y.astype(BF16)
        else:
            kv[p.seq, part, (k - 1) * cols : k * cols] = y.astype(BF16)

    def over(source, index, seq):
        return pltpu.make_async_remote_copy(
            src_ref=source,
            dst_ref=source,
            send_sem=kv_s.at[index],
            recv_sem=kv_r.at[index],
            device_id=(p.row, seq, p.me),
            device_id_type=MESH,
        )

    direct(1)
    direct(2)
    loads[2].wait()
    to_sib, to_far, onward = [], [], []
    for r in range(rows):
        part = slice(r * span, (r + 1) * span)
        to_sib.append(over(kv.at[p.seq, part], r, sibling))
        to_far.append(over(kv.at[p.seq, part], rows + r, 2 + core))
        onward.append(over(kv.at[core, part], 2 * rows + r, sibling))

        @pl.loop(0, span // 128)
        def _(i, r=r):
            piece = pl.ds(pl.multiple_of(r * span + i * 128, 128), 128)
            x = x_ref[piece, :].astype(F32)
            inv = lax.rsqrt(jnp.mean(x * x, axis=-1, keepdims=True) + EPS)
            xn1[piece, :] = (x * inv * gain[...]).astype(BF16)

        project(r, 1)
        project(r, 2)

        @pl.when(upper == 0)
        def _(r=r):
            to_far[r].start()

        @pl.when(core == 0)
        def _(r=r):
            to_sib[r].start()

    direct(0)
    for r in range(rows):
        project(r, 0)
    stores = [
        pltpu.make_async_copy(vqkv, vqkv_hbm, store_sems.at[1]),
        pltpu.make_async_copy(xn1, xn1_hbm, store_sems.at[2]),
    ]
    for copy in stores:
        copy.start()

    query_pos = p.seq * span + lax.broadcasted_iota(jnp.int32, (span, span), 0)
    key_pos = lax.broadcasted_iota(jnp.int32, (span, span), 1)

    def absorb(r, j, fresh=False):
        part = slice(r * span, (r + 1) * span)
        for head in range(heads):
            at = slice(head * HD, (head + 1) * HD)
            to = slice(cols + head * HD, cols + (head + 1) * HD)
            one = (slice(None), slice(r * heads + head, r * heads + head + 1))
            scores = scores_of(
                q_ref[part, at], kv[j, part, at], query_pos, key_pos, j * span, lengths[r]
            )
            best = jnp.max(scores, axis=-1, keepdims=True)
            if not fresh:
                best = jnp.maximum(best, top[one])
            expo = jnp.exp(scores - best)
            summed = jnp.sum(expo, axis=-1, keepdims=True)
            mixed = nn(expo.astype(BF16), kv[j, part, to])
            if not fresh:
                fade = jnp.exp(top[one] - best)
                summed += weight[one] * fade
                mixed += acc[part, at] * fade
            top[one] = best
            weight[one] = summed
            acc[part, at] = mixed

    gather.first()
    for r in range(rows):
        absorb(r, p.seq, True)
    gather.middle()

    loads[3].wait()
    vdown[hidden:, :] = jnp.zeros((hpad - hidden, width), BF16)
    left, right = three_terms(t_down[...], b_down[...])
    for n in range(0, width, 512):
        at = slice(n, n + 512)
        v = wdown[:, at].astype(F32) + SCALE * tn(left, right[:, at])
        vdown[:hidden, at] = v.astype(BF16)
        squares[1:2, at] = jnp.sum(v * v, axis=0, keepdims=True)
    square_copies = []
    for step in range(1, PARTS):
        to = lax.rem(p.me + step, PARTS)
        square_copies.append(
            p.send(squares, land_squares.at[step - 1], (square_s, square_r), step - 1, to)
        )
    stores.append(pltpu.make_async_copy(vdown, vdown_hbm, store_sems.at[3]))
    stores[-1].start()
    shares = []

    def share(plane, steps):
        for step in steps:
            view = gather.view(plane * RING + p.side(step))
            index = len(shares)
            shares.append(
                pltpu.make_async_remote_copy(
                    src_ref=view,
                    dst_ref=view,
                    send_sem=share_s.at[index],
                    recv_sem=share_r.at[index],
                    device_id=(p.row, sibling, p.me),
                    device_id_type=MESH,
                )
            )

            shares[-1].start()

    share(p.z, (1, 2, 3))

    loads[4].wait()
    ones = jnp.ones((8, width), BF16)
    for k in range(2):
        left, right = three_terms(b_gu[k], t_gu[k])
        base = k * hpad
        vgu[base + hidden : base + hpad, :] = jnp.zeros((hpad - hidden, width), BF16)
        n2_gu[:, base + hidden : base + hpad] = jnp.ones((1, hpad - hidden), F32)
        for n in range(0, hidden, 128):
            size = min(128, hidden - n)
            v = wgu[k, n : n + size, :].astype(F32) + SCALE * tn(left[:, n : n + size], right)
            vgu[base + n : base + n + size, :] = v.astype(BF16)
            n2_gu[:, base + n : base + n + size] = nt(ones, (v * v).astype(BF16))[:1]
        units = slice(base, base + hidden)
        s_gu[:, base : base + hpad] = jnp.zeros((1, hpad), F32)
        s_gu[:, units] = m_gu[k : k + 1, :] * lax.rsqrt(n2_gu[:, units])
    stores.append(pltpu.make_async_copy(vgu, vgu_hbm, store_sems.at[4]))
    stores[-1].start()
    gather.late()

    @pl.when(core == 1)
    def _():
        for r in range(rows):
            to_sib[r].wait_recv()
            absorb(r, p.seq - 1)

    for copy in shares:
        copy.wait_recv()
    half = rows_of(p.z, RING * cols)
    stores.append(pltpu.make_async_copy(vfull.at[half], vout_hbm.at[half], store_sems.at[0]))
    stores[-1].start()

    def from_far(r):
        @pl.when(upper == 1)
        def _():
            to_far[r].wait_recv()
            onward[r].start()
            absorb(r, core)
            onward[r].wait_recv()
            absorb(r, 1 - core)

    from_far(0)
    gather.end()
    share(p.far, (0, 1, 2, 3))
    for r in range(1, rows):
        from_far(r)

    @pl.loop(p.seq + 1, kv.shape[0])
    def _(j):
        kv[j] = jnp.zeros(kv.shape[1:], BF16)

    stores.append(pltpu.make_async_copy(kv, kv_hbm, store_sems.at[5]))
    stores[-1].start()
    for r in range(rows):
        part = slice(r * span, (r + 1) * span)
        for head in range(heads):
            at = slice(head * HD, (head + 1) * HD)
            one = (slice(None), slice(r * heads + head, r * heads + head + 1))
            mixed_ref[part, at] = (acc[part, at] / weight[one]).astype(BF16)
            lse_ref[part, at] = jnp.broadcast_to(top[one] + jnp.log(weight[one]), (span, HD))
    av_out[...] = nn(at_mine[...], vfull[my_cols, :]) / spread
    at_down = t_down[...].astype(BF16)
    av_down[...] = nn(at_down, vdown[:hidden, :]) / spread
    for copy in square_copies:
        copy.wait_recv()
    total = squares[...]
    for step in range(PARTS - 1):
        total += land_squares[step]
    n2_model[...] = total
    s_out[...] = m_out[...] * lax.rsqrt(total[0:1])
    s_down[...] = m_down[...] * lax.rsqrt(total[1:2])
    for copy in at_copies + shares[RING - 1 :]:
        copy.wait_recv()
    half = rows_of(p.far, RING * cols)
    stores.append(pltpu.make_async_copy(vfull.at[half], vout_hbm.at[half], store_sems.at[6]))
    stores[-1].start()
    for copy in at_copies + square_copies + shares:
        copy.wait_send()
    for copy in stores:
        copy.wait()

    @pl.when(upper == 0)
    def _():
        for r in range(rows):
            to_far[r].wait_send()

    @pl.when(core == 0)
    def _():
        for r in range(rows):
            to_sib[r].wait_send()

    @pl.when(upper == 1)
    def _():
        for r in range(rows):
            onward[r].wait_send()


def front(rows, seqs, spread, lengths, *rest):
    x, w_qkv, _, _, w_down = rest[-5:]
    tokens, width = x.shape
    cols = w_qkv.shape[2]
    heads = cols // HD
    hidden = w_down.shape[0]
    hpad = pad_to(hidden)
    span = tokens // rows
    shape = jax.ShapeDtypeStruct
    dma = pltpu.SemaphoreType.DMA
    vmem = pltpu.VMEM
    out_shape = (
        shape((tokens, cols), BF16),
        shape((tokens, 3 * cols), BF16),
        shape((tokens, cols), BF16),
        shape((tokens, cols), F32),
        shape((1, 3 * cols), F32),
        shape((1, 2 * hpad), F32),
        shape((8, width), F32),
        shape((1, 3 * cols), F32),
        shape((1, 2 * hpad), F32),
        shape((1, width), F32),
        shape((1, width), F32),
        shape((RANK, width), BF16),
        shape((RANK, width), F32),
        shape((RANK, width), F32),
        shape((tokens, width), BF16),
        shape((width, 3 * cols), BF16),
        shape((PARTS * cols, width), BF16),
        shape((2 * hpad, width), BF16),
        shape((hpad, width), BF16),
        shape((seqs, tokens, 2 * cols), BF16),
    )
    scratch = [
        vmem((tokens, width), BF16),
        vmem((3, width, cols), BF16),
        vmem((cols, width), BF16),
        vmem((2, hidden, width), BF16),
        vmem((hidden, width), BF16),
        vmem((tokens, width), BF16),
        vmem((width, 3 * cols), BF16),
        vmem((PARTS * cols, width), BF16),
        vmem((2 * hpad, width), BF16),
        vmem((hpad, width), BF16),
        vmem((seqs, tokens, 2 * cols), BF16),
        vmem((tokens, cols), F32),
        vmem((span, rows * heads), F32),
        vmem((span, rows * heads), F32),
        vmem((8, width), F32),
        vmem((PARTS - 1, 8, width), F32),
        vmem((RANK, cols), BF16),
        dma((5,)),
        dma((7,)),
        dma((GATHER_SEMS,)),
        dma((GATHER_SEMS,)),
        dma((PARTS,)),
        dma((PARTS,)),
        dma((3 * rows,)),
        dma((3 * rows,)),
    ] + [dma((PARTS - 1,))] * 4
    anywhere = pl.BlockSpec(memory_space=pl.ANY)
    return pl.pallas_call(
        functools.partial(front_kernel, rows, spread),
        out_shape=out_shape,
        in_specs=[pl.BlockSpec(memory_space=pltpu.SMEM)] + [VMEM] * 15 + [anywhere] * 5,
        out_specs=[VMEM] * 14 + [anywhere] * 6,
        scratch_shapes=scratch,
        compiler_params=pltpu.CompilerParams(
            collective_id=4, has_side_effects=True, vmem_limit_bytes=ROOM
        ),
    )(lengths, *rest)


def finish_kernel(
    hidden,
    summed,
    summed_qkv,
    m_qkv,
    m_out,
    m_gu,
    m_down,
    n2_model,
    b_out,
    b_down,
    vdown_hbm,
    vout_hbm,
    out_hbm,
    gx_hbm,
    output,
    grad_x,
    gm_qkv,
    ga_qkv,
    gb_qkv,
    gm_out,
    ga_out,
    gb_out,
    gm_gu,
    ga_gu,
    gb_gu,
    gm_down,
    ga_down,
    gb_down,
    vout,
    vdown,
    held,
    sems,
):
    cols, width = vout.shape
    hpad = vdown.shape[0]
    load = pltpu.make_async_copy(vout_hbm.at[rows_of(lax.axis_index("head"), cols)], vout, sems.at[0])
    load.start()
    load_down = pltpu.make_async_copy(vdown_hbm, vdown, sems.at[33])
    load_down.start()
    moves = []
    tokens = output.shape[0]
    for i in range(8):
        part = pl.ds(i * tokens // 8, tokens // 8)
        for k, src in enumerate((out_hbm, gx_hbm)):
            moves.append(pltpu.make_async_copy(src.at[part], held.at[k, part], sems.at[1 + 2 * i + k]))
            moves[-1].start()
    for i in range(8):
        part = pl.ds(i * tokens // 8, tokens // 8)
        for k, dst in enumerate((output, grad_x)):
            moves[2 * i + k].wait()
            moves.append(pltpu.make_async_copy(held.at[k, part], dst.at[part], sems.at[17 + 2 * i + k]))
            moves[-1].start()

    def block(first):
        return summed[first * RANK : (first + 1) * RANK, :]

    own_qkv = slice(COMMON_QKV, COMMON_QKV + RANK)
    for k in range(3):
        at = slice(k * cols, (k + 1) * cols)
        ga_qkv[k] = SCALE * summed_qkv[k * RANK : (k + 1) * RANK, :]
        gb_qkv[k] = SCALE * summed_qkv[own_qkv, at]
        e_one = summed_qkv[COMMON_QKV : COMMON_QKV + 1, (3 + k) * cols : (4 + k) * cols]
        gm_qkv[k : k + 1, :] = e_one / m_qkv[k : k + 1, :]
    for k in range(2):
        ga_gu[k] = SCALE * block(k)
    e_out = summed[7 * RANK : 7 * RANK + 1, :]
    e_down = summed[7 * RANK + 1 : 7 * RANK + 2, :]
    ratio_out = e_out / n2_model[0:1, :]
    ratio_down = e_down / n2_model[1:2, :]
    gm_out[...] = e_out / m_out[...]
    gm_down[...] = e_down / m_down[...]
    gb_out[...] = SCALE * (block(2) - block(5) * ratio_out)
    gb_down[...] = SCALE * (block(3) - block(6) * ratio_down)
    own_rows = slice(COMMON_FEED, COMMON_FEED + RANK)
    fold_rows = slice(COMMON_FEED + RANK, COMMON_FEED + OWN_FEED)
    fits = width - 2 * hpad
    gb = summed[own_rows, : 2 * hpad]
    e_gu = summed[COMMON_FEED + RANK : COMMON_FEED + RANK + 1, fits:]
    for k in range(2):
        at = slice(k * hpad, k * hpad + hidden)
        gb_gu[k] = SCALE * gb[:, at]
        gm_gu[k : k + 1, :] = e_gu[:, at] / m_gu[k : k + 1, :]
    back_down = (b_down[...] * ratio_down).astype(BF16)
    load_down.wait()
    down = jnp.concatenate([summed[own_rows, 2 * hpad :], summed[fold_rows, : hpad - fits]], axis=1)
    down = down - nt(back_down, vdown[...])
    ga_down[...] = SCALE * down[:, :hidden]
    load.wait()
    back_out = (b_out[...] * ratio_out).astype(BF16)
    at = rows_of(lax.axis_index("head"), cols)
    ga_out[...] = SCALE * (summed[4 * RANK : 5 * RANK, at] - nt(back_out, vout[...]))
    for move in moves[16:]:
        move.wait()


def finish(hidden, cols, summed, *rest):
    width = summed.shape[1]
    tokens = rest[-1].shape[0]
    shape = jax.ShapeDtypeStruct
    out_shape = (
        shape((tokens, width), BF16),
        shape((tokens, width), BF16),
        shape((3, cols), F32),
        shape((3, RANK, width), F32),
        shape((3, RANK, cols), F32),
        shape((1, width), F32),
        shape((RANK, cols), F32),
        shape((RANK, width), F32),
        shape((2, hidden), F32),
        shape((2, RANK, width), F32),
        shape((2, RANK, hidden), F32),
        shape((1, width), F32),
        shape((RANK, hidden), F32),
        shape((RANK, width), F32),
    )
    anywhere = pl.BlockSpec(memory_space=pl.ANY)
    return pl.pallas_call(
        functools.partial(finish_kernel, hidden),
        out_shape=out_shape,
        in_specs=[VMEM] * 9 + [anywhere] * 4,
        out_specs=[anywhere] * 2 + [VMEM] * 12,
        scratch_shapes=[
            pltpu.VMEM((cols, width), BF16),
            pltpu.VMEM(rest[-4].shape, BF16),
            pltpu.VMEM((2, tokens, width), BF16),
            pltpu.SemaphoreType.DMA((34,)),
        ],
        compiler_params=pltpu.CompilerParams(vmem_limit_bytes=ROOM),
    )(summed, *rest)


def shards(
    layer_input,
    cotangent,
    lengths,
    gain_attn,
    gain_ffn,
    w_qkv,
    m_qkv,
    a_qkv,
    b_qkv,
    w_out,
    m_out,
    a_out,
    b_out,
    w_gu,
    m_gu,
    a_gu,
    b_gu,
    w_down,
    m_down,
    a_down,
    b_down,
):
    rows, span, width = layer_input.shape
    seqs = lax.axis_size("seq")
    tokens = rows * span
    cols = w_qkv.shape[2]
    hidden = w_gu.shape[2]
    hpad = pad_to(hidden)

    positions = lax.axis_index("seq") * span + jnp.arange(span, dtype=jnp.int32)
    freqs = ROPE_BASE ** (-jnp.arange(HD // 2, dtype=F32) * 2.0 / HD)
    turned = positions.astype(F32)[:, None] * freqs[None, :]
    cosines = jnp.concatenate([jnp.cos(turned)] * 2, axis=1)
    sines = jnp.concatenate([-jnp.sin(turned), jnp.sin(turned)], axis=1)
    x = layer_input.reshape(tokens, width)
    t_qkv, t_gu = a_qkv.transpose(0, 2, 1), a_gu.transpose(0, 2, 1)
    t_out, t_down = a_out.T, a_down.T
    (
        query,
        kept,
        mixed,
        lse,
        n2_qkv,
        n2_gu,
        n2_model,
        s_qkv,
        s_gu,
        s_out,
        s_down,
        full_t_out,
        av_out,
        av_down,
        normed1,
        vb_qkv,
        full_out,
        vb_gu,
        vb_down,
        pairs,
    ) = front(
        rows,
        seqs,
        float(lax.axis_size("row") * seqs),
        lengths,
        gain_attn[None],
        m_qkv,
        m_out[None],
        m_gu,
        m_down[None],
        t_qkv,
        b_qkv,
        t_out,
        b_out,
        t_gu,
        b_gu,
        t_down,
        b_down,
        cosines,
        sines,
        x,
        w_qkv,
        w_out,
        w_gu.transpose(0, 2, 1),
        w_down,
    )
    cot = cotangent.reshape(tokens, width)
    (
        hidden1,
        grad_h1,
        grad_mixed,
        pack,
        ffn_part,
    ) = feed(
        span,
        lengths,
        mixed,
        s_out,
        gain_ffn[None],
        s_gu,
        s_down,
        n2_gu,
        b_gu,
        t_gu.reshape(2 * RANK, width),
        t_down,
        b_down,
        b_out,
        full_t_out,
        av_out,
        av_down,
        x,
        cot,
        full_out,
        vb_gu,
        vb_down,
    )
    dqkv, e_qkv, output, e_down = back(
        rows,
        lengths,
        cosines,
        sines,
        s_qkv,
        s_down,
        query,
        mixed,
        lse,
        grad_mixed,
        kept,
        hidden1,
        cot,
        pairs,
        ffn_part,
    )
    grad_x, summed, summed_qkv = close(
        cols,
        dqkv,
        vb_qkv,
        normed1,
        x,
        grad_h1,
        pack,
        gain_attn[None],
        b_qkv,
        t_qkv.reshape(3 * RANK, width),
        e_qkv,
        n2_qkv,
        e_down,
    )
    (
        output,
        grad_x,
        gm_qkv,
        ga_qkv,
        gb_qkv,
        gm_out,
        ga_out,
        gb_out,
        gm_gu,
        ga_gu,
        gb_gu,
        gm_down,
        ga_down,
        gb_down,
    ) = finish(
        hidden,
        cols,
        summed,
        summed_qkv,
        m_qkv,
        m_out[None],
        m_gu,
        m_down[None],
        n2_model,
        b_out,
        b_down,
        vb_down,
        full_out,
        output,
        grad_x,
    )
    return (
        output.reshape(rows, span, width),
        grad_x.reshape(rows, span, width),
        gm_qkv,
        ga_qkv.transpose(0, 2, 1),
        gb_qkv,
        gm_out[0],
        ga_out.T,
        gb_out,
        gm_gu,
        ga_gu.transpose(0, 2, 1),
        gb_gu,
        gm_down[0],
        ga_down.T,
        gb_down,
    )


def solution(mesh):
    placed = (
        P("row", "seq", None),
        P("row", "seq", None),
        P("row"),
        P(),
        P(),
        P(None, None, "head"),
        P(None, "head"),
        P(),
        P(None, None, "head"),
        P("head", None),
        P(),
        P("head", None),
        P(),
        P(None, None, "head"),
        P(None, "head"),
        P(),
        P(None, None, "head"),
        P("head", None),
        P(),
        P("head", None),
        P(),
    )
    return jax.shard_map(
        shards,
        mesh=mesh,
        in_specs=placed,
        out_specs=(
            P("row", "seq", None),
            P("row", "seq", None),
            P(None, "head"),
            P(),
            P(None, None, "head"),
            P(),
            P("head", None),
            P(),
            P(None, "head"),
            P(),
            P(None, None, "head"),
            P(),
            P("head", None),
            P(),
        ),
        check_vma=False,
    )
```

```python
import functools

import jax
import jax.numpy as jnp
import numpy as np
from jax import lax
from jax.experimental import pallas as pl
from jax.experimental.pallas import tpu as pltpu
from jax.sharding import PartitionSpec as P

HD = 128
RANK = 16
SCALE = 2.0
EPS = 1e-05
ROPE_BASE = 10000.0
MASKED = -1000000000.0
F32 = jnp.float32
BF16 = jnp.bfloat16


def pad_to(n, m=256):
    return -(-n // m) * m


def mm(a, b, dims):
    return lax.dot_general(a, b, (dims, ((), ())), preferred_element_type=F32)


def nn(a, b):
    return mm(a, b, ((1,), (0,)))


def nt(a, b):
    return mm(a, b, ((1,), (1,)))


def tn(a, b):
    return mm(a, b, ((0,), (0,)))


MESH = pl.DeviceIdType.MESH
VMEM = pl.BlockSpec(memory_space=pltpu.VMEM)
ROOM = 60 * 2**20
RING = 4
PARTS = 8


class Place:
    def __init__(self):
        self.row, self.seq, self.me = (lax.axis_index(n) for n in ("row", "seq", "head"))
        self.y = lax.rem(self.me, RING)
        self.z = self.me // RING
        self.far = 1 - self.z
        self.cross = self.far * RING + self.y

    def side(self, step):
        return lax.rem(self.y + step + RING, RING)

    def at(self, head):
        return (self.row, self.seq, head)

    def greet(self):
        barrier = pltpu.get_barrier_semaphore()
        for step in range(1, PARTS):
            pl.semaphore_signal(
                barrier, inc=1, device_id=self.at(lax.rem(self.me + step, PARTS)), device_id_type=MESH
            )
        pl.semaphore_wait(barrier, PARTS - 1)

    def send(self, source, target, sems, index, head):
        copy = pltpu.make_async_remote_copy(
            src_ref=source,
            dst_ref=target,
            send_sem=sems[0].at[index],
            recv_sem=sems[1].at[index],
            device_id=self.at(head),
            device_id_type=MESH,
        )
        copy.start()
        return copy


def rows_of(index, count):
    return pl.ds(pl.multiple_of(index * count, count), count)


EVEN = {"a": (0, 640, 1152), "b": (1152, 1536, 2048)}
RING_FIRST = {"a": (0, 768, 1536), "b": (1536, 1792, 2048)}
RING_MOST = {"a": (0, 896, 1792), "b": (1792, 1920, 2048)}
UP, DOWN = 1, -1


def span_of(spans, which, half=None):
    first, split, last = spans[which]
    if half == UP:
        last = split
    if half == DOWN:
        first = split
    return first, last


class Gather:
    def __init__(self, place, buf, chunk, sems, spans, stride=None, offset=0):
        self.place, self.buf, self.chunk, self.sems, self.spans = place, buf, chunk, sems, spans
        self.stride, self.offset = stride or chunk, offset
        self.sent = []

    def view(self, head, which=None, half=None):
        first = head * self.stride + self.offset * self.chunk
        rows = pl.ds(pl.multiple_of(first, self.chunk), self.chunk)
        if which is None:
            return self.buf.at[rows]
        first, last = span_of(self.spans, which, half)
        return self.buf.at[rows, first:last]

    def pass_on(self, head, which, half, index, to):
        view = self.view(head, which, half)
        copy = self.place.send(view, view, self.sems, index, to)
        self.sent.append(copy)
        return copy

    def ring(self, head, which, index):
        p = self.place
        return {
            way: self.pass_on(head, which, None, index + i, p.z * RING + p.side(way))
            for i, way in enumerate((UP, DOWN))
        }

    def relay(self, copies, plane, which, index, then=None):
        p = self.place
        made = []
        for i, way in enumerate((UP, DOWN)):
            copies[way].wait_recv()
            head = plane * RING + p.side(-way)
            made.append(self.pass_on(head, which, way, index + i, p.z * RING + p.side(way)))
            if then is not None:
                then(head, i)
        return made

    def start(self):
        p = self.place
        self.rest = []
        self.a_cross = self.pass_on(p.me, "a", None, 0, p.cross)
        self.b_ring = self.ring(p.me, "b", 6)
        self.a_ring = self.ring(p.me, "a", 8)
        self.rest.append(self.pass_on(p.me, "b", None, 1, p.cross))

    def first(self):
        p = self.place

        def across(head, i):
            self.rest.append(self.pass_on(head, "b", None, 2 + i, p.cross))

        self.b_relay = self.relay(self.b_ring, p.z, "b", 10, across)
        self.a_cross.wait_recv()
        self.far_ring = self.ring(p.cross, "a", 14)
        self.a_relay = self.relay(self.a_ring, p.z, "a", 12)

    def middle(self):
        p = self.place
        opposite = p.z * RING + p.side(2)
        for i, way in enumerate((UP, DOWN)):
            self.b_relay[i].wait_recv()
            self.rest.append(self.pass_on(opposite, "b", way, 4 + i, p.cross))
        for copy in self.a_relay:
            copy.wait_recv()

    def late(self):
        self.rest += self.relay(self.far_ring, self.place.far, "a", 16)

    def end(self):
        for copy in self.rest:
            copy.wait_recv()
        for copy in self.sent:
            copy.wait_send()


GATHER_SEMS = 18


class Scatter:
    def __init__(self, place, src, out, chunk, spans, scratch):
        self.place, self.src, self.out, self.chunk = place, src, out, chunk
        self.spans = spans
        self.cut = spans["a"][2]
        (
            self.far_b,
            self.hold_b,
            self.relay_b,
            self.land_b,
            self.hold_a,
            self.relay_a,
            self.land_a,
            self.hold_far,
            self.land_far,
            s,
            r,
        ) = scratch
        self.sems = (s, r)
        self.sent = []
        self.a_relay = [None, None]
        self.a_other = [[], []]

    @staticmethod
    def scratch(chunk, width, spans):
        a = spans["a"][2]
        b = width - a
        return [
            pltpu.VMEM((RING, chunk, b), BF16),
            pltpu.VMEM((3, chunk, b), BF16),
            pltpu.VMEM((chunk, b), BF16),
            pltpu.VMEM((2, chunk, b), BF16),
            pltpu.VMEM((2, 2, chunk, a), BF16),
            pltpu.VMEM((2, chunk, a), BF16),
            pltpu.VMEM((2, 2, chunk, a), BF16),
            pltpu.VMEM((chunk, a), BF16),
            pltpu.VMEM((chunk, a), BF16),
            pltpu.SemaphoreType.DMA((21,)),
            pltpu.SemaphoreType.DMA((21,)),
        ]

    def send(self, source, target, index, head):
        copy = self.place.send(source, target, self.sems, index, head)
        self.sent.append(copy)
        return copy

    def mine(self, plane, y, which):
        first, last = span_of(self.spans, which)
        return self.src[rows_of(plane * RING + y, self.chunk), first:last].astype(F32)

    def within(self, which, half):
        base = self.spans[which][0]
        first, last = span_of(self.spans, which, half)
        return slice(first - base, last - base)

    def opposite(self, source, target, which, index):
        p = self.place
        made = {}
        for i, half in enumerate((UP, DOWN)):
            part = self.within(which, half)
            made[half] = self.send(
                source(half, part), target.at[:, part], index + i, p.z * RING + p.side(-half)
            )
        return made

    def start_b(self):
        p = self.place
        self.across = []
        for i, step in enumerate((2, DOWN, UP, 0)):
            view = self.src.at[rows_of(p.far * RING + p.side(step), self.chunk), self.cut :]
            self.across.append(self.send(view, self.far_b.at[i], i, p.cross))

    def start_a(self, k):
        p = self.place
        plane = p.z if k else p.far
        rows = rows_of(plane * RING + p.side(2), self.chunk)

        def source(half, part):
            return self.src.at[rows, part]

        self.a_relay[k] = self.opposite(source, self.relay_a.at[k], "a", 5 + 2 * k)

    def start_other(self, k):
        p = self.place
        plane = p.z if k else p.far
        for i, way in enumerate((DOWN, UP)):
            part = self.within("a", way)
            to = p.side(way)
            self.a_other[k].append(
                self.send(
                    self.src.at[rows_of(plane * RING + to, self.chunk), part],
                    self.land_a.at[k, i, :, part],
                    17 + 2 * k + i,
                    p.z * RING + to,
                )
            )

    def first(self):
        p = self.place
        self.a_direct = []
        for k, plane in enumerate((p.far, p.z)):
            made = {}
            for i, way in enumerate((DOWN, UP)):
                half = -way
                part = self.within("a", half)
                self.a_relay[k][half].wait_recv()
                rows = rows_of(plane * RING + p.side(way), self.chunk)
                self.hold_a[k, i, :, part] = (
                    self.src[rows, part].astype(F32) + self.relay_a[k, :, part].astype(F32)
                ).astype(BF16)
                made[way] = self.send(
                    self.hold_a.at[k, i, :, part],
                    self.land_a.at[k, i, :, part],
                    9 + 2 * k + i,
                    p.z * RING + p.side(way),
                )
            self.a_direct.append(made)
        self.across[0].wait_recv()
        total = self.mine(p.z, p.side(2), "b") + self.far_b[0].astype(F32)
        self.hold_b[2] = total.astype(BF16)

        def source(half, part):
            return self.hold_b.at[2, :, part]

        self.b_relay = self.opposite(source, self.relay_b, "b", 13)

    def middle(self):
        p = self.place
        total = self.mine(p.far, p.y, "a")
        for i, way in enumerate((DOWN, UP)):
            self.a_direct[0][way].wait_recv()
            self.a_other[0][i].wait_recv()
            total += self.land_a[0, i].astype(F32)
        self.hold_far[...] = total.astype(BF16)
        self.last = self.send(self.hold_far, self.land_far, 4, p.cross)

    def late(self):
        p = self.place
        self.b_direct = []
        for i, way in enumerate((DOWN, UP)):
            half = -way
            part = self.within("b", half)
            self.across[1 + i].wait_recv()
            total = self.mine(p.z, p.side(way), "b") + self.far_b[1 + i].astype(F32)
            self.b_relay[half].wait_recv()
            self.hold_b[i] = total.astype(BF16)
            self.hold_b[i, :, part] = (
                total[:, part] + self.relay_b[:, part].astype(F32)
            ).astype(BF16)
            self.b_direct.append(
                self.send(
                    self.hold_b.at[i], self.land_b.at[i], 15 + i, p.z * RING + p.side(way)
                )
            )

    def end(self):
        p = self.place
        total = self.mine(p.z, p.y, "a")
        for i, way in enumerate((DOWN, UP)):
            self.a_direct[1][way].wait_recv()
            self.a_other[1][i].wait_recv()
            total += self.land_a[1, i].astype(F32)
        self.across[3].wait_recv()
        rest = self.mine(p.z, p.y, "b") + self.far_b[3].astype(F32)
        for i in range(2):
            self.b_direct[i].wait_recv()
            rest += self.land_b[i].astype(F32)
        self.out[:, self.cut :] = rest
        self.last.wait_recv()
        self.out[:, : self.cut] = total + self.land_far[...].astype(F32)
        for copy in self.sent:
            copy.wait_send()


def feed_kernel(
    span,
    lengths,
    mixed_ref,
    s_out,
    gain,
    s_gu,
    s_down,
    n2_gu,
    b_gu_raw,
    t_gu,
    t_down,
    b_down,
    b_out,
    at_out,
    av_out,
    av_down,
    x_hbm,
    cot_hbm,
    vout_hbm,
    vgu_hbm,
    vdown_hbm,
    h1_ref,
    dh1_ref,
    dmix_ref,
    pack,
    ffn_hbm,
    ffn_ref,
    vout,
    vgu,
    vdown,
    dys,
    xn2,
    part,
    dhid,
    hid,
    dgu,
    x_own,
    mixed_own,
    dmix_own,
    attn,
    sum_own,
    b_gu,
    at_down,
    local_sems,
    swap_s,
    swap_r,
    back_s,
    back_r,
    gather_s,
    gather_r,
    *scatter_scratch,
):
    tokens, width = xn2.shape
    chunk = tokens // PARTS
    block = tokens // 2
    cols = mixed_ref.shape[1]
    hpad = hid.shape[1]
    tile = 256
    p = Place()
    own = rows_of(p.me, chunk)
    loads = []
    for i, (src, dst) in enumerate(
        [
            (x_hbm.at[own], x_own),
            (vout_hbm, vout),
            (cot_hbm, dys),
            (vdown_hbm, vdown),
            (vgu_hbm, vgu),
        ]
    ):
        loads.append(pltpu.make_async_copy(src, dst, local_sems.at[i]))
        loads[-1].start()
    p.greet()

    my_cols = rows_of(p.me, cols)
    swaps = []
    for step in range(1, PARTS):
        to = lax.rem(p.me + step, PARTS)
        swaps.append(
            p.send(
                mixed_ref.at[rows_of(to, chunk)],
                mixed_own.at[:, my_cols],
                (swap_s, swap_r),
                step - 1,
                to,
            )
        )
    mixed_own[:, my_cols] = mixed_ref[own, :]

    hidden = t_down.shape[1]
    b_gu[...] = jnp.zeros_like(b_gu)
    at_down[...] = jnp.zeros_like(at_down)
    for k in range(2):
        b_gu[:, k * hpad : k * hpad + hidden] = b_gu_raw[k].astype(BF16)
    at_down[:, :hidden] = t_down[...].astype(BF16)
    def back_hidden(half):
        rows = slice(half * block, (half + 1) * block)

        @pl.loop(0, hpad // tile)
        def _(n):
            units = rows_of(n, tile)
            dhid[rows, units] = nt(dys[rows, :], vdown[units, :]).astype(BF16)


    for copy in swaps:
        copy.wait_recv()
    loads[0].wait()
    loads[1].wait()

    @pl.loop(0, width // 512)
    def _(n):
        part_cols = rows_of(n, 512)
        attn[:, part_cols] = nn(mixed_own[...], vout[:, part_cols]) * s_out[:, part_cols]

    h1_ref[...] = x_own[...].astype(F32) + attn[...]
    inv2 = lax.rsqrt(jnp.mean(h1_ref[...] * h1_ref[...], axis=-1, keepdims=True) + EPS)
    xn2[own, :] = (h1_ref[...] * inv2 * gain[...]).astype(BF16)
    gather = Gather(p, xn2, chunk, (gather_s, gather_r), EVEN)
    gather.start()
    own_rows = slice(COMMON_FEED, COMMON_FEED + RANK)
    fold_rows = slice(COMMON_FEED + RANK, COMMON_FEED + OWN_FEED)
    e_row = slice(COMMON_FEED + RANK, COMMON_FEED + RANK + 1)
    e_first = width - 2 * hpad
    pack[...] = jnp.zeros_like(pack)
    at = 5 * RANK
    for piece in (av_out, av_down):
        pack[at : at + RANK, :] = piece[...]
        at += RANK
    loads[2].wait()
    loads[3].wait()
    seq = lax.axis_index("seq")

    @pl.loop(0, PARTS)
    def _(i):
        rows = rows_of(i, chunk)
        base = lax.rem(i * chunk, span)
        length = lengths[0]
        for r in range(1, tokens // span):
            length = jnp.where(i * chunk >= r * span, lengths[r], length)
        pos = seq * span + base + lax.broadcasted_iota(jnp.int32, (chunk, 1), 0)
        live = (pos < length).astype(F32)
        dys[rows, :] = (dys[rows, :].astype(F32) * live * s_down[...]).astype(BF16)

    back_hidden(0)
    back_hidden(1)
    loads[4].wait()

    def hidden_units(plane):
        rows = rows_of(plane, block)

        @pl.loop(0, hpad // tile)
        def _(n):
            at_gate = rows_of(n, tile)
            at_up = rows_of(n + hpad // tile, tile)
            of_gate = rows_of(n + e_first // tile, tile)
            of_up = rows_of(n + (e_first + hpad) // tile, tile)
            gate = nt(xn2[rows, :], vgu[at_gate, :]) * s_gu[:, at_gate]
            up = nt(xn2[rows, :], vgu[at_up, :]) * s_gu[:, at_up]
            sigma = jax.nn.sigmoid(gate)
            active = gate * sigma
            hid[rows, at_gate] = (active * up).astype(BF16)
            back = dhid[rows, at_gate].astype(F32)
            grad_gate = back * up * sigma * (1.0 + gate * (1.0 - sigma))
            grad_up = back * active
            pack[e_row, of_gate] += jnp.sum(grad_gate * gate, axis=0, keepdims=True)
            pack[e_row, of_up] += jnp.sum(grad_up * up, axis=0, keepdims=True)
            dgu[rows, at_gate] = (grad_gate * s_gu[:, at_gate]).astype(BF16)
            dgu[rows, at_up] = (grad_up * s_gu[:, at_up]).astype(BF16)

    def back_part(plane, first, last):
        rows = rows_of(plane, block)

        @pl.loop(first // 512, last // 512)
        def _(n):
            part_cols = rows_of(n, 512)
            part[rows, part_cols] = nn(dgu[rows, :], vgu[:, part_cols]).astype(BF16)

    scatter = Scatter(p, part, sum_own, chunk, EVEN, scatter_scratch)
    gather.first()
    gather.middle()
    hidden_units(p.z)
    gather.late()
    back_part(p.z, 0, width)
    scatter.start_a(1)
    scatter.start_other(1)
    gather.end()
    hidden_units(p.far)
    back_part(p.far, 1024, width)
    scatter.start_b()
    back_part(p.far, 0, 1024)
    scatter.start_a(0)
    scatter.start_other(0)

    def forward_part(half):
        rows = slice(half * block, (half + 1) * block)

        @pl.loop(0, width // 512)
        def _(n):
            part_cols = rows_of(n, 512)
            ffn_ref[rows, part_cols] = nn(hid[rows, :], vdown[:, part_cols]).astype(BF16)

    t_one = []
    for k in range(2):
        part_cols = slice(k * hpad, (k + 1) * hpad)
        t_one.append(nt(b_gu[:, part_cols], dgu[:, part_cols]).astype(BF16))
    t_one = jnp.concatenate(t_one, axis=0)
    left_gu = t_gu[...].astype(BF16)
    x_gu = nt(left_gu, xn2[...]).astype(BF16)
    scatter.first()
    ratio = pack[e_row, e_first:] / n2_gu[...]
    back_gu = (b_gu[...].astype(F32) * ratio).astype(BF16)
    for n in range(0, width, 512):
        at = slice(n, n + 512)
        first = nn(t_one, xn2[:, at])
        for k in range(2):
            units = slice(k * hpad, (k + 1) * hpad)
            pack[k * RANK : (k + 1) * RANK, at] = first[k * RANK : (k + 1) * RANK] - nn(
                back_gu[:, units], vgu[units, at]
            )
    forward_part(0)
    forward_part(1)
    store = pltpu.make_async_copy(ffn_ref, ffn_hbm, local_sems.at[6])
    store.start()
    scatter.middle()
    scatter.late()
    for k in range(2):
        part_cols = slice(k * hpad, (k + 1) * hpad)
        both = slice(k * RANK, (k + 1) * RANK)
        pack[own_rows, part_cols] = (
            nn(x_gu[both], dgu[:, part_cols])
            - nt(left_gu[both], vgu[part_cols, :]) * ratio[:, part_cols]
        )
    back_down = nt(b_down[...].astype(BF16), dys[...]).astype(BF16)
    ga_down = nn(back_down, hid[...])
    fits = width - 2 * hpad
    pack[own_rows, 2 * hpad :] = ga_down[:, :fits]
    pack[fold_rows, : hpad - fits] = ga_down[:, fits:]
    x_down = nt(at_down[...], hid[...]).astype(BF16)
    for n in range(0, width, 512):
        pack[3 * RANK : 4 * RANK, n : n + 512] = nn(x_down, dys[:, n : n + 512])
    scatter.end()

    length = lengths[0]
    for r in range(1, tokens // span):
        length = jnp.where(p.me * chunk >= r * span, lengths[r], length)
    pos = seq * span + lax.rem(p.me * chunk, span) + lax.broadcasted_iota(jnp.int32, (chunk, 1), 0)
    live = (pos < length).astype(F32)
    dy_copy = pltpu.make_async_copy(cot_hbm.at[own], x_own, local_sems.at[5])
    dy_copy.start()
    scaled = sum_own[...] * gain[...]
    h1 = h1_ref[...]
    mean = jnp.mean(scaled * h1, axis=-1, keepdims=True)
    dy_copy.wait()
    grad = x_own[...].astype(F32) * live + inv2 * (scaled - h1 * (inv2 * inv2 * mean))
    dh1_ref[...] = grad
    low = grad.astype(BF16).astype(F32)
    pack[7 * RANK : 7 * RANK + 1, :] = jnp.sum(low * attn[...], axis=0, keepdims=True)
    das = (low * s_out[...]).astype(BF16)

    @pl.loop(0, width // 512)
    def _(n):
        part_cols = rows_of(n, 512)
        dmix_own[:, part_cols] = nt(das, vout[part_cols, :]).astype(BF16)

    backs = []
    for step in range(1, PARTS):
        to = lax.rem(p.me + step, PARTS)
        backs.append(
            p.send(
                dmix_own.at[:, rows_of(to, cols)],
                dmix_ref.at[own],
                (back_s, back_r),
                step - 1,
                to,
            )
        )
    dmix_ref[own, :] = dmix_own[:, my_cols]
    t_out = nt(b_out[...].astype(BF16), das).astype(BF16)
    pack[4 * RANK : 5 * RANK, :] = nn(t_out, mixed_own[...])
    x_out = nt(at_out[...], mixed_own[...]).astype(BF16)
    pack[2 * RANK : 3 * RANK, :] = nn(x_out, das)
    for copy in backs:
        copy.wait_recv()
    for copy in swaps + backs:
        copy.wait_send()
    store.wait()


def feed(span, lengths, mixed, *rest):
    tokens, cols = mixed.shape
    hpad, width = rest[-1].shape
    chunk = tokens // PARTS
    shape = jax.ShapeDtypeStruct
    out_shape = (
        shape((chunk, width), F32),
        shape((chunk, width), F32),
        shape((tokens, cols), BF16),
        shape((COMMON_FEED + OWN_FEED, width), F32),
        shape((tokens, width), BF16),
    )
    dma = pltpu.SemaphoreType.DMA
    scratch = [
        pltpu.VMEM((tokens, width), BF16),
        pltpu.VMEM((width, width), BF16),
        pltpu.VMEM((2 * hpad, width), BF16),
        pltpu.VMEM((hpad, width), BF16),
        pltpu.VMEM((tokens, width), BF16),
        pltpu.VMEM((tokens, width), BF16),
        pltpu.VMEM((tokens, width), BF16),
        pltpu.VMEM((tokens, hpad), BF16),
        pltpu.VMEM((tokens, hpad), BF16),
        pltpu.VMEM((tokens, 2 * hpad), BF16),
        pltpu.VMEM((chunk, width), BF16),
        pltpu.VMEM((chunk, width), BF16),
        pltpu.VMEM((chunk, width), BF16),
        pltpu.VMEM((chunk, width), F32),
        pltpu.VMEM((chunk, width), F32),
        pltpu.VMEM((RANK, 2 * hpad), BF16),
        pltpu.VMEM((RANK, hpad), BF16),
        dma((7,)),
        dma((PARTS - 1,)),
        dma((PARTS - 1,)),
        dma((PARTS - 1,)),
        dma((PARTS - 1,)),
        dma((GATHER_SEMS,)),
        dma((GATHER_SEMS,)),
    ]
    scratch += Scatter.scratch(chunk, width, EVEN)
    anywhere = pl.BlockSpec(memory_space=pl.ANY)
    return pl.pallas_call(
        functools.partial(feed_kernel, span),
        out_shape=out_shape,
        in_specs=[pl.BlockSpec(memory_space=pltpu.SMEM)] + [VMEM] * 14 + [anywhere] * 5,
        out_specs=[VMEM] * 4 + [anywhere],
        scratch_shapes=scratch,
        compiler_params=pltpu.CompilerParams(
            collective_id=1, has_side_effects=True, vmem_limit_bytes=ROOM
        ),
    )(lengths, mixed, *rest)


def turn(values, cosines, sines):
    return values * cosines + pltpu.roll(values, HD // 2, 1) * sines


def scores_of(q, keys, query_pos, key_pos, first, length):
    scores = nt(q, keys) * HD ** (-0.5)
    at = key_pos + first
    return jnp.where((at <= query_pos) & (at < length), scores, MASKED)


def back_kernel(
    rows,
    lengths,
    s_qkv,
    s_down,
    q_hbm,
    mixed_hbm,
    lse_hbm,
    dmix_hbm,
    kept_hbm,
    h1_hbm,
    cot_hbm,
    kv_hbm,
    ffn_hbm,
    table_hbm,
    dqkv_ref,
    e_qkv,
    out_ref,
    e_down,
    gather_s,
    gather_r,
    q_ref,
    mixed_ref,
    lse_ref,
    dmix_ref,
    kept_ref,
    h1_ref,
    kv_ref,
    ffn_ref,
    dkv,
    sib_far,
    hold,
    far,
    sib,
    dq,
    inner,
    total_own,
    dy_own,
    cosines,
    sines,
    local_sems,
    send_sems,
    recv_sems,
    *scratch,
):
    tokens, cols = q_ref.shape
    span = tokens // rows
    heads = cols // HD
    chunk = tokens // PARTS
    p = Place()
    core = lax.rem(p.seq, 2)
    upper = p.seq // 2
    sibling = upper * 2 + 1 - core
    loads = []
    for i, (src, dst) in enumerate(
        [
            (ffn_hbm, ffn_ref),
            (kv_hbm, kv_ref),
            (q_hbm, q_ref),
            (dmix_hbm, dmix_ref),
            (mixed_hbm, mixed_ref),
            (lse_hbm, lse_ref),
            (kept_hbm, kept_ref),
            (h1_hbm, h1_ref),
            (cot_hbm.at[rows_of(p.me, chunk)], dy_own),
            (table_hbm.at[0, rows_of(p.seq, span)], cosines),
            (table_hbm.at[1, rows_of(p.seq, span)], sines),
        ]
    ):
        loads.append(pltpu.make_async_copy(src, dst, local_sems.at[i]))
        loads[-1].start()
    barrier = pltpu.get_barrier_semaphore()
    for step in range(1, PARTS):
        place = p.at(lax.rem(p.me + step, PARTS))
        pl.semaphore_signal(barrier, inc=1, device_id=place, device_id_type=MESH)
    for seq in (sibling, (1 - upper) * 2 + core):
        pl.semaphore_signal(barrier, inc=1, device_id=(p.row, seq, p.me), device_id_type=MESH)
    e_qkv[...] = jnp.zeros_like(e_qkv)
    dq[...] = jnp.zeros_like(dq)
    pl.semaphore_wait(barrier, PARTS + 1)
    loads[0].wait()
    scatter = Scatter(p, ffn_ref, total_own, chunk, RING_FIRST, scratch)
    scatter.start_b()
    scatter.start_a(0)
    scatter.start_a(1)

    def over(source, target, index, seq):
        return pltpu.make_async_remote_copy(
            src_ref=source,
            dst_ref=target,
            send_sem=send_sems.at[index],
            recv_sem=recv_sems.at[index],
            device_id=(p.row, seq, p.me),
            device_id_type=MESH,
        )

    to_sib_far = []
    to_sib = []
    to_far = []
    for r in range(rows):
        part = slice(r * span, (r + 1) * span)
        to_sib_far.append(over(dkv.at[1 - core, part], sib_far.at[part], r, sibling))
        to_sib.append(over(dkv.at[upper * 2, part], sib.at[part], rows + r, sibling))
        to_far.append(over(hold.at[part], far.at[part], 2 * rows + r, core))

    for load in loads[1:7] + loads[9:]:
        load.wait()
    query_pos = p.seq * span + lax.broadcasted_iota(jnp.int32, (span, span), 0)
    key_pos = lax.broadcasted_iota(jnp.int32, (span, span), 1)

    for r in range(rows):
        part = slice(r * span, (r + 1) * span)
        for head in range(heads):
            at = slice(head * HD, (head + 1) * HD)
            i = r * heads + head
            inner[:, i : i + 1] = jnp.sum(
                dmix_ref[part, at].astype(F32) * mixed_ref[part, at].astype(F32),
                axis=-1,
                keepdims=True,
            )

    def blocks(r, head, first, last):
        part = slice(r * span, (r + 1) * span)
        kcols = slice(head * HD, (head + 1) * HD)
        vcols = slice(cols + head * HD, cols + (head + 1) * HD)
        i = r * heads + head

        @pl.loop(first, last)
        def _(j):
            q = q_ref[part, kcols]
            do = dmix_ref[part, kcols]
            lse = lse_ref[part, head * HD : head * HD + 1]
            scores = scores_of(q, kv_ref[j, part, kcols], query_pos, key_pos, j * span, lengths[r])
            probs = jnp.exp(scores - lse)
            dkv[j, part, vcols] = tn(probs.astype(BF16), do).astype(BF16)
            grad = (probs * (nt(do, kv_ref[j, part, vcols]) - inner[:, i : i + 1])).astype(BF16)
            dq[part, kcols] += nn(grad, kv_ref[j, part, kcols])
            dkv[j, part, kcols] = (tn(grad, q) * HD ** (-0.5)).astype(BF16)

    def onward(r):
        part = slice(r * span, (r + 1) * span)

        @pl.when(upper == 1)
        def _():
            to_sib_far[r].wait_recv()
            hold[part] = (dkv[core, part].astype(F32) + sib_far[part].astype(F32)).astype(BF16)
            to_far[r].start()

    def emit(part, at, grad):
        held = kept_ref[part, at].astype(F32)
        e_qkv[:, at] += jnp.sum(grad * held, axis=0, keepdims=True)
        dqkv_ref[part, at] = (grad * s_qkv[:, at]).astype(BF16)

    def results():
        loads[7].wait()
        loads[8].wait()
        length = lengths[0]
        for r in range(1, rows):
            length = jnp.where(p.me * chunk >= r * span, lengths[r], length)
        first = p.seq * span + lax.rem(p.me * chunk, span)
        pos = first + lax.broadcasted_iota(jnp.int32, (chunk, 1), 0)
        live = (pos < length).astype(F32)
        ffn = total_own[...] * s_down[...]
        out_ref[rows_of(p.me, chunk), :] = ((h1_ref[...] + ffn) * live).astype(BF16)
        e_down[...] = jnp.sum(dy_own[...].astype(F32) * live * ffn, axis=0, keepdims=True)

    for r in range(rows):
        for head in range(heads):
            blocks(r, head, 0, 2 * upper)

        @pl.when(upper == 1)
        def _(r=r):
            to_sib_far[r].start()

        if r == 0:
            scatter.first()
            scatter.start_other(0)
            scatter.start_other(1)
        else:
            onward(r - 1)
    for r in range(rows):
        for head in range(heads):
            blocks(r, head, 2 * upper, p.seq + 1)
            if r == 0 and head == 0:
                scatter.middle()
                scatter.late()
                onward(rows - 1)
            if r == 1 and head == 0:
                scatter.end()
                results()
                gather = Gather(p, out_ref, chunk, (gather_s, gather_r), RING_FIRST)
                gather.start()

        @pl.when(core == 1)
        def _(r=r):
            to_sib[r].start()

    gather.first()
    for r in range(rows):
        part = slice(r * span, (r + 1) * span)
        for head in range(heads):
            at = slice(head * HD, (head + 1) * HD)
            emit(part, at, turn(dq[part, at] * HD ** (-0.5), cosines[...], -sines[...]))
    gather.middle()

    for r in range(rows):
        part = slice(r * span, (r + 1) * span)

        @pl.when(core == 0)
        def _(r=r):
            to_sib[r].wait_recv()

        @pl.when(upper == 0)
        def _(r=r):
            to_far[r].wait_recv()

        for head in range(2 * heads):
            at = slice(head * HD, (head + 1) * HD)
            grad = dkv[p.seq, part, at].astype(F32)
            grad = grad + jnp.where(core == 0, sib[part, at].astype(F32), 0.0)
            grad = grad + jnp.where(upper == 0, far[part, at].astype(F32), 0.0)
            if head < heads:
                grad = turn(grad, cosines[...], -sines[...])
            emit(part, slice(cols + head * HD, cols + (head + 1) * HD), grad)
        if r == 0:
            gather.late()
    gather.end()

    for r in range(rows):

        @pl.when(upper == 1)
        def _(r=r):
            to_sib_far[r].wait_send()
            to_far[r].wait_send()

        @pl.when(core == 1)
        def _(r=r):
            to_sib[r].wait_send()


def back(rows, lengths, *rest):
    q, mixed, lse, dmix, kept, h1, _, kv, ffn, _ = rest[-10:]
    tokens, cols = q.shape
    width = ffn.shape[1]
    chunk = tokens // PARTS
    shape = jax.ShapeDtypeStruct
    dma = pltpu.SemaphoreType.DMA
    out_shape = (
        shape((tokens, 3 * cols), BF16),
        shape((1, 3 * cols), F32),
        shape((tokens, width), BF16),
        shape((1, width), F32),
    )
    scratch = [
        dma((GATHER_SEMS,)),
        dma((GATHER_SEMS,)),
        pltpu.VMEM(q.shape, BF16),
        pltpu.VMEM(mixed.shape, BF16),
        pltpu.VMEM(lse.shape, F32),
        pltpu.VMEM(dmix.shape, BF16),
        pltpu.VMEM(kept.shape, BF16),
        pltpu.VMEM(h1.shape, F32),
        pltpu.VMEM(kv.shape, BF16),
        pltpu.VMEM(ffn.shape, BF16),
        pltpu.VMEM(kv.shape, BF16),
        pltpu.VMEM((tokens, 2 * cols), BF16),
        pltpu.VMEM((tokens, 2 * cols), BF16),
        pltpu.VMEM((tokens, 2 * cols), BF16),
        pltpu.VMEM((tokens, 2 * cols), BF16),
        pltpu.VMEM((tokens, cols), F32),
        pltpu.VMEM((tokens // rows, rows * cols // HD), F32),
        pltpu.VMEM((chunk, width), F32),
        pltpu.VMEM((chunk, width), BF16),
        pltpu.VMEM((tokens // rows, HD), F32),
        pltpu.VMEM((tokens // rows, HD), F32),
        dma((11,)),
        dma((3 * rows,)),
        dma((3 * rows,)),
    ]
    scratch += Scatter.scratch(chunk, width, RING_FIRST)
    return pl.pallas_call(
        functools.partial(back_kernel, rows),
        out_shape=out_shape,
        in_specs=[pl.BlockSpec(memory_space=pltpu.SMEM)]
        + [VMEM] * 2
        + [pl.BlockSpec(memory_space=pl.ANY)] * 10,
        out_specs=[VMEM] * len(out_shape),
        scratch_shapes=scratch,
        compiler_params=pltpu.CompilerParams(
            collective_id=2, has_side_effects=True, vmem_limit_bytes=ROOM
        ),
    )(lengths, *rest)


COMMON_FEED, OWN_FEED = 128, 32
COMMON_QKV, OWN_QKV = 48, 16


class Total:
    def __init__(self, place, common, scratch):
        self.p = p = place
        self.common = common
        (
            self.send_buf,
            self.land_row,
            self.by_row,
            self.land_seq,
            self.mine,
            self.across,
            self.held,
            *self.sems,
        ) = scratch
        self.rows = [(lax.rem(p.row + step, RING), p.seq, p.me) for step in range(1, RING)]
        self.seqs = [(p.row, lax.rem(p.seq + step, RING), p.me) for step in range(1, RING)]
        self.heads = [p.at(lax.rem(p.me + step, PARTS)) for step in range(1, PARTS)]

    @staticmethod
    def scratch(common, own):
        dma = pltpu.SemaphoreType.DMA
        piece = (common + own, 128)
        return [
            pltpu.VMEM((RING * RING, *piece), BF16),
            pltpu.VMEM((RING - 1, RING, *piece), BF16),
            pltpu.VMEM((RING, *piece), BF16),
            pltpu.VMEM((RING - 1, *piece), BF16),
            pltpu.VMEM(piece, BF16),
            pltpu.VMEM((PARTS - 1, common, 128), BF16),
            pltpu.VMEM((RING * RING, *piece), BF16),
        ] + [dma((n,)) for n in (3, 3, 3, 3, PARTS - 1, PARTS - 1, 3, 3, 3, 3)]

    def greet(self):
        barrier = pltpu.get_barrier_semaphore()
        for place in self.rows + self.seqs + self.heads:
            pl.semaphore_signal(barrier, inc=1, device_id=place, device_id_type=MESH)
        pl.semaphore_wait(barrier, 2 * (RING - 1) + PARTS - 1)

    def fill(self, rows, source):
        for piece in range(RING * RING):
            self.send_buf[piece, rows] = source[:, piece * 128 : (piece + 1) * 128].astype(BF16)

    def copies(self, source, target, ends, stage):
        made = []
        for step, place in enumerate(ends):
            made.append(
                pltpu.make_async_remote_copy(
                    src_ref=source(place),
                    dst_ref=target(step),
                    send_sem=self.sems[2 * stage].at[step],
                    recv_sem=self.sems[2 * stage + 1].at[step],
                    device_id=place,
                    device_id_type=MESH,
                )
            )
            made[-1].start()
        return made

    def start(self):
        self.wait = self.copies(
            lambda place: self.send_buf.at[rows_of(place[0], RING)],
            lambda step: self.land_row.at[step],
            self.rows,
            0,
        )

    def second(self):
        for copy in self.wait:
            copy.wait()
        for q in range(RING):
            total = self.send_buf[self.p.row * RING + q].astype(F32)
            for step in range(RING - 1):
                total += self.land_row[step, q].astype(F32)
            self.by_row[q] = total.astype(BF16)
        self.wait = self.copies(
            lambda place: self.by_row.at[place[1]], lambda step: self.land_seq.at[step], self.seqs, 1
        )

    def third(self):
        for copy in self.wait:
            copy.wait()
        total = self.by_row[self.p.seq].astype(F32)
        for step in range(RING - 1):
            total += self.land_seq[step].astype(F32)
        self.mine[...] = total.astype(BF16)
        self.wait = self.copies(
            lambda place: self.mine.at[: self.common],
            lambda step: self.across.at[step],
            self.heads,
            2,
        )

    def fourth(self):
        for copy in self.wait:
            copy.wait()
        shared = self.mine[: self.common].astype(F32)
        for step in range(PARTS - 1):
            shared += self.across[step].astype(F32)
        here = self.p.row * RING + self.p.seq
        self.held[here, : self.common] = shared.astype(BF16)
        self.held[here, self.common :] = self.mine[self.common :]
        view = self.held.at[here]
        self.wait = self.copies(lambda place: view, lambda step: view, self.seqs, 3)

    def fifth(self):
        for copy in self.wait:
            copy.wait()
        view = self.held.at[rows_of(self.p.row, RING)]
        self.wait = self.copies(lambda place: view, lambda step: view, self.rows, 4)

    def end(self, out):
        for copy in self.wait:
            copy.wait()
        for piece in range(RING * RING):
            out[:, piece * 128 : (piece + 1) * 128] = self.held[piece].astype(F32)


def close_kernel(
    cols,
    dqkv_hbm,
    vqkv_hbm,
    xn1_hbm,
    x_hbm,
    dh1_hbm,
    pack_hbm,
    gain,
    b_raw,
    t_raw,
    e_qkv,
    n2_qkv,
    e_down,
    gx_ref,
    sum_feed,
    sum_qkv,
    part,
    pack,
    dqkv_ref,
    vqkv,
    dh1_ref,
    pack_feed,
    xn1,
    x_own,
    total_own,
    b_qkv,
    local_sems,
    gather_s,
    gather_r,
    *scratch,
):
    tokens, width = xn1_hbm.shape
    chunk = tokens // PARTS
    p = Place()
    own = rows_of(p.me, chunk)
    totals = Total(p, COMMON_QKV, scratch[:17])
    early = Total(p, COMMON_FEED, scratch[17:34])
    loads = []
    for i, (src, dst) in enumerate(
        [
            (dqkv_hbm, dqkv_ref),
            (vqkv_hbm, vqkv),
            (pack_hbm, pack_feed),
            (xn1_hbm, xn1),
            (x_hbm.at[own], x_own),
            (dh1_hbm, dh1_ref),
        ]
    ):
        loads.append(pltpu.make_async_copy(src, dst, local_sems.at[i]))
        loads[-1].start()
    totals.greet()
    loads[0].wait()
    loads[1].wait()

    def back_part(first, last):
        @pl.loop(first // 256, last // 256)
        def _(n):
            at = rows_of(n, 256)
            part[:, at] = nt(dqkv_ref[...], vqkv[at, :]).astype(BF16)

    scatter = Scatter(p, part, total_own, chunk, EVEN, scratch[34:])
    back_part(1024, width)
    scatter.start_b()
    back_part(0, 1024)
    scatter.start_a(0)
    scatter.start_a(1)
    scatter.start_other(0)
    scatter.start_other(1)
    loads[2].wait()
    early.fill(slice(None), pack_feed)
    row = 7 * RANK + 1
    early.fill(slice(row, row + 1), e_down)
    early.start()

    b_qkv[...] = jnp.zeros_like(b_qkv)
    for k in range(3):
        b_qkv[k * RANK : (k + 1) * RANK, k * cols : (k + 1) * cols] = b_raw[k].astype(BF16)
    t_qkv = t_raw[...].astype(BF16)
    ratio = e_qkv[...] / n2_qkv[...]
    back_qkv = (b_qkv[...].astype(F32) * ratio).astype(BF16)
    t_one = nt(b_qkv[...], dqkv_ref[...]).astype(BF16)
    loads[3].wait()
    t_two = nt(t_qkv, xn1[...]).astype(BF16)
    scatter.first()
    early.second()
    for n in range(0, width, 512):
        at = slice(n, n + 512)
        pack[: 3 * RANK, at] = nn(t_one, xn1[:, at]) - nt(back_qkv, vqkv[at, :])
        if n == width // 2:
            scatter.middle()
    gb = nn(t_two, dqkv_ref[...]) - nn(t_qkv, vqkv[...]) * ratio
    pack[COMMON_QKV:, :] = jnp.zeros((OWN_QKV, width), F32)
    for k in range(3):
        pack[COMMON_QKV:, k * cols : (k + 1) * cols] = gb[
            k * RANK : (k + 1) * RANK, k * cols : (k + 1) * cols
        ]
    pack[COMMON_QKV : COMMON_QKV + 1, 3 * cols : 6 * cols] = e_qkv[...]
    totals.fill(slice(None), pack)
    totals.start()
    scatter.late()
    early.third()
    loads[4].wait()
    loads[5].wait()
    x = x_own[...].astype(F32)
    inv1 = lax.rsqrt(jnp.mean(x * x, axis=-1, keepdims=True) + EPS)
    scatter.end()
    scaled = total_own[...] * gain[...]
    mean = jnp.mean(scaled * x, axis=-1, keepdims=True)
    grad = dh1_ref[...] + inv1 * (scaled - x * (inv1 * inv1 * mean))
    gx_ref[own, :] = grad.astype(BF16)
    gather = Gather(p, gx_ref, chunk, (gather_s, gather_r), EVEN)
    gather.start()
    totals.second()
    early.fourth()
    gather.first()
    totals.third()
    early.fifth()
    gather.middle()
    totals.fourth()
    gather.late()
    totals.fifth()
    early.end(sum_feed)
    gather.end()
    totals.end(sum_qkv)


def close(cols, dqkv, vqkv, xn1, x, dh1, pack, *rest):
    tokens, width = xn1.shape
    chunk = tokens // PARTS
    shape = jax.ShapeDtypeStruct
    dma = pltpu.SemaphoreType.DMA
    out_shape = (
        shape((tokens, width), BF16),
        shape((COMMON_FEED + OWN_FEED, width), F32),
        shape((COMMON_QKV + OWN_QKV, width), F32),
    )
    scratch = [
        pltpu.VMEM((tokens, width), BF16),
        pltpu.VMEM((COMMON_QKV + OWN_QKV, width), F32),
        pltpu.VMEM(dqkv.shape, BF16),
        pltpu.VMEM(vqkv.shape, BF16),
        pltpu.VMEM(dh1.shape, F32),
        pltpu.VMEM(pack.shape, F32),
        pltpu.VMEM((tokens, width), BF16),
        pltpu.VMEM((chunk, width), BF16),
        pltpu.VMEM((chunk, width), F32),
        pltpu.VMEM((3 * RANK, 3 * cols), BF16),
        dma((6,)),
        dma((GATHER_SEMS,)),
        dma((GATHER_SEMS,)),
    ]
    scratch += Total.scratch(COMMON_QKV, OWN_QKV) + Total.scratch(COMMON_FEED, OWN_FEED)
    scratch += Scatter.scratch(chunk, width, EVEN)
    return pl.pallas_call(
        functools.partial(close_kernel, cols),
        out_shape=out_shape,
        in_specs=[pl.BlockSpec(memory_space=pl.ANY)] * 6 + [VMEM] * len(rest),
        out_specs=[VMEM] * 3,
        scratch_shapes=scratch,
        compiler_params=pltpu.CompilerParams(
            collective_id=3, has_side_effects=True, vmem_limit_bytes=ROOM
        ),
    )(dqkv, vqkv, xn1, x, dh1, pack, *rest)


def three_terms(left, right):
    def split(a):
        high = a.astype(BF16)
        return high, (a - high.astype(F32)).astype(BF16)

    left_high, left_low = split(left)
    right_high, right_low = split(right)
    return (
        jnp.concatenate([left_high, left_low, left_high], axis=0),
        jnp.concatenate([right_high, right_high, right_low], axis=0),
    )


def front_kernel(
    rows,
    spread,
    lengths,
    gain,
    m_qkv,
    m_out,
    m_gu,
    m_down,
    t_qkv,
    b_qkv,
    t_out,
    b_out,
    t_gu,
    b_gu,
    t_down,
    b_down,
    x_hbm,
    wqkv_hbm,
    wout_hbm,
    wgu_hbm,
    wdown_hbm,
    table_hbm,
    q_ref,
    kept_ref,
    mixed_ref,
    lse_ref,
    n2_qkv,
    n2_gu,
    n2_model,
    s_qkv,
    s_gu,
    s_out,
    s_down,
    at_out,
    av_out,
    av_down,
    xn1_hbm,
    vqkv_hbm,
    vout_hbm,
    vgu_hbm,
    vdown_hbm,
    kv_hbm,
    x_ref,
    wqkv,
    wout,
    wgu,
    wdown,
    xn1,
    vqkv,
    vfull,
    vgu,
    vdown,
    kv,
    acc,
    top,
    weight,
    squares,
    land_squares,
    at_mine,
    cosines,
    sines,
    load_sems,
    store_sems,
    gather_s,
    gather_r,
    share_s,
    share_r,
    kv_s,
    kv_r,
    square_s,
    square_r,
    at_s,
    at_r,
):
    tokens, width = x_ref.shape
    span = tokens // rows
    cols = q_ref.shape[1]
    heads = cols // HD
    hidden = wdown.shape[0]
    hpad = vdown.shape[0]
    p = Place()
    core = lax.rem(p.seq, 2)
    upper = p.seq // 2
    sibling = upper * 2 + 1 - core
    loads = []
    pairs = [(wout_hbm, wout), (wqkv_hbm, wqkv), (x_hbm, x_ref), (wdown_hbm, wdown), (wgu_hbm, wgu)]
    here = rows_of(p.seq, span)
    pairs += [(table_hbm.at[0, here], cosines), (table_hbm.at[1, here], sines)]
    for i, (src, dst) in enumerate(pairs):
        loads.append(pltpu.make_async_copy(src, dst, load_sems.at[i]))
        loads[-1].start()
    barrier = pltpu.get_barrier_semaphore()
    for step in range(1, PARTS):
        place = p.at(lax.rem(p.me + step, PARTS))
        pl.semaphore_signal(barrier, inc=1, device_id=place, device_id_type=MESH)
    for seq in (sibling, (1 - upper) * 2 + core):
        pl.semaphore_signal(barrier, inc=1, device_id=(p.row, seq, p.me), device_id_type=MESH)

    left, right = three_terms(t_out[...], b_out[...])
    my_cols = rows_of(p.me, cols)
    loads[0].wait()
    squares[...] = jnp.zeros_like(squares)
    for n in range(0, width, 512):
        at = slice(n, n + 512)
        v = wout[:, at].astype(F32) + SCALE * tn(left, right[:, at])
        vfull[my_cols, at] = v.astype(BF16)
        squares[0:1, at] = jnp.sum(v * v, axis=0, keepdims=True)
    at_mine[...] = t_out[...].astype(BF16)
    at_out[:, my_cols] = t_out[...].astype(BF16)
    pl.semaphore_wait(barrier, PARTS + 1)
    gather = Gather(p, vfull, cols // 2, (gather_s, gather_r), RING_MOST, cols, core)
    gather.start()
    at_copies = []
    for step in range(1, PARTS):
        to = lax.rem(p.me + step, PARTS)
        at_copies.append(p.send(at_mine, at_out.at[:, my_cols], (at_s, at_r), step - 1, to))

    loads[1].wait()

    def direct(k):
        left, right = three_terms(t_qkv[k], b_qkv[k])
        at = slice(k * cols, (k + 1) * cols)
        total = jnp.zeros((1, cols), F32)
        for n in range(0, width, 512):
            part = slice(n, n + 512)
            v = wqkv[k, part, :].astype(F32) + SCALE * tn(left[:, part], right)
            vqkv[part, at] = v.astype(BF16)
            total += jnp.sum(v * v, axis=0, keepdims=True)
        n2_qkv[:, at] = total
        s_qkv[:, at] = m_qkv[k : k + 1, :] * lax.rsqrt(total)

    def project(r, k):
        part = slice(r * span, (r + 1) * span)
        at = slice(k * cols, (k + 1) * cols)
        y = nn(xn1[part, :], vqkv[:, at]) * s_qkv[:, at]
        kept_ref[part, at] = y.astype(BF16)
        if k < 2:
            y = jnp.concatenate(
                [turn(y[:, h * HD : (h + 1) * HD], cosines[...], sines[...]) for h in range(heads)],
                axis=1,
            )
        if k == 0:
            q_ref[part, :] = y.astype(BF16)
        else:
            kv[p.seq, part, (k - 1) * cols : k * cols] = y.astype(BF16)

    def over(source, index, seq):
        return pltpu.make_async_remote_copy(
            src_ref=source,
            dst_ref=source,
            send_sem=kv_s.at[index],
            recv_sem=kv_r.at[index],
            device_id=(p.row, seq, p.me),
            device_id_type=MESH,
        )

    direct(1)
    direct(2)
    for load in (loads[2], loads[5], loads[6]):
        load.wait()
    to_sib, to_far, onward = [], [], []
    for r in range(rows):
        part = slice(r * span, (r + 1) * span)
        to_sib.append(over(kv.at[p.seq, part], r, sibling))
        to_far.append(over(kv.at[p.seq, part], rows + r, 2 + core))
        onward.append(over(kv.at[core, part], 2 * rows + r, sibling))

        @pl.loop(0, span // 128)
        def _(i, r=r):
            piece = pl.ds(pl.multiple_of(r * span + i * 128, 128), 128)
            x = x_ref[piece, :].astype(F32)
            inv = lax.rsqrt(jnp.mean(x * x, axis=-1, keepdims=True) + EPS)
            xn1[piece, :] = (x * inv * gain[...]).astype(BF16)

        project(r, 1)
        project(r, 2)

        @pl.when(upper == 0)
        def _(r=r):
            to_far[r].start()

        @pl.when(core == 0)
        def _(r=r):
            to_sib[r].start()

    direct(0)
    for r in range(rows):
        project(r, 0)
    stores = [
        pltpu.make_async_copy(vqkv, vqkv_hbm, store_sems.at[1]),
        pltpu.make_async_copy(xn1, xn1_hbm, store_sems.at[2]),
    ]
    for copy in stores:
        copy.start()

    query_pos = p.seq * span + lax.broadcasted_iota(jnp.int32, (span, span), 0)
    key_pos = lax.broadcasted_iota(jnp.int32, (span, span), 1)

    def absorb(r, j, fresh=False):
        part = slice(r * span, (r + 1) * span)
        for head in range(heads):
            at = slice(head * HD, (head + 1) * HD)
            to = slice(cols + head * HD, cols + (head + 1) * HD)
            one = (slice(None), slice(r * heads + head, r * heads + head + 1))
            scores = scores_of(
                q_ref[part, at], kv[j, part, at], query_pos, key_pos, j * span, lengths[r]
            )
            best = jnp.max(scores, axis=-1, keepdims=True)
            if not fresh:
                best = jnp.maximum(best, top[one])
            expo = jnp.exp(scores - best)
            summed = jnp.sum(expo, axis=-1, keepdims=True)
            mixed = nn(expo.astype(BF16), kv[j, part, to])
            if not fresh:
                fade = jnp.exp(top[one] - best)
                summed += weight[one] * fade
                mixed += acc[part, at] * fade
            top[one] = best
            weight[one] = summed
            acc[part, at] = mixed

    gather.first()
    for r in range(rows):
        absorb(r, p.seq, True)
    gather.middle()

    loads[3].wait()
    vdown[hidden:, :] = jnp.zeros((hpad - hidden, width), BF16)
    left, right = three_terms(t_down[...], b_down[...])
    for n in range(0, width, 512):
        at = slice(n, n + 512)
        v = wdown[:, at].astype(F32) + SCALE * tn(left, right[:, at])
        vdown[:hidden, at] = v.astype(BF16)
        squares[1:2, at] = jnp.sum(v * v, axis=0, keepdims=True)
    square_copies = []
    for step in range(1, PARTS):
        to = lax.rem(p.me + step, PARTS)
        square_copies.append(
            p.send(squares, land_squares.at[step - 1], (square_s, square_r), step - 1, to)
        )
    stores.append(pltpu.make_async_copy(vdown, vdown_hbm, store_sems.at[3]))
    stores[-1].start()
    shares = []

    def share(plane, steps):
        for step in steps:
            view = gather.view(plane * RING + p.side(step))
            index = len(shares)
            shares.append(
                pltpu.make_async_remote_copy(
                    src_ref=view,
                    dst_ref=view,
                    send_sem=share_s.at[index],
                    recv_sem=share_r.at[index],
                    device_id=(p.row, sibling, p.me),
                    device_id_type=MESH,
                )
            )

            shares[-1].start()

    share(p.z, (1, 2, 3))

    loads[4].wait()
    ones = jnp.ones((8, width), BF16)
    for k in range(2):
        left, right = three_terms(b_gu[k], t_gu[k])
        base = k * hpad
        vgu[base + hidden : base + hpad, :] = jnp.zeros((hpad - hidden, width), BF16)
        n2_gu[:, base + hidden : base + hpad] = jnp.ones((1, hpad - hidden), F32)
        for n in range(0, hidden, 128):
            size = min(128, hidden - n)
            v = wgu[k, n : n + size, :].astype(F32) + SCALE * tn(left[:, n : n + size], right)
            vgu[base + n : base + n + size, :] = v.astype(BF16)
            n2_gu[:, base + n : base + n + size] = nt(ones, (v * v).astype(BF16))[:1]
        units = slice(base, base + hidden)
        s_gu[:, base : base + hpad] = jnp.zeros((1, hpad), F32)
        s_gu[:, units] = m_gu[k : k + 1, :] * lax.rsqrt(n2_gu[:, units])
    stores.append(pltpu.make_async_copy(vgu, vgu_hbm, store_sems.at[4]))
    stores[-1].start()
    gather.late()

    @pl.when(core == 1)
    def _():
        for r in range(rows):
            to_sib[r].wait_recv()
            absorb(r, p.seq - 1)

    for copy in shares:
        copy.wait_recv()
    half = rows_of(p.z, RING * cols)
    stores.append(pltpu.make_async_copy(vfull.at[half], vout_hbm.at[half], store_sems.at[0]))
    stores[-1].start()

    def from_far(r):
        @pl.when(upper == 1)
        def _():
            to_far[r].wait_recv()
            onward[r].start()
            absorb(r, core)
            onward[r].wait_recv()
            absorb(r, 1 - core)

    from_far(0)
    gather.end()
    share(p.far, (0, 1, 2, 3))
    for r in range(1, rows):
        from_far(r)

    @pl.loop(p.seq + 1, kv.shape[0])
    def _(j):
        kv[j] = jnp.zeros(kv.shape[1:], BF16)

    stores.append(pltpu.make_async_copy(kv, kv_hbm, store_sems.at[5]))
    stores[-1].start()
    for r in range(rows):
        part = slice(r * span, (r + 1) * span)
        for head in range(heads):
            at = slice(head * HD, (head + 1) * HD)
            one = (slice(None), slice(r * heads + head, r * heads + head + 1))
            mixed_ref[part, at] = (acc[part, at] / weight[one]).astype(BF16)
            lse_ref[part, at] = jnp.broadcast_to(top[one] + jnp.log(weight[one]), (span, HD))
    av_out[...] = nn(at_mine[...], vfull[my_cols, :]) / spread
    at_down = t_down[...].astype(BF16)
    av_down[...] = nn(at_down, vdown[:hidden, :]) / spread
    for copy in square_copies:
        copy.wait_recv()
    total = squares[...]
    for step in range(PARTS - 1):
        total += land_squares[step]
    n2_model[...] = total
    s_out[...] = m_out[...] * lax.rsqrt(total[0:1])
    s_down[...] = m_down[...] * lax.rsqrt(total[1:2])
    for copy in at_copies + shares[RING - 1 :]:
        copy.wait_recv()
    half = rows_of(p.far, RING * cols)
    stores.append(pltpu.make_async_copy(vfull.at[half], vout_hbm.at[half], store_sems.at[6]))
    stores[-1].start()
    for copy in at_copies + square_copies + shares:
        copy.wait_send()
    for copy in stores:
        copy.wait()

    @pl.when(upper == 0)
    def _():
        for r in range(rows):
            to_far[r].wait_send()

    @pl.when(core == 0)
    def _():
        for r in range(rows):
            to_sib[r].wait_send()

    @pl.when(upper == 1)
    def _():
        for r in range(rows):
            onward[r].wait_send()


def front(rows, seqs, spread, lengths, *rest):
    x, w_qkv, _, _, w_down, _ = rest[-6:]
    tokens, width = x.shape
    cols = w_qkv.shape[2]
    heads = cols // HD
    hidden = w_down.shape[0]
    hpad = pad_to(hidden)
    span = tokens // rows
    shape = jax.ShapeDtypeStruct
    dma = pltpu.SemaphoreType.DMA
    vmem = pltpu.VMEM
    out_shape = (
        shape((tokens, cols), BF16),
        shape((tokens, 3 * cols), BF16),
        shape((tokens, cols), BF16),
        shape((tokens, cols), F32),
        shape((1, 3 * cols), F32),
        shape((1, 2 * hpad), F32),
        shape((8, width), F32),
        shape((1, 3 * cols), F32),
        shape((1, 2 * hpad), F32),
        shape((1, width), F32),
        shape((1, width), F32),
        shape((RANK, width), BF16),
        shape((RANK, width), F32),
        shape((RANK, width), F32),
        shape((tokens, width), BF16),
        shape((width, 3 * cols), BF16),
        shape((PARTS * cols, width), BF16),
        shape((2 * hpad, width), BF16),
        shape((hpad, width), BF16),
        shape((seqs, tokens, 2 * cols), BF16),
    )
    scratch = [
        vmem((tokens, width), BF16),
        vmem((3, width, cols), BF16),
        vmem((cols, width), BF16),
        vmem((2, hidden, width), BF16),
        vmem((hidden, width), BF16),
        vmem((tokens, width), BF16),
        vmem((width, 3 * cols), BF16),
        vmem((PARTS * cols, width), BF16),
        vmem((2 * hpad, width), BF16),
        vmem((hpad, width), BF16),
        vmem((seqs, tokens, 2 * cols), BF16),
        vmem((tokens, cols), F32),
        vmem((span, rows * heads), F32),
        vmem((span, rows * heads), F32),
        vmem((8, width), F32),
        vmem((PARTS - 1, 8, width), F32),
        vmem((RANK, cols), BF16),
        vmem((span, HD), F32),
        vmem((span, HD), F32),
        dma((7,)),
        dma((7,)),
        dma((GATHER_SEMS,)),
        dma((GATHER_SEMS,)),
        dma((PARTS,)),
        dma((PARTS,)),
        dma((3 * rows,)),
        dma((3 * rows,)),
    ] + [dma((PARTS - 1,))] * 4
    anywhere = pl.BlockSpec(memory_space=pl.ANY)
    return pl.pallas_call(
        functools.partial(front_kernel, rows, spread),
        out_shape=out_shape,
        in_specs=[pl.BlockSpec(memory_space=pltpu.SMEM)] + [VMEM] * 13 + [anywhere] * 6,
        out_specs=[VMEM] * 14 + [anywhere] * 6,
        scratch_shapes=scratch,
        compiler_params=pltpu.CompilerParams(
            collective_id=4, has_side_effects=True, vmem_limit_bytes=ROOM
        ),
    )(lengths, *rest)


def finish_kernel(
    hidden,
    summed,
    summed_qkv,
    m_qkv,
    m_out,
    m_gu,
    m_down,
    n2_model,
    b_out,
    b_down,
    vdown_hbm,
    vout_hbm,
    out_hbm,
    gx_hbm,
    output,
    grad_x,
    gm_qkv,
    ga_qkv,
    gb_qkv,
    gm_out,
    ga_out,
    gb_out,
    gm_gu,
    ga_gu,
    gb_gu,
    gm_down,
    ga_down,
    gb_down,
    vout,
    vdown,
    held,
    sems,
):
    cols, width = vout.shape
    hpad = vdown.shape[0]
    load = pltpu.make_async_copy(vout_hbm.at[rows_of(lax.axis_index("head"), cols)], vout, sems.at[0])
    load.start()
    load_down = pltpu.make_async_copy(vdown_hbm, vdown, sems.at[33])
    load_down.start()
    moves = []
    tokens = output.shape[0]
    for i in range(8):
        part = pl.ds(i * tokens // 8, tokens // 8)
        for k, src in enumerate((out_hbm, gx_hbm)):
            moves.append(pltpu.make_async_copy(src.at[part], held.at[k, part], sems.at[1 + 2 * i + k]))
            moves[-1].start()
    for i in range(8):
        part = pl.ds(i * tokens // 8, tokens // 8)
        for k, dst in enumerate((output, grad_x)):
            moves[2 * i + k].wait()
            moves.append(pltpu.make_async_copy(held.at[k, part], dst.at[part], sems.at[17 + 2 * i + k]))
            moves[-1].start()

    def block(first):
        return summed[first * RANK : (first + 1) * RANK, :]

    own_qkv = slice(COMMON_QKV, COMMON_QKV + RANK)
    for k in range(3):
        at = slice(k * cols, (k + 1) * cols)
        ga_qkv[k] = SCALE * summed_qkv[k * RANK : (k + 1) * RANK, :]
        gb_qkv[k] = SCALE * summed_qkv[own_qkv, at]
        e_one = summed_qkv[COMMON_QKV : COMMON_QKV + 1, (3 + k) * cols : (4 + k) * cols]
        gm_qkv[k : k + 1, :] = e_one / m_qkv[k : k + 1, :]
    for k in range(2):
        ga_gu[k] = SCALE * block(k)
    e_out = summed[7 * RANK : 7 * RANK + 1, :]
    e_down = summed[7 * RANK + 1 : 7 * RANK + 2, :]
    ratio_out = e_out / n2_model[0:1, :]
    ratio_down = e_down / n2_model[1:2, :]
    gm_out[...] = e_out / m_out[...]
    gm_down[...] = e_down / m_down[...]
    gb_out[...] = SCALE * (block(2) - block(5) * ratio_out)
    gb_down[...] = SCALE * (block(3) - block(6) * ratio_down)
    own_rows = slice(COMMON_FEED, COMMON_FEED + RANK)
    fold_rows = slice(COMMON_FEED + RANK, COMMON_FEED + OWN_FEED)
    fits = width - 2 * hpad
    gb = summed[own_rows, : 2 * hpad]
    e_gu = summed[COMMON_FEED + RANK : COMMON_FEED + RANK + 1, fits:]
    for k in range(2):
        at = slice(k * hpad, k * hpad + hidden)
        gb_gu[k] = SCALE * gb[:, at]
        gm_gu[k : k + 1, :] = e_gu[:, at] / m_gu[k : k + 1, :]
    back_down = (b_down[...] * ratio_down).astype(BF16)
    load_down.wait()
    down = jnp.concatenate([summed[own_rows, 2 * hpad :], summed[fold_rows, : hpad - fits]], axis=1)
    down = down - nt(back_down, vdown[...])
    ga_down[...] = SCALE * down[:, :hidden]
    load.wait()
    back_out = (b_out[...] * ratio_out).astype(BF16)
    at = rows_of(lax.axis_index("head"), cols)
    ga_out[...] = SCALE * (summed[4 * RANK : 5 * RANK, at] - nt(back_out, vout[...]))
    for move in moves[16:]:
        move.wait()


def finish(hidden, cols, summed, *rest):
    width = summed.shape[1]
    tokens = rest[-1].shape[0]
    shape = jax.ShapeDtypeStruct
    out_shape = (
        shape((tokens, width), BF16),
        shape((tokens, width), BF16),
        shape((3, cols), F32),
        shape((3, RANK, width), F32),
        shape((3, RANK, cols), F32),
        shape((1, width), F32),
        shape((RANK, cols), F32),
        shape((RANK, width), F32),
        shape((2, hidden), F32),
        shape((2, RANK, width), F32),
        shape((2, RANK, hidden), F32),
        shape((1, width), F32),
        shape((RANK, hidden), F32),
        shape((RANK, width), F32),
    )
    anywhere = pl.BlockSpec(memory_space=pl.ANY)
    return pl.pallas_call(
        functools.partial(finish_kernel, hidden),
        out_shape=out_shape,
        in_specs=[VMEM] * 9 + [anywhere] * 4,
        out_specs=[anywhere] * 2 + [VMEM] * 12,
        scratch_shapes=[
            pltpu.VMEM((cols, width), BF16),
            pltpu.VMEM(rest[-4].shape, BF16),
            pltpu.VMEM((2, tokens, width), BF16),
            pltpu.SemaphoreType.DMA((34,)),
        ],
        compiler_params=pltpu.CompilerParams(vmem_limit_bytes=ROOM),
    )(summed, *rest)


def rope_table(slots):
    freqs = np.float32(ROPE_BASE) ** (-np.arange(HD // 2, dtype=np.float32) * np.float32(2.0 / HD))
    turned = np.arange(slots, dtype=np.float32)[:, None] * freqs[None, :]
    cosines, sines = np.cos(turned), np.sin(turned)
    return np.stack(
        [np.concatenate([cosines, cosines], axis=1), np.concatenate([-sines, sines], axis=1)]
    ).astype(np.float32)


def shards(
    layer_input,
    cotangent,
    lengths,
    gain_attn,
    gain_ffn,
    w_qkv,
    m_qkv,
    a_qkv,
    b_qkv,
    w_out,
    m_out,
    a_out,
    b_out,
    w_gu,
    m_gu,
    a_gu,
    b_gu,
    w_down,
    m_down,
    a_down,
    b_down,
):
    rows, span, width = layer_input.shape
    seqs = lax.axis_size("seq")
    tokens = rows * span
    cols = w_qkv.shape[2]
    hidden = w_gu.shape[2]
    hpad = pad_to(hidden)

    table = jnp.asarray(rope_table(span * seqs))
    x = layer_input.reshape(tokens, width)
    t_qkv, t_gu = a_qkv.transpose(0, 2, 1), a_gu.transpose(0, 2, 1)
    t_out, t_down = a_out.T, a_down.T
    (
        query,
        kept,
        mixed,
        lse,
        n2_qkv,
        n2_gu,
        n2_model,
        s_qkv,
        s_gu,
        s_out,
        s_down,
        full_t_out,
        av_out,
        av_down,
        normed1,
        vb_qkv,
        full_out,
        vb_gu,
        vb_down,
        pairs,
    ) = front(
        rows,
        seqs,
        float(lax.axis_size("row") * seqs),
        lengths,
        gain_attn[None],
        m_qkv,
        m_out[None],
        m_gu,
        m_down[None],
        t_qkv,
        b_qkv,
        t_out,
        b_out,
        t_gu,
        b_gu,
        t_down,
        b_down,
        x,
        w_qkv,
        w_out,
        w_gu.transpose(0, 2, 1),
        w_down,
        table,
    )
    cot = cotangent.reshape(tokens, width)
    (
        hidden1,
        grad_h1,
        grad_mixed,
        pack,
        ffn_part,
    ) = feed(
        span,
        lengths,
        mixed,
        s_out,
        gain_ffn[None],
        s_gu,
        s_down,
        n2_gu,
        b_gu,
        t_gu.reshape(2 * RANK, width),
        t_down,
        b_down,
        b_out,
        full_t_out,
        av_out,
        av_down,
        x,
        cot,
        full_out,
        vb_gu,
        vb_down,
    )
    dqkv, e_qkv, output, e_down = back(
        rows,
        lengths,
        s_qkv,
        s_down,
        query,
        mixed,
        lse,
        grad_mixed,
        kept,
        hidden1,
        cot,
        pairs,
        ffn_part,
        table,
    )
    grad_x, summed, summed_qkv = close(
        cols,
        dqkv,
        vb_qkv,
        normed1,
        x,
        grad_h1,
        pack,
        gain_attn[None],
        b_qkv,
        t_qkv.reshape(3 * RANK, width),
        e_qkv,
        n2_qkv,
        e_down,
    )
    (
        output,
        grad_x,
        gm_qkv,
        ga_qkv,
        gb_qkv,
        gm_out,
        ga_out,
        gb_out,
        gm_gu,
        ga_gu,
        gb_gu,
        gm_down,
        ga_down,
        gb_down,
    ) = finish(
        hidden,
        cols,
        summed,
        summed_qkv,
        m_qkv,
        m_out[None],
        m_gu,
        m_down[None],
        n2_model,
        b_out,
        b_down,
        vb_down,
        full_out,
        output,
        grad_x,
    )
    return (
        output.reshape(rows, span, width),
        grad_x.reshape(rows, span, width),
        gm_qkv,
        ga_qkv.transpose(0, 2, 1),
        gb_qkv,
        gm_out[0],
        ga_out.T,
        gb_out,
        gm_gu,
        ga_gu.transpose(0, 2, 1),
        gb_gu,
        gm_down[0],
        ga_down.T,
        gb_down,
    )


def solution(mesh):
    placed = (
        P("row", "seq", None),
        P("row", "seq", None),
        P("row"),
        P(),
        P(),
        P(None, None, "head"),
        P(None, "head"),
        P(),
        P(None, None, "head"),
        P("head", None),
        P(),
        P("head", None),
        P(),
        P(None, None, "head"),
        P(None, "head"),
        P(),
        P(None, None, "head"),
        P("head", None),
        P(),
        P("head", None),
        P(),
    )
    return jax.shard_map(
        shards,
        mesh=mesh,
        in_specs=placed,
        out_specs=(
            P("row", "seq", None),
            P("row", "seq", None),
            P(None, "head"),
            P(),
            P(None, None, "head"),
            P(),
            P("head", None),
            P(),
            P(None, "head"),
            P(),
            P(None, None, "head"),
            P(),
            P("head", None),
            P(),
        ),
        check_vma=False,
    )
```

```python
import functools

import jax
import jax.numpy as jnp
from jax import lax
from jax.experimental import pallas as pl
from jax.experimental.pallas import tpu as pltpu
from jax.sharding import PartitionSpec as P

HD = 128
RANK = 16
SCALE = 2.0
EPS = 1e-05
ROPE_BASE = 10000.0
MASKED = -1000000000.0
F32 = jnp.float32
BF16 = jnp.bfloat16


def pad_to(n, m=256):
    return -(-n // m) * m


def mm(a, b, dims):
    return lax.dot_general(a, b, (dims, ((), ())), preferred_element_type=F32)


def nn(a, b):
    return mm(a, b, ((1,), (0,)))


def nt(a, b):
    return mm(a, b, ((1,), (1,)))


def tn(a, b):
    return mm(a, b, ((0,), (0,)))


MESH = pl.DeviceIdType.MESH
VMEM = pl.BlockSpec(memory_space=pltpu.VMEM)
ROOM = 60 * 2**20
RING = 4
PARTS = 8


class Place:
    def __init__(self):
        self.row, self.seq, self.me = (lax.axis_index(n) for n in ("row", "seq", "head"))
        self.y = lax.rem(self.me, RING)
        self.z = self.me // RING
        self.far = 1 - self.z
        self.cross = self.far * RING + self.y

    def side(self, step):
        return lax.rem(self.y + step + RING, RING)

    def at(self, head):
        return (self.row, self.seq, head)

    def greet(self):
        barrier = pltpu.get_barrier_semaphore()
        for step in range(1, PARTS):
            pl.semaphore_signal(
                barrier, inc=1, device_id=self.at(lax.rem(self.me + step, PARTS)), device_id_type=MESH
            )
        pl.semaphore_wait(barrier, PARTS - 1)

    def send(self, source, target, sems, index, head):
        copy = pltpu.make_async_remote_copy(
            src_ref=source,
            dst_ref=target,
            send_sem=sems[0].at[index],
            recv_sem=sems[1].at[index],
            device_id=self.at(head),
            device_id_type=MESH,
        )
        copy.start()
        return copy


def rows_of(index, count):
    return pl.ds(pl.multiple_of(index * count, count), count)


EVEN = {"a": (0, 640, 1152), "b": (1152, 1536, 2048)}
RING_FIRST = {"a": (0, 768, 1536), "b": (1536, 1792, 2048)}
RING_MOST = {"a": (0, 896, 1792), "b": (1792, 1920, 2048)}
UP, DOWN = 1, -1


def span_of(spans, which, half=None):
    first, split, last = spans[which]
    if half == UP:
        last = split
    if half == DOWN:
        first = split
    return first, last


class Gather:
    def __init__(self, place, buf, chunk, sems, spans, stride=None, offset=0):
        self.place, self.buf, self.chunk, self.sems, self.spans = place, buf, chunk, sems, spans
        self.stride, self.offset = stride or chunk, offset
        self.sent = []

    def view(self, head, which=None, half=None):
        first = head * self.stride + self.offset * self.chunk
        rows = pl.ds(pl.multiple_of(first, self.chunk), self.chunk)
        if which is None:
            return self.buf.at[rows]
        first, last = span_of(self.spans, which, half)
        return self.buf.at[rows, first:last]

    def pass_on(self, head, which, half, index, to):
        view = self.view(head, which, half)
        copy = self.place.send(view, view, self.sems, index, to)
        self.sent.append(copy)
        return copy

    def ring(self, head, which, index):
        p = self.place
        return {
            way: self.pass_on(head, which, None, index + i, p.z * RING + p.side(way))
            for i, way in enumerate((UP, DOWN))
        }

    def relay(self, copies, plane, which, index, then=None):
        p = self.place
        made = []
        for i, way in enumerate((UP, DOWN)):
            copies[way].wait_recv()
            head = plane * RING + p.side(-way)
            made.append(self.pass_on(head, which, way, index + i, p.z * RING + p.side(way)))
            if then is not None:
                then(head, i)
        return made

    def start(self):
        p = self.place
        self.rest = []
        self.a_cross = self.pass_on(p.me, "a", None, 0, p.cross)
        self.b_ring = self.ring(p.me, "b", 6)
        self.a_ring = self.ring(p.me, "a", 8)
        self.rest.append(self.pass_on(p.me, "b", None, 1, p.cross))

    def first(self):
        p = self.place

        def across(head, i):
            self.rest.append(self.pass_on(head, "b", None, 2 + i, p.cross))

        self.b_relay = self.relay(self.b_ring, p.z, "b", 10, across)
        self.a_cross.wait_recv()
        self.far_ring = self.ring(p.cross, "a", 14)
        self.a_relay = self.relay(self.a_ring, p.z, "a", 12)

    def middle(self):
        p = self.place
        opposite = p.z * RING + p.side(2)
        for i, way in enumerate((UP, DOWN)):
            self.b_relay[i].wait_recv()
            self.rest.append(self.pass_on(opposite, "b", way, 4 + i, p.cross))
        for copy in self.a_relay:
            copy.wait_recv()

    def late(self):
        self.rest += self.relay(self.far_ring, self.place.far, "a", 16)

    def end(self):
        for copy in self.rest:
            copy.wait_recv()
        for copy in self.sent:
            copy.wait_send()


GATHER_SEMS = 18


class Scatter:
    def __init__(self, place, src, out, chunk, spans, scratch):
        self.place, self.src, self.out, self.chunk = place, src, out, chunk
        self.spans = spans
        self.cut = spans["a"][2]
        (
            self.far_b,
            self.hold_b,
            self.relay_b,
            self.land_b,
            self.hold_a,
            self.relay_a,
            self.land_a,
            self.hold_far,
            self.land_far,
            s,
            r,
        ) = scratch
        self.sems = (s, r)
        self.sent = []
        self.a_relay = [None, None]
        self.a_other = [[], []]

    @staticmethod
    def scratch(chunk, width, spans):
        a = spans["a"][2]
        b = width - a
        return [
            pltpu.VMEM((RING, chunk, b), BF16),
            pltpu.VMEM((3, chunk, b), BF16),
            pltpu.VMEM((chunk, b), BF16),
            pltpu.VMEM((2, chunk, b), BF16),
            pltpu.VMEM((2, 2, chunk, a), BF16),
            pltpu.VMEM((2, chunk, a), BF16),
            pltpu.VMEM((2, 2, chunk, a), BF16),
            pltpu.VMEM((chunk, a), BF16),
            pltpu.VMEM((chunk, a), BF16),
            pltpu.SemaphoreType.DMA((21,)),
            pltpu.SemaphoreType.DMA((21,)),
        ]

    def send(self, source, target, index, head):
        copy = self.place.send(source, target, self.sems, index, head)
        self.sent.append(copy)
        return copy

    def mine(self, plane, y, which):
        first, last = span_of(self.spans, which)
        return self.src[rows_of(plane * RING + y, self.chunk), first:last].astype(F32)

    def within(self, which, half):
        base = self.spans[which][0]
        first, last = span_of(self.spans, which, half)
        return slice(first - base, last - base)

    def opposite(self, source, target, which, index):
        p = self.place
        made = {}
        for i, half in enumerate((UP, DOWN)):
            part = self.within(which, half)
            made[half] = self.send(
                source(half, part), target.at[:, part], index + i, p.z * RING + p.side(-half)
            )
        return made

    def start_b(self):
        p = self.place
        self.across = []
        for i, step in enumerate((2, DOWN, UP, 0)):
            view = self.src.at[rows_of(p.far * RING + p.side(step), self.chunk), self.cut :]
            self.across.append(self.send(view, self.far_b.at[i], i, p.cross))

    def start_a(self, k):
        p = self.place
        plane = p.z if k else p.far
        rows = rows_of(plane * RING + p.side(2), self.chunk)

        def source(half, part):
            return self.src.at[rows, part]

        self.a_relay[k] = self.opposite(source, self.relay_a.at[k], "a", 5 + 2 * k)

    def start_other(self, k):
        p = self.place
        plane = p.z if k else p.far
        for i, way in enumerate((DOWN, UP)):
            part = self.within("a", way)
            to = p.side(way)
            self.a_other[k].append(
                self.send(
                    self.src.at[rows_of(plane * RING + to, self.chunk), part],
                    self.land_a.at[k, i, :, part],
                    17 + 2 * k + i,
                    p.z * RING + to,
                )
            )

    def first(self):
        p = self.place
        self.a_direct = []
        for k, plane in enumerate((p.far, p.z)):
            made = {}
            for i, way in enumerate((DOWN, UP)):
                half = -way
                part = self.within("a", half)
                self.a_relay[k][half].wait_recv()
                rows = rows_of(plane * RING + p.side(way), self.chunk)
                self.hold_a[k, i, :, part] = (
                    self.src[rows, part].astype(F32) + self.relay_a[k, :, part].astype(F32)
                ).astype(BF16)
                made[way] = self.send(
                    self.hold_a.at[k, i, :, part],
                    self.land_a.at[k, i, :, part],
                    9 + 2 * k + i,
                    p.z * RING + p.side(way),
                )
            self.a_direct.append(made)
        self.across[0].wait_recv()
        total = self.mine(p.z, p.side(2), "b") + self.far_b[0].astype(F32)
        self.hold_b[2] = total.astype(BF16)

        def source(half, part):
            return self.hold_b.at[2, :, part]

        self.b_relay = self.opposite(source, self.relay_b, "b", 13)

    def middle(self):
        p = self.place
        total = self.mine(p.far, p.y, "a")
        for i, way in enumerate((DOWN, UP)):
            self.a_direct[0][way].wait_recv()
            self.a_other[0][i].wait_recv()
            total += self.land_a[0, i].astype(F32)
        self.hold_far[...] = total.astype(BF16)
        self.last = self.send(self.hold_far, self.land_far, 4, p.cross)

    def late(self):
        p = self.place
        self.b_direct = []
        for i, way in enumerate((DOWN, UP)):
            half = -way
            part = self.within("b", half)
            self.across[1 + i].wait_recv()
            total = self.mine(p.z, p.side(way), "b") + self.far_b[1 + i].astype(F32)
            self.b_relay[half].wait_recv()
            self.hold_b[i] = total.astype(BF16)
            self.hold_b[i, :, part] = (
                total[:, part] + self.relay_b[:, part].astype(F32)
            ).astype(BF16)
            self.b_direct.append(
                self.send(
                    self.hold_b.at[i], self.land_b.at[i], 15 + i, p.z * RING + p.side(way)
                )
            )

    def end(self):
        p = self.place
        total = self.mine(p.z, p.y, "a")
        for i, way in enumerate((DOWN, UP)):
            self.a_direct[1][way].wait_recv()
            self.a_other[1][i].wait_recv()
            total += self.land_a[1, i].astype(F32)
        self.across[3].wait_recv()
        rest = self.mine(p.z, p.y, "b") + self.far_b[3].astype(F32)
        for i in range(2):
            self.b_direct[i].wait_recv()
            rest += self.land_b[i].astype(F32)
        self.out[:, self.cut :] = rest
        self.last.wait_recv()
        self.out[:, : self.cut] = total + self.land_far[...].astype(F32)
        for copy in self.sent:
            copy.wait_send()


def feed_kernel(
    span,
    lengths,
    mixed_ref,
    s_out,
    gain,
    s_gu,
    s_down,
    n2_gu,
    b_gu_raw,
    t_gu,
    t_down,
    b_down,
    b_out,
    at_out,
    av_out,
    av_down,
    x_hbm,
    cot_hbm,
    vout_hbm,
    vgu_hbm,
    vdown_hbm,
    h1_ref,
    dh1_ref,
    dmix_ref,
    pack,
    ffn_hbm,
    ffn_ref,
    vout,
    vgu,
    vdown,
    dys,
    xn2,
    part,
    dhid,
    hid,
    dgu,
    x_own,
    mixed_own,
    dmix_own,
    attn,
    sum_own,
    b_gu,
    at_down,
    local_sems,
    swap_s,
    swap_r,
    back_s,
    back_r,
    gather_s,
    gather_r,
    *scatter_scratch,
):
    tokens, width = xn2.shape
    chunk = tokens // PARTS
    block = tokens // 2
    cols = mixed_ref.shape[1]
    hpad = hid.shape[1]
    tile = 256
    p = Place()
    own = rows_of(p.me, chunk)
    loads = []
    for i, (src, dst) in enumerate(
        [
            (x_hbm.at[own], x_own),
            (vout_hbm, vout),
            (cot_hbm, dys),
            (vdown_hbm, vdown),
            (vgu_hbm, vgu),
        ]
    ):
        loads.append(pltpu.make_async_copy(src, dst, local_sems.at[i]))
        loads[-1].start()
    p.greet()

    my_cols = rows_of(p.me, cols)
    swaps = []
    for step in range(1, PARTS):
        to = lax.rem(p.me + step, PARTS)
        swaps.append(
            p.send(
                mixed_ref.at[rows_of(to, chunk)],
                mixed_own.at[:, my_cols],
                (swap_s, swap_r),
                step - 1,
                to,
            )
        )
    mixed_own[:, my_cols] = mixed_ref[own, :]

    hidden = t_down.shape[1]
    b_gu[...] = jnp.zeros_like(b_gu)
    at_down[...] = jnp.zeros_like(at_down)
    for k in range(2):
        b_gu[:, k * hpad : k * hpad + hidden] = b_gu_raw[k].astype(BF16)
    at_down[:, :hidden] = t_down[...].astype(BF16)
    def back_hidden(half):
        rows = slice(half * block, (half + 1) * block)

        @pl.loop(0, hpad // tile)
        def _(n):
            units = rows_of(n, tile)
            dhid[rows, units] = nt(dys[rows, :], vdown[units, :]).astype(BF16)


    for copy in swaps:
        copy.wait_recv()
    loads[0].wait()
    loads[1].wait()

    @pl.loop(0, width // 512)
    def _(n):
        part_cols = rows_of(n, 512)
        attn[:, part_cols] = nn(mixed_own[...], vout[:, part_cols]) * s_out[:, part_cols]

    h1_ref[...] = x_own[...].astype(F32) + attn[...]
    inv2 = lax.rsqrt(jnp.mean(h1_ref[...] * h1_ref[...], axis=-1, keepdims=True) + EPS)
    xn2[own, :] = (h1_ref[...] * inv2 * gain[...]).astype(BF16)
    gather = Gather(p, xn2, chunk, (gather_s, gather_r), EVEN)
    gather.start()
    own_rows = slice(COMMON_FEED, COMMON_FEED + RANK)
    fold_rows = slice(COMMON_FEED + RANK, COMMON_FEED + OWN_FEED)
    e_row = slice(COMMON_FEED + RANK, COMMON_FEED + RANK + 1)
    e_first = width - 2 * hpad
    pack[...] = jnp.zeros_like(pack)
    at = 5 * RANK
    for piece in (av_out, av_down):
        pack[at : at + RANK, :] = piece[...]
        at += RANK
    loads[2].wait()
    loads[3].wait()
    seq = lax.axis_index("seq")

    @pl.loop(0, PARTS)
    def _(i):
        rows = rows_of(i, chunk)
        base = lax.rem(i * chunk, span)
        length = lengths[0]
        for r in range(1, tokens // span):
            length = jnp.where(i * chunk >= r * span, lengths[r], length)
        pos = seq * span + base + lax.broadcasted_iota(jnp.int32, (chunk, 1), 0)
        live = (pos < length).astype(F32)
        dys[rows, :] = (dys[rows, :].astype(F32) * live * s_down[...]).astype(BF16)

    back_hidden(0)
    back_hidden(1)
    loads[4].wait()

    def hidden_units(plane):
        rows = rows_of(plane, block)

        @pl.loop(0, hpad // tile)
        def _(n):
            at_gate = rows_of(n, tile)
            at_up = rows_of(n + hpad // tile, tile)
            of_gate = rows_of(n + e_first // tile, tile)
            of_up = rows_of(n + (e_first + hpad) // tile, tile)
            gate = nt(xn2[rows, :], vgu[at_gate, :]) * s_gu[:, at_gate]
            up = nt(xn2[rows, :], vgu[at_up, :]) * s_gu[:, at_up]
            sigma = jax.nn.sigmoid(gate)
            active = gate * sigma
            hid[rows, at_gate] = (active * up).astype(BF16)
            back = dhid[rows, at_gate].astype(F32)
            grad_gate = back * up * sigma * (1.0 + gate * (1.0 - sigma))
            grad_up = back * active
            pack[e_row, of_gate] += jnp.sum(grad_gate * gate, axis=0, keepdims=True)
            pack[e_row, of_up] += jnp.sum(grad_up * up, axis=0, keepdims=True)
            dgu[rows, at_gate] = (grad_gate * s_gu[:, at_gate]).astype(BF16)
            dgu[rows, at_up] = (grad_up * s_gu[:, at_up]).astype(BF16)

    def back_part(plane, first, last):
        rows = rows_of(plane, block)

        @pl.loop(first // 512, last // 512)
        def _(n):
            part_cols = rows_of(n, 512)
            part[rows, part_cols] = nn(dgu[rows, :], vgu[:, part_cols]).astype(BF16)

    scatter = Scatter(p, part, sum_own, chunk, EVEN, scatter_scratch)
    gather.first()
    gather.middle()
    hidden_units(p.z)
    gather.late()
    back_part(p.z, 0, width)
    scatter.start_a(1)
    scatter.start_other(1)
    gather.end()
    hidden_units(p.far)
    back_part(p.far, 1024, width)
    scatter.start_b()
    back_part(p.far, 0, 1024)
    scatter.start_a(0)
    scatter.start_other(0)

    def forward_part(half):
        rows = slice(half * block, (half + 1) * block)

        @pl.loop(0, width // 512)
        def _(n):
            part_cols = rows_of(n, 512)
            ffn_ref[rows, part_cols] = nn(hid[rows, :], vdown[:, part_cols]).astype(BF16)

    t_one = []
    for k in range(2):
        part_cols = slice(k * hpad, (k + 1) * hpad)
        t_one.append(nt(b_gu[:, part_cols], dgu[:, part_cols]).astype(BF16))
    t_one = jnp.concatenate(t_one, axis=0)
    left_gu = t_gu[...].astype(BF16)
    x_gu = nt(left_gu, xn2[...]).astype(BF16)
    scatter.first()
    ratio = pack[e_row, e_first:] / n2_gu[...]
    back_gu = (b_gu[...].astype(F32) * ratio).astype(BF16)
    for n in range(0, width, 512):
        at = slice(n, n + 512)
        first = nn(t_one, xn2[:, at])
        for k in range(2):
            units = slice(k * hpad, (k + 1) * hpad)
            pack[k * RANK : (k + 1) * RANK, at] = first[k * RANK : (k + 1) * RANK] - nn(
                back_gu[:, units], vgu[units, at]
            )
    forward_part(0)
    forward_part(1)
    store = pltpu.make_async_copy(ffn_ref, ffn_hbm, local_sems.at[6])
    store.start()
    scatter.middle()
    scatter.late()
    for k in range(2):
        part_cols = slice(k * hpad, (k + 1) * hpad)
        both = slice(k * RANK, (k + 1) * RANK)
        pack[own_rows, part_cols] = (
            nn(x_gu[both], dgu[:, part_cols])
            - nt(left_gu[both], vgu[part_cols, :]) * ratio[:, part_cols]
        )
    back_down = nt(b_down[...].astype(BF16), dys[...]).astype(BF16)
    ga_down = nn(back_down, hid[...])
    fits = width - 2 * hpad
    pack[own_rows, 2 * hpad :] = ga_down[:, :fits]
    pack[fold_rows, : hpad - fits] = ga_down[:, fits:]
    x_down = nt(at_down[...], hid[...]).astype(BF16)
    for n in range(0, width, 512):
        pack[3 * RANK : 4 * RANK, n : n + 512] = nn(x_down, dys[:, n : n + 512])
    scatter.end()

    length = lengths[0]
    for r in range(1, tokens // span):
        length = jnp.where(p.me * chunk >= r * span, lengths[r], length)
    pos = seq * span + lax.rem(p.me * chunk, span) + lax.broadcasted_iota(jnp.int32, (chunk, 1), 0)
    live = (pos < length).astype(F32)
    dy_copy = pltpu.make_async_copy(cot_hbm.at[own], x_own, local_sems.at[5])
    dy_copy.start()
    scaled = sum_own[...] * gain[...]
    h1 = h1_ref[...]
    mean = jnp.mean(scaled * h1, axis=-1, keepdims=True)
    dy_copy.wait()
    grad = x_own[...].astype(F32) * live + inv2 * (scaled - h1 * (inv2 * inv2 * mean))
    dh1_ref[...] = grad
    low = grad.astype(BF16).astype(F32)
    pack[7 * RANK : 7 * RANK + 1, :] = jnp.sum(low * attn[...], axis=0, keepdims=True)
    das = (low * s_out[...]).astype(BF16)

    @pl.loop(0, width // 512)
    def _(n):
        part_cols = rows_of(n, 512)
        dmix_own[:, part_cols] = nt(das, vout[part_cols, :]).astype(BF16)

    backs = []
    for step in range(1, PARTS):
        to = lax.rem(p.me + step, PARTS)
        backs.append(
            p.send(
                dmix_own.at[:, rows_of(to, cols)],
                dmix_ref.at[own],
                (back_s, back_r),
                step - 1,
                to,
            )
        )
    dmix_ref[own, :] = dmix_own[:, my_cols]
    t_out = nt(b_out[...].astype(BF16), das).astype(BF16)
    pack[4 * RANK : 5 * RANK, :] = nn(t_out, mixed_own[...])
    x_out = nt(at_out[...], mixed_own[...]).astype(BF16)
    pack[2 * RANK : 3 * RANK, :] = nn(x_out, das)
    for copy in backs:
        copy.wait_recv()
    for copy in swaps + backs:
        copy.wait_send()
    store.wait()


def feed(span, lengths, mixed, *rest):
    tokens, cols = mixed.shape
    hpad, width = rest[-1].shape
    chunk = tokens // PARTS
    shape = jax.ShapeDtypeStruct
    out_shape = (
        shape((chunk, width), F32),
        shape((chunk, width), F32),
        shape((tokens, cols), BF16),
        shape((COMMON_FEED + OWN_FEED, width), F32),
        shape((tokens, width), BF16),
    )
    dma = pltpu.SemaphoreType.DMA
    scratch = [
        pltpu.VMEM((tokens, width), BF16),
        pltpu.VMEM((width, width), BF16),
        pltpu.VMEM((2 * hpad, width), BF16),
        pltpu.VMEM((hpad, width), BF16),
        pltpu.VMEM((tokens, width), BF16),
        pltpu.VMEM((tokens, width), BF16),
        pltpu.VMEM((tokens, width), BF16),
        pltpu.VMEM((tokens, hpad), BF16),
        pltpu.VMEM((tokens, hpad), BF16),
        pltpu.VMEM((tokens, 2 * hpad), BF16),
        pltpu.VMEM((chunk, width), BF16),
        pltpu.VMEM((chunk, width), BF16),
        pltpu.VMEM((chunk, width), BF16),
        pltpu.VMEM((chunk, width), F32),
        pltpu.VMEM((chunk, width), F32),
        pltpu.VMEM((RANK, 2 * hpad), BF16),
        pltpu.VMEM((RANK, hpad), BF16),
        dma((7,)),
        dma((PARTS - 1,)),
        dma((PARTS - 1,)),
        dma((PARTS - 1,)),
        dma((PARTS - 1,)),
        dma((GATHER_SEMS,)),
        dma((GATHER_SEMS,)),
    ]
    scratch += Scatter.scratch(chunk, width, EVEN)
    anywhere = pl.BlockSpec(memory_space=pl.ANY)
    return pl.pallas_call(
        functools.partial(feed_kernel, span),
        out_shape=out_shape,
        in_specs=[pl.BlockSpec(memory_space=pltpu.SMEM)] + [VMEM] * 14 + [anywhere] * 5,
        out_specs=[VMEM] * 4 + [anywhere],
        scratch_shapes=scratch,
        compiler_params=pltpu.CompilerParams(
            collective_id=1, has_side_effects=True, vmem_limit_bytes=ROOM
        ),
    )(lengths, mixed, *rest)


def turn(values, cosines, sines):
    return values * cosines + pltpu.roll(values, HD // 2, 1) * sines


def scores_of(q, keys, query_pos, key_pos, first, length):
    scores = nt(q, keys) * HD ** (-0.5)
    at = key_pos + first
    return jnp.where((at <= query_pos) & (at < length), scores, MASKED)


def back_kernel(
    rows,
    lengths,
    cosines,
    sines,
    s_qkv,
    s_down,
    q_hbm,
    mixed_hbm,
    lse_hbm,
    dmix_hbm,
    kept_hbm,
    h1_hbm,
    cot_hbm,
    kv_hbm,
    ffn_hbm,
    dqkv_ref,
    e_qkv,
    out_ref,
    e_down,
    gather_s,
    gather_r,
    q_ref,
    mixed_ref,
    lse_ref,
    dmix_ref,
    kept_ref,
    h1_ref,
    kv_ref,
    ffn_ref,
    dkv,
    sib_far,
    hold,
    far,
    sib,
    dq,
    inner,
    total_own,
    dy_own,
    local_sems,
    send_sems,
    recv_sems,
    *scratch,
):
    tokens, cols = q_ref.shape
    span = tokens // rows
    heads = cols // HD
    chunk = tokens // PARTS
    p = Place()
    core = lax.rem(p.seq, 2)
    upper = p.seq // 2
    sibling = upper * 2 + 1 - core
    loads = []
    for i, (src, dst) in enumerate(
        [
            (ffn_hbm, ffn_ref),
            (kv_hbm, kv_ref),
            (q_hbm, q_ref),
            (dmix_hbm, dmix_ref),
            (mixed_hbm, mixed_ref),
            (lse_hbm, lse_ref),
            (kept_hbm, kept_ref),
            (h1_hbm, h1_ref),
            (cot_hbm.at[rows_of(p.me, chunk)], dy_own),
        ]
    ):
        loads.append(pltpu.make_async_copy(src, dst, local_sems.at[i]))
        loads[-1].start()
    barrier = pltpu.get_barrier_semaphore()
    for step in range(1, PARTS):
        place = p.at(lax.rem(p.me + step, PARTS))
        pl.semaphore_signal(barrier, inc=1, device_id=place, device_id_type=MESH)
    for seq in (sibling, (1 - upper) * 2 + core):
        pl.semaphore_signal(barrier, inc=1, device_id=(p.row, seq, p.me), device_id_type=MESH)
    e_qkv[...] = jnp.zeros_like(e_qkv)
    dq[...] = jnp.zeros_like(dq)
    pl.semaphore_wait(barrier, PARTS + 1)
    loads[0].wait()
    scatter = Scatter(p, ffn_ref, total_own, chunk, RING_FIRST, scratch)
    scatter.start_b()
    scatter.start_a(0)
    scatter.start_a(1)

    def over(source, target, index, seq):
        return pltpu.make_async_remote_copy(
            src_ref=source,
            dst_ref=target,
            send_sem=send_sems.at[index],
            recv_sem=recv_sems.at[index],
            device_id=(p.row, seq, p.me),
            device_id_type=MESH,
        )

    to_sib_far = []
    to_sib = []
    to_far = []
    for r in range(rows):
        part = slice(r * span, (r + 1) * span)
        to_sib_far.append(over(dkv.at[1 - core, part], sib_far.at[part], r, sibling))
        to_sib.append(over(dkv.at[upper * 2, part], sib.at[part], rows + r, sibling))
        to_far.append(over(hold.at[part], far.at[part], 2 * rows + r, core))

    for load in loads[1:7]:
        load.wait()
    query_pos = p.seq * span + lax.broadcasted_iota(jnp.int32, (span, span), 0)
    key_pos = lax.broadcasted_iota(jnp.int32, (span, span), 1)

    for r in range(rows):
        part = slice(r * span, (r + 1) * span)
        for head in range(heads):
            at = slice(head * HD, (head + 1) * HD)
            i = r * heads + head
            inner[:, i : i + 1] = jnp.sum(
                dmix_ref[part, at].astype(F32) * mixed_ref[part, at].astype(F32),
                axis=-1,
                keepdims=True,
            )

    def blocks(r, head, first, last):
        part = slice(r * span, (r + 1) * span)
        kcols = slice(head * HD, (head + 1) * HD)
        vcols = slice(cols + head * HD, cols + (head + 1) * HD)
        i = r * heads + head

        @pl.loop(first, last)
        def _(j):
            q = q_ref[part, kcols]
            do = dmix_ref[part, kcols]
            lse = lse_ref[part, head * HD : head * HD + 1]
            scores = scores_of(q, kv_ref[j, part, kcols], query_pos, key_pos, j * span, lengths[r])
            probs = jnp.exp(scores - lse)
            dkv[j, part, vcols] = tn(probs.astype(BF16), do).astype(BF16)
            grad = (probs * (nt(do, kv_ref[j, part, vcols]) - inner[:, i : i + 1])).astype(BF16)
            dq[part, kcols] += nn(grad, kv_ref[j, part, kcols])
            dkv[j, part, kcols] = (tn(grad, q) * HD ** (-0.5)).astype(BF16)

    def onward(r):
        part = slice(r * span, (r + 1) * span)

        @pl.when(upper == 1)
        def _():
            to_sib_far[r].wait_recv()
            hold[part] = (dkv[core, part].astype(F32) + sib_far[part].astype(F32)).astype(BF16)
            to_far[r].start()

    def emit(part, at, grad):
        held = kept_ref[part, at].astype(F32)
        e_qkv[:, at] += jnp.sum(grad * held, axis=0, keepdims=True)
        dqkv_ref[part, at] = (grad * s_qkv[:, at]).astype(BF16)

    def results():
        loads[7].wait()
        loads[8].wait()
        length = lengths[0]
        for r in range(1, rows):
            length = jnp.where(p.me * chunk >= r * span, lengths[r], length)
        first = p.seq * span + lax.rem(p.me * chunk, span)
        pos = first + lax.broadcasted_iota(jnp.int32, (chunk, 1), 0)
        live = (pos < length).astype(F32)
        ffn = total_own[...] * s_down[...]
        out_ref[rows_of(p.me, chunk), :] = ((h1_ref[...] + ffn) * live).astype(BF16)
        e_down[...] = jnp.sum(dy_own[...].astype(F32) * live * ffn, axis=0, keepdims=True)

    for r in range(rows):
        for head in range(heads):
            blocks(r, head, 0, 2 * upper)

        @pl.when(upper == 1)
        def _(r=r):
            to_sib_far[r].start()

        if r == 0:
            scatter.first()
            scatter.start_other(0)
            scatter.start_other(1)
        else:
            onward(r - 1)
    for r in range(rows):
        for head in range(heads):
            blocks(r, head, 2 * upper, p.seq + 1)
            if r == 0 and head == 0:
                scatter.middle()
                scatter.late()
                onward(rows - 1)
            if r == 1 and head == 0:
                scatter.end()
                results()
                gather = Gather(p, out_ref, chunk, (gather_s, gather_r), RING_FIRST)
                gather.start()

        @pl.when(core == 1)
        def _(r=r):
            to_sib[r].start()

    gather.first()
    for r in range(rows):
        part = slice(r * span, (r + 1) * span)
        for head in range(heads):
            at = slice(head * HD, (head + 1) * HD)
            emit(part, at, turn(dq[part, at] * HD ** (-0.5), cosines[...], -sines[...]))
    gather.middle()

    for r in range(rows):
        part = slice(r * span, (r + 1) * span)

        @pl.when(core == 0)
        def _(r=r):
            to_sib[r].wait_recv()

        @pl.when(upper == 0)
        def _(r=r):
            to_far[r].wait_recv()

        for head in range(2 * heads):
            at = slice(head * HD, (head + 1) * HD)
            grad = dkv[p.seq, part, at].astype(F32)
            grad = grad + jnp.where(core == 0, sib[part, at].astype(F32), 0.0)
            grad = grad + jnp.where(upper == 0, far[part, at].astype(F32), 0.0)
            if head < heads:
                grad = turn(grad, cosines[...], -sines[...])
            emit(part, slice(cols + head * HD, cols + (head + 1) * HD), grad)
        if r == 0:
            gather.late()
    gather.end()

    for r in range(rows):

        @pl.when(upper == 1)
        def _(r=r):
            to_sib_far[r].wait_send()
            to_far[r].wait_send()

        @pl.when(core == 1)
        def _(r=r):
            to_sib[r].wait_send()


def back(rows, lengths, *rest):
    q, mixed, lse, dmix, kept, h1, _, kv, ffn = rest[-9:]
    tokens, cols = q.shape
    width = ffn.shape[1]
    chunk = tokens // PARTS
    shape = jax.ShapeDtypeStruct
    dma = pltpu.SemaphoreType.DMA
    out_shape = (
        shape((tokens, 3 * cols), BF16),
        shape((1, 3 * cols), F32),
        shape((tokens, width), BF16),
        shape((1, width), F32),
    )
    scratch = [
        dma((GATHER_SEMS,)),
        dma((GATHER_SEMS,)),
        pltpu.VMEM(q.shape, BF16),
        pltpu.VMEM(mixed.shape, BF16),
        pltpu.VMEM(lse.shape, F32),
        pltpu.VMEM(dmix.shape, BF16),
        pltpu.VMEM(kept.shape, BF16),
        pltpu.VMEM(h1.shape, F32),
        pltpu.VMEM(kv.shape, BF16),
        pltpu.VMEM(ffn.shape, BF16),
        pltpu.VMEM(kv.shape, BF16),
        pltpu.VMEM((tokens, 2 * cols), BF16),
        pltpu.VMEM((tokens, 2 * cols), BF16),
        pltpu.VMEM((tokens, 2 * cols), BF16),
        pltpu.VMEM((tokens, 2 * cols), BF16),
        pltpu.VMEM((tokens, cols), F32),
        pltpu.VMEM((tokens // rows, rows * cols // HD), F32),
        pltpu.VMEM((chunk, width), F32),
        pltpu.VMEM((chunk, width), BF16),
        dma((9,)),
        dma((3 * rows,)),
        dma((3 * rows,)),
    ]
    scratch += Scatter.scratch(chunk, width, RING_FIRST)
    return pl.pallas_call(
        functools.partial(back_kernel, rows),
        out_shape=out_shape,
        in_specs=[pl.BlockSpec(memory_space=pltpu.SMEM)]
        + [VMEM] * 4
        + [pl.BlockSpec(memory_space=pl.ANY)] * 9,
        out_specs=[VMEM] * len(out_shape),
        scratch_shapes=scratch,
        compiler_params=pltpu.CompilerParams(
            collective_id=2, has_side_effects=True, vmem_limit_bytes=ROOM
        ),
    )(lengths, *rest)


COMMON_FEED, OWN_FEED = 128, 32
COMMON_QKV, OWN_QKV = 48, 16


class Total:
    def __init__(self, place, common, scratch):
        self.p = p = place
        self.common = common
        (
            self.send_buf,
            self.land_row,
            self.by_row,
            self.land_seq,
            self.mine,
            self.across,
            self.held,
            *self.sems,
        ) = scratch
        self.rows = [(lax.rem(p.row + step, RING), p.seq, p.me) for step in range(1, RING)]
        self.seqs = [(p.row, lax.rem(p.seq + step, RING), p.me) for step in range(1, RING)]
        self.heads = [p.at(lax.rem(p.me + step, PARTS)) for step in range(1, PARTS)]

    @staticmethod
    def scratch(common, own):
        dma = pltpu.SemaphoreType.DMA
        piece = (common + own, 128)
        return [
            pltpu.VMEM((RING * RING, *piece), BF16),
            pltpu.VMEM((RING - 1, RING, *piece), BF16),
            pltpu.VMEM((RING, *piece), BF16),
            pltpu.VMEM((RING - 1, *piece), BF16),
            pltpu.VMEM(piece, BF16),
            pltpu.VMEM((PARTS - 1, common, 128), BF16),
            pltpu.VMEM((RING * RING, *piece), BF16),
        ] + [dma((n,)) for n in (3, 3, 3, 3, PARTS - 1, PARTS - 1, 3, 3, 3, 3)]

    def greet(self):
        barrier = pltpu.get_barrier_semaphore()
        for place in self.rows + self.seqs + self.heads:
            pl.semaphore_signal(barrier, inc=1, device_id=place, device_id_type=MESH)
        pl.semaphore_wait(barrier, 2 * (RING - 1) + PARTS - 1)

    def fill(self, rows, source):
        for piece in range(RING * RING):
            self.send_buf[piece, rows] = source[:, piece * 128 : (piece + 1) * 128].astype(BF16)

    def copies(self, source, target, ends, stage):
        made = []
        for step, place in enumerate(ends):
            made.append(
                pltpu.make_async_remote_copy(
                    src_ref=source(place),
                    dst_ref=target(step),
                    send_sem=self.sems[2 * stage].at[step],
                    recv_sem=self.sems[2 * stage + 1].at[step],
                    device_id=place,
                    device_id_type=MESH,
                )
            )
            made[-1].start()
        return made

    def start(self):
        self.wait = self.copies(
            lambda place: self.send_buf.at[rows_of(place[0], RING)],
            lambda step: self.land_row.at[step],
            self.rows,
            0,
        )

    def second(self):
        for copy in self.wait:
            copy.wait()
        for q in range(RING):
            total = self.send_buf[self.p.row * RING + q].astype(F32)
            for step in range(RING - 1):
                total += self.land_row[step, q].astype(F32)
            self.by_row[q] = total.astype(BF16)
        self.wait = self.copies(
            lambda place: self.by_row.at[place[1]], lambda step: self.land_seq.at[step], self.seqs, 1
        )

    def third(self):
        for copy in self.wait:
            copy.wait()
        total = self.by_row[self.p.seq].astype(F32)
        for step in range(RING - 1):
            total += self.land_seq[step].astype(F32)
        self.mine[...] = total.astype(BF16)
        self.wait = self.copies(
            lambda place: self.mine.at[: self.common],
            lambda step: self.across.at[step],
            self.heads,
            2,
        )

    def fourth(self):
        for copy in self.wait:
            copy.wait()
        shared = self.mine[: self.common].astype(F32)
        for step in range(PARTS - 1):
            shared += self.across[step].astype(F32)
        here = self.p.row * RING + self.p.seq
        self.held[here, : self.common] = shared.astype(BF16)
        self.held[here, self.common :] = self.mine[self.common :]
        view = self.held.at[here]
        self.wait = self.copies(lambda place: view, lambda step: view, self.seqs, 3)

    def fifth(self):
        for copy in self.wait:
            copy.wait()
        view = self.held.at[rows_of(self.p.row, RING)]
        self.wait = self.copies(lambda place: view, lambda step: view, self.rows, 4)

    def end(self, out):
        for copy in self.wait:
            copy.wait()
        for piece in range(RING * RING):
            out[:, piece * 128 : (piece + 1) * 128] = self.held[piece].astype(F32)


def close_kernel(
    cols,
    dqkv_hbm,
    vqkv_hbm,
    xn1_hbm,
    x_hbm,
    dh1_hbm,
    pack_hbm,
    gain,
    b_raw,
    t_raw,
    e_qkv,
    n2_qkv,
    e_down,
    gx_ref,
    sum_feed,
    sum_qkv,
    part,
    pack,
    dqkv_ref,
    vqkv,
    dh1_ref,
    pack_feed,
    xn1,
    x_own,
    total_own,
    b_qkv,
    local_sems,
    gather_s,
    gather_r,
    *scratch,
):
    tokens, width = xn1_hbm.shape
    chunk = tokens // PARTS
    p = Place()
    own = rows_of(p.me, chunk)
    totals = Total(p, COMMON_QKV, scratch[:17])
    early = Total(p, COMMON_FEED, scratch[17:34])
    loads = []
    for i, (src, dst) in enumerate(
        [
            (dqkv_hbm, dqkv_ref),
            (vqkv_hbm, vqkv),
            (pack_hbm, pack_feed),
            (xn1_hbm, xn1),
            (x_hbm.at[own], x_own),
            (dh1_hbm, dh1_ref),
        ]
    ):
        loads.append(pltpu.make_async_copy(src, dst, local_sems.at[i]))
        loads[-1].start()
    totals.greet()
    loads[0].wait()
    loads[1].wait()

    def back_part(first, last):
        @pl.loop(first // 256, last // 256)
        def _(n):
            at = rows_of(n, 256)
            part[:, at] = nt(dqkv_ref[...], vqkv[at, :]).astype(BF16)

    scatter = Scatter(p, part, total_own, chunk, EVEN, scratch[34:])
    back_part(1024, width)
    scatter.start_b()
    back_part(0, 1024)
    scatter.start_a(0)
    scatter.start_a(1)
    scatter.start_other(0)
    scatter.start_other(1)
    loads[2].wait()
    early.fill(slice(None), pack_feed)
    row = 7 * RANK + 1
    early.fill(slice(row, row + 1), e_down)
    early.start()

    b_qkv[...] = jnp.zeros_like(b_qkv)
    for k in range(3):
        b_qkv[k * RANK : (k + 1) * RANK, k * cols : (k + 1) * cols] = b_raw[k].astype(BF16)
    t_qkv = t_raw[...].astype(BF16)
    ratio = e_qkv[...] / n2_qkv[...]
    back_qkv = (b_qkv[...].astype(F32) * ratio).astype(BF16)
    t_one = nt(b_qkv[...], dqkv_ref[...]).astype(BF16)
    loads[3].wait()
    t_two = nt(t_qkv, xn1[...]).astype(BF16)
    scatter.first()
    early.second()
    for n in range(0, width, 512):
        at = slice(n, n + 512)
        pack[: 3 * RANK, at] = nn(t_one, xn1[:, at]) - nt(back_qkv, vqkv[at, :])
        if n == width // 2:
            scatter.middle()
    gb = nn(t_two, dqkv_ref[...]) - nn(t_qkv, vqkv[...]) * ratio
    pack[COMMON_QKV:, :] = jnp.zeros((OWN_QKV, width), F32)
    for k in range(3):
        pack[COMMON_QKV:, k * cols : (k + 1) * cols] = gb[
            k * RANK : (k + 1) * RANK, k * cols : (k + 1) * cols
        ]
    pack[COMMON_QKV : COMMON_QKV + 1, 3 * cols : 6 * cols] = e_qkv[...]
    totals.fill(slice(None), pack)
    totals.start()
    scatter.late()
    early.third()
    loads[4].wait()
    loads[5].wait()
    x = x_own[...].astype(F32)
    inv1 = lax.rsqrt(jnp.mean(x * x, axis=-1, keepdims=True) + EPS)
    scatter.end()
    scaled = total_own[...] * gain[...]
    mean = jnp.mean(scaled * x, axis=-1, keepdims=True)
    grad = dh1_ref[...] + inv1 * (scaled - x * (inv1 * inv1 * mean))
    gx_ref[own, :] = grad.astype(BF16)
    gather = Gather(p, gx_ref, chunk, (gather_s, gather_r), EVEN)
    gather.start()
    totals.second()
    early.fourth()
    gather.first()
    totals.third()
    early.fifth()
    gather.middle()
    totals.fourth()
    gather.late()
    totals.fifth()
    early.end(sum_feed)
    gather.end()
    totals.end(sum_qkv)


def close(cols, dqkv, vqkv, xn1, x, dh1, pack, *rest):
    tokens, width = xn1.shape
    chunk = tokens // PARTS
    shape = jax.ShapeDtypeStruct
    dma = pltpu.SemaphoreType.DMA
    out_shape = (
        shape((tokens, width), BF16),
        shape((COMMON_FEED + OWN_FEED, width), F32),
        shape((COMMON_QKV + OWN_QKV, width), F32),
    )
    scratch = [
        pltpu.VMEM((tokens, width), BF16),
        pltpu.VMEM((COMMON_QKV + OWN_QKV, width), F32),
        pltpu.VMEM(dqkv.shape, BF16),
        pltpu.VMEM(vqkv.shape, BF16),
        pltpu.VMEM(dh1.shape, F32),
        pltpu.VMEM(pack.shape, F32),
        pltpu.VMEM((tokens, width), BF16),
        pltpu.VMEM((chunk, width), BF16),
        pltpu.VMEM((chunk, width), F32),
        pltpu.VMEM((3 * RANK, 3 * cols), BF16),
        dma((6,)),
        dma((GATHER_SEMS,)),
        dma((GATHER_SEMS,)),
    ]
    scratch += Total.scratch(COMMON_QKV, OWN_QKV) + Total.scratch(COMMON_FEED, OWN_FEED)
    scratch += Scatter.scratch(chunk, width, EVEN)
    return pl.pallas_call(
        functools.partial(close_kernel, cols),
        out_shape=out_shape,
        in_specs=[pl.BlockSpec(memory_space=pl.ANY)] * 6 + [VMEM] * len(rest),
        out_specs=[VMEM] * 3,
        scratch_shapes=scratch,
        compiler_params=pltpu.CompilerParams(
            collective_id=3, has_side_effects=True, vmem_limit_bytes=ROOM
        ),
    )(dqkv, vqkv, xn1, x, dh1, pack, *rest)


def three_terms(left, right):
    def split(a):
        high = a.astype(BF16)
        return high, (a - high.astype(F32)).astype(BF16)

    left_high, left_low = split(left)
    right_high, right_low = split(right)
    return (
        jnp.concatenate([left_high, left_low, left_high], axis=0),
        jnp.concatenate([right_high, right_high, right_low], axis=0),
    )


def front_kernel(
    rows,
    spread,
    lengths,
    gain,
    m_qkv,
    m_out,
    m_gu,
    m_down,
    t_qkv,
    b_qkv,
    t_out,
    b_out,
    t_gu,
    b_gu,
    t_down,
    b_down,
    cosines,
    sines,
    x_hbm,
    wqkv_hbm,
    wout_hbm,
    wgu_hbm,
    wdown_hbm,
    q_ref,
    kept_ref,
    mixed_ref,
    lse_ref,
    n2_qkv,
    n2_gu,
    n2_model,
    s_qkv,
    s_gu,
    s_out,
    s_down,
    at_out,
    av_out,
    av_down,
    xn1_hbm,
    vqkv_hbm,
    vout_hbm,
    vgu_hbm,
    vdown_hbm,
    kv_hbm,
    x_ref,
    wqkv,
    wout,
    wgu,
    wdown,
    xn1,
    vqkv,
    vfull,
    vgu,
    vdown,
    kv,
    acc,
    top,
    weight,
    squares,
    land_squares,
    at_mine,
    load_sems,
    store_sems,
    gather_s,
    gather_r,
    share_s,
    share_r,
    kv_s,
    kv_r,
    square_s,
    square_r,
    at_s,
    at_r,
):
    tokens, width = x_ref.shape
    span = tokens // rows
    cols = q_ref.shape[1]
    heads = cols // HD
    hidden = wdown.shape[0]
    hpad = vdown.shape[0]
    p = Place()
    core = lax.rem(p.seq, 2)
    upper = p.seq // 2
    sibling = upper * 2 + 1 - core
    loads = []
    pairs = [(wout_hbm, wout), (wqkv_hbm, wqkv), (x_hbm, x_ref), (wdown_hbm, wdown), (wgu_hbm, wgu)]
    for i, (src, dst) in enumerate(pairs):
        loads.append(pltpu.make_async_copy(src, dst, load_sems.at[i]))
        loads[-1].start()
    barrier = pltpu.get_barrier_semaphore()
    for step in range(1, PARTS):
        place = p.at(lax.rem(p.me + step, PARTS))
        pl.semaphore_signal(barrier, inc=1, device_id=place, device_id_type=MESH)
    for seq in (sibling, (1 - upper) * 2 + core):
        pl.semaphore_signal(barrier, inc=1, device_id=(p.row, seq, p.me), device_id_type=MESH)

    left, right = three_terms(t_out[...], b_out[...])
    my_cols = rows_of(p.me, cols)
    loads[0].wait()
    squares[...] = jnp.zeros_like(squares)
    for n in range(0, width, 512):
        at = slice(n, n + 512)
        v = wout[:, at].astype(F32) + SCALE * tn(left, right[:, at])
        vfull[my_cols, at] = v.astype(BF16)
        squares[0:1, at] = jnp.sum(v * v, axis=0, keepdims=True)
    at_mine[...] = t_out[...].astype(BF16)
    at_out[:, my_cols] = t_out[...].astype(BF16)
    pl.semaphore_wait(barrier, PARTS + 1)
    gather = Gather(p, vfull, cols // 2, (gather_s, gather_r), RING_MOST, cols, core)
    gather.start()
    at_copies = []
    for step in range(1, PARTS):
        to = lax.rem(p.me + step, PARTS)
        at_copies.append(p.send(at_mine, at_out.at[:, my_cols], (at_s, at_r), step - 1, to))

    loads[1].wait()

    def direct(k):
        left, right = three_terms(t_qkv[k], b_qkv[k])
        at = slice(k * cols, (k + 1) * cols)
        total = jnp.zeros((1, cols), F32)
        for n in range(0, width, 512):
            part = slice(n, n + 512)
            v = wqkv[k, part, :].astype(F32) + SCALE * tn(left[:, part], right)
            vqkv[part, at] = v.astype(BF16)
            total += jnp.sum(v * v, axis=0, keepdims=True)
        n2_qkv[:, at] = total
        s_qkv[:, at] = m_qkv[k : k + 1, :] * lax.rsqrt(total)

    def project(r, k):
        part = slice(r * span, (r + 1) * span)
        at = slice(k * cols, (k + 1) * cols)
        y = nn(xn1[part, :], vqkv[:, at]) * s_qkv[:, at]
        kept_ref[part, at] = y.astype(BF16)
        if k < 2:
            y = jnp.concatenate(
                [turn(y[:, h * HD : (h + 1) * HD], cosines[...], sines[...]) for h in range(heads)],
                axis=1,
            )
        if k == 0:
            q_ref[part, :] = y.astype(BF16)
        else:
            kv[p.seq, part, (k - 1) * cols : k * cols] = y.astype(BF16)

    def over(source, index, seq):
        return pltpu.make_async_remote_copy(
            src_ref=source,
            dst_ref=source,
            send_sem=kv_s.at[index],
            recv_sem=kv_r.at[index],
            device_id=(p.row, seq, p.me),
            device_id_type=MESH,
        )

    direct(1)
    direct(2)
    loads[2].wait()
    to_sib, to_far, onward = [], [], []
    for r in range(rows):
        part = slice(r * span, (r + 1) * span)
        to_sib.append(over(kv.at[p.seq, part], r, sibling))
        to_far.append(over(kv.at[p.seq, part], rows + r, 2 + core))
        onward.append(over(kv.at[core, part], 2 * rows + r, sibling))

        @pl.loop(0, span // 128)
        def _(i, r=r):
            piece = pl.ds(pl.multiple_of(r * span + i * 128, 128), 128)
            x = x_ref[piece, :].astype(F32)
            inv = lax.rsqrt(jnp.mean(x * x, axis=-1, keepdims=True) + EPS)
            xn1[piece, :] = (x * inv * gain[...]).astype(BF16)

        project(r, 1)
        project(r, 2)

        @pl.when(upper == 0)
        def _(r=r):
            to_far[r].start()

        @pl.when(core == 0)
        def _(r=r):
            to_sib[r].start()

    direct(0)
    for r in range(rows):
        project(r, 0)
    stores = [
        pltpu.make_async_copy(vqkv, vqkv_hbm, store_sems.at[1]),
        pltpu.make_async_copy(xn1, xn1_hbm, store_sems.at[2]),
    ]
    for copy in stores:
        copy.start()

    query_pos = p.seq * span + lax.broadcasted_iota(jnp.int32, (span, span), 0)
    key_pos = lax.broadcasted_iota(jnp.int32, (span, span), 1)

    def absorb(r, j, fresh=False):
        part = slice(r * span, (r + 1) * span)
        for head in range(heads):
            at = slice(head * HD, (head + 1) * HD)
            to = slice(cols + head * HD, cols + (head + 1) * HD)
            one = (slice(None), slice(r * heads + head, r * heads + head + 1))
            scores = scores_of(
                q_ref[part, at], kv[j, part, at], query_pos, key_pos, j * span, lengths[r]
            )
            best = jnp.max(scores, axis=-1, keepdims=True)
            if not fresh:
                best = jnp.maximum(best, top[one])
            expo = jnp.exp(scores - best)
            summed = jnp.sum(expo, axis=-1, keepdims=True)
            mixed = nn(expo.astype(BF16), kv[j, part, to])
            if not fresh:
                fade = jnp.exp(top[one] - best)
                summed += weight[one] * fade
                mixed += acc[part, at] * fade
            top[one] = best
            weight[one] = summed
            acc[part, at] = mixed

    gather.first()
    for r in range(rows):
        absorb(r, p.seq, True)
    gather.middle()

    loads[3].wait()
    vdown[hidden:, :] = jnp.zeros((hpad - hidden, width), BF16)
    left, right = three_terms(t_down[...], b_down[...])
    for n in range(0, width, 512):
        at = slice(n, n + 512)
        v = wdown[:, at].astype(F32) + SCALE * tn(left, right[:, at])
        vdown[:hidden, at] = v.astype(BF16)
        squares[1:2, at] = jnp.sum(v * v, axis=0, keepdims=True)
    square_copies = []
    for step in range(1, PARTS):
        to = lax.rem(p.me + step, PARTS)
        square_copies.append(
            p.send(squares, land_squares.at[step - 1], (square_s, square_r), step - 1, to)
        )
    stores.append(pltpu.make_async_copy(vdown, vdown_hbm, store_sems.at[3]))
    stores[-1].start()
    shares = []

    def share(plane, steps):
        for step in steps:
            view = gather.view(plane * RING + p.side(step))
            index = len(shares)
            shares.append(
                pltpu.make_async_remote_copy(
                    src_ref=view,
                    dst_ref=view,
                    send_sem=share_s.at[index],
                    recv_sem=share_r.at[index],
                    device_id=(p.row, sibling, p.me),
                    device_id_type=MESH,
                )
            )

            shares[-1].start()

    share(p.z, (1, 2, 3))

    loads[4].wait()
    ones = jnp.ones((8, width), BF16)
    for k in range(2):
        left, right = three_terms(b_gu[k], t_gu[k])
        base = k * hpad
        vgu[base + hidden : base + hpad, :] = jnp.zeros((hpad - hidden, width), BF16)
        n2_gu[:, base + hidden : base + hpad] = jnp.ones((1, hpad - hidden), F32)
        for n in range(0, hidden, 128):
            size = min(128, hidden - n)
            v = wgu[k, n : n + size, :].astype(F32) + SCALE * tn(left[:, n : n + size], right)
            vgu[base + n : base + n + size, :] = v.astype(BF16)
            n2_gu[:, base + n : base + n + size] = nt(ones, (v * v).astype(BF16))[:1]
        units = slice(base, base + hidden)
        s_gu[:, base : base + hpad] = jnp.zeros((1, hpad), F32)
        s_gu[:, units] = m_gu[k : k + 1, :] * lax.rsqrt(n2_gu[:, units])
    stores.append(pltpu.make_async_copy(vgu, vgu_hbm, store_sems.at[4]))
    stores[-1].start()
    gather.late()

    @pl.when(core == 1)
    def _():
        for r in range(rows):
            to_sib[r].wait_recv()
            absorb(r, p.seq - 1)

    for copy in shares:
        copy.wait_recv()
    half = rows_of(p.z, RING * cols)
    stores.append(pltpu.make_async_copy(vfull.at[half], vout_hbm.at[half], store_sems.at[0]))
    stores[-1].start()

    def from_far(r):
        @pl.when(upper == 1)
        def _():
            to_far[r].wait_recv()
            onward[r].start()
            absorb(r, core)
            onward[r].wait_recv()
            absorb(r, 1 - core)

    from_far(0)
    gather.end()
    share(p.far, (0, 1, 2, 3))
    for r in range(1, rows):
        from_far(r)

    @pl.loop(p.seq + 1, kv.shape[0])
    def _(j):
        kv[j] = jnp.zeros(kv.shape[1:], BF16)

    stores.append(pltpu.make_async_copy(kv, kv_hbm, store_sems.at[5]))
    stores[-1].start()
    for r in range(rows):
        part = slice(r * span, (r + 1) * span)
        for head in range(heads):
            at = slice(head * HD, (head + 1) * HD)
            one = (slice(None), slice(r * heads + head, r * heads + head + 1))
            mixed_ref[part, at] = (acc[part, at] / weight[one]).astype(BF16)
            lse_ref[part, at] = jnp.broadcast_to(top[one] + jnp.log(weight[one]), (span, HD))
    av_out[...] = nn(at_mine[...], vfull[my_cols, :]) / spread
    at_down = t_down[...].astype(BF16)
    av_down[...] = nn(at_down, vdown[:hidden, :]) / spread
    for copy in square_copies:
        copy.wait_recv()
    total = squares[...]
    for step in range(PARTS - 1):
        total += land_squares[step]
    n2_model[...] = total
    s_out[...] = m_out[...] * lax.rsqrt(total[0:1])
    s_down[...] = m_down[...] * lax.rsqrt(total[1:2])
    for copy in at_copies + shares[RING - 1 :]:
        copy.wait_recv()
    half = rows_of(p.far, RING * cols)
    stores.append(pltpu.make_async_copy(vfull.at[half], vout_hbm.at[half], store_sems.at[6]))
    stores[-1].start()
    for copy in at_copies + square_copies + shares:
        copy.wait_send()
    for copy in stores:
        copy.wait()

    @pl.when(upper == 0)
    def _():
        for r in range(rows):
            to_far[r].wait_send()

    @pl.when(core == 0)
    def _():
        for r in range(rows):
            to_sib[r].wait_send()

    @pl.when(upper == 1)
    def _():
        for r in range(rows):
            onward[r].wait_send()


def front(rows, seqs, spread, lengths, *rest):
    x, w_qkv, _, _, w_down = rest[-5:]
    tokens, width = x.shape
    cols = w_qkv.shape[2]
    heads = cols // HD
    hidden = w_down.shape[0]
    hpad = pad_to(hidden)
    span = tokens // rows
    shape = jax.ShapeDtypeStruct
    dma = pltpu.SemaphoreType.DMA
    vmem = pltpu.VMEM
    out_shape = (
        shape((tokens, cols), BF16),
        shape((tokens, 3 * cols), BF16),
        shape((tokens, cols), BF16),
        shape((tokens, cols), F32),
        shape((1, 3 * cols), F32),
        shape((1, 2 * hpad), F32),
        shape((8, width), F32),
        shape((1, 3 * cols), F32),
        shape((1, 2 * hpad), F32),
        shape((1, width), F32),
        shape((1, width), F32),
        shape((RANK, width), BF16),
        shape((RANK, width), F32),
        shape((RANK, width), F32),
        shape((tokens, width), BF16),
        shape((width, 3 * cols), BF16),
        shape((PARTS * cols, width), BF16),
        shape((2 * hpad, width), BF16),
        shape((hpad, width), BF16),
        shape((seqs, tokens, 2 * cols), BF16),
    )
    scratch = [
        vmem((tokens, width), BF16),
        vmem((3, width, cols), BF16),
        vmem((cols, width), BF16),
        vmem((2, hidden, width), BF16),
        vmem((hidden, width), BF16),
        vmem((tokens, width), BF16),
        vmem((width, 3 * cols), BF16),
        vmem((PARTS * cols, width), BF16),
        vmem((2 * hpad, width), BF16),
        vmem((hpad, width), BF16),
        vmem((seqs, tokens, 2 * cols), BF16),
        vmem((tokens, cols), F32),
        vmem((span, rows * heads), F32),
        vmem((span, rows * heads), F32),
        vmem((8, width), F32),
        vmem((PARTS - 1, 8, width), F32),
        vmem((RANK, cols), BF16),
        dma((5,)),
        dma((7,)),
        dma((GATHER_SEMS,)),
        dma((GATHER_SEMS,)),
        dma((PARTS,)),
        dma((PARTS,)),
        dma((3 * rows,)),
        dma((3 * rows,)),
    ] + [dma((PARTS - 1,))] * 4
    anywhere = pl.BlockSpec(memory_space=pl.ANY)
    return pl.pallas_call(
        functools.partial(front_kernel, rows, spread),
        out_shape=out_shape,
        in_specs=[pl.BlockSpec(memory_space=pltpu.SMEM)] + [VMEM] * 15 + [anywhere] * 5,
        out_specs=[VMEM] * 14 + [anywhere] * 6,
        scratch_shapes=scratch,
        compiler_params=pltpu.CompilerParams(
            collective_id=4, has_side_effects=True, vmem_limit_bytes=ROOM
        ),
    )(lengths, *rest)


def finish_kernel(
    hidden,
    summed,
    summed_qkv,
    m_qkv,
    m_out,
    m_gu,
    m_down,
    n2_model,
    b_out,
    b_down,
    vdown_hbm,
    vout_hbm,
    out_hbm,
    gx_hbm,
    output,
    grad_x,
    gm_qkv,
    ga_qkv,
    gb_qkv,
    gm_out,
    ga_out,
    gb_out,
    gm_gu,
    ga_gu,
    gb_gu,
    gm_down,
    ga_down,
    gb_down,
    vout,
    vdown,
    held,
    sems,
):
    cols, width = vout.shape
    hpad = vdown.shape[0]
    load = pltpu.make_async_copy(vout_hbm.at[rows_of(lax.axis_index("head"), cols)], vout, sems.at[0])
    load.start()
    load_down = pltpu.make_async_copy(vdown_hbm, vdown, sems.at[33])
    load_down.start()
    moves = []
    tokens = output.shape[0]
    for i in range(8):
        part = pl.ds(i * tokens // 8, tokens // 8)
        for k, src in enumerate((out_hbm, gx_hbm)):
            moves.append(pltpu.make_async_copy(src.at[part], held.at[k, part], sems.at[1 + 2 * i + k]))
            moves[-1].start()
    for i in range(8):
        part = pl.ds(i * tokens // 8, tokens // 8)
        for k, dst in enumerate((output, grad_x)):
            moves[2 * i + k].wait()
            moves.append(pltpu.make_async_copy(held.at[k, part], dst.at[part], sems.at[17 + 2 * i + k]))
            moves[-1].start()

    def block(first):
        return summed[first * RANK : (first + 1) * RANK, :]

    own_qkv = slice(COMMON_QKV, COMMON_QKV + RANK)
    for k in range(3):
        at = slice(k * cols, (k + 1) * cols)
        ga_qkv[k] = SCALE * summed_qkv[k * RANK : (k + 1) * RANK, :]
        gb_qkv[k] = SCALE * summed_qkv[own_qkv, at]
        e_one = summed_qkv[COMMON_QKV : COMMON_QKV + 1, (3 + k) * cols : (4 + k) * cols]
        gm_qkv[k : k + 1, :] = e_one / m_qkv[k : k + 1, :]
    for k in range(2):
        ga_gu[k] = SCALE * block(k)
    e_out = summed[7 * RANK : 7 * RANK + 1, :]
    e_down = summed[7 * RANK + 1 : 7 * RANK + 2, :]
    ratio_out = e_out / n2_model[0:1, :]
    ratio_down = e_down / n2_model[1:2, :]
    gm_out[...] = e_out / m_out[...]
    gm_down[...] = e_down / m_down[...]
    gb_out[...] = SCALE * (block(2) - block(5) * ratio_out)
    gb_down[...] = SCALE * (block(3) - block(6) * ratio_down)
    own_rows = slice(COMMON_FEED, COMMON_FEED + RANK)
    fold_rows = slice(COMMON_FEED + RANK, COMMON_FEED + OWN_FEED)
    fits = width - 2 * hpad
    gb = summed[own_rows, : 2 * hpad]
    e_gu = summed[COMMON_FEED + RANK : COMMON_FEED + RANK + 1, fits:]
    for k in range(2):
        at = slice(k * hpad, k * hpad + hidden)
        gb_gu[k] = SCALE * gb[:, at]
        gm_gu[k : k + 1, :] = e_gu[:, at] / m_gu[k : k + 1, :]
    back_down = (b_down[...] * ratio_down).astype(BF16)
    load_down.wait()
    down = jnp.concatenate([summed[own_rows, 2 * hpad :], summed[fold_rows, : hpad - fits]], axis=1)
    down = down - nt(back_down, vdown[...])
    ga_down[...] = SCALE * down[:, :hidden]
    load.wait()
    back_out = (b_out[...] * ratio_out).astype(BF16)
    at = rows_of(lax.axis_index("head"), cols)
    ga_out[...] = SCALE * (summed[4 * RANK : 5 * RANK, at] - nt(back_out, vout[...]))
    for move in moves[16:]:
        move.wait()


def finish(hidden, cols, summed, *rest):
    width = summed.shape[1]
    tokens = rest[-1].shape[0]
    shape = jax.ShapeDtypeStruct
    out_shape = (
        shape((tokens, width), BF16),
        shape((tokens, width), BF16),
        shape((3, cols), F32),
        shape((3, RANK, width), F32),
        shape((3, RANK, cols), F32),
        shape((1, width), F32),
        shape((RANK, cols), F32),
        shape((RANK, width), F32),
        shape((2, hidden), F32),
        shape((2, RANK, width), F32),
        shape((2, RANK, hidden), F32),
        shape((1, width), F32),
        shape((RANK, hidden), F32),
        shape((RANK, width), F32),
    )
    anywhere = pl.BlockSpec(memory_space=pl.ANY)
    return pl.pallas_call(
        functools.partial(finish_kernel, hidden),
        out_shape=out_shape,
        in_specs=[VMEM] * 9 + [anywhere] * 4,
        out_specs=[anywhere] * 2 + [VMEM] * 12,
        scratch_shapes=[
            pltpu.VMEM((cols, width), BF16),
            pltpu.VMEM(rest[-4].shape, BF16),
            pltpu.VMEM((2, tokens, width), BF16),
            pltpu.SemaphoreType.DMA((34,)),
        ],
        compiler_params=pltpu.CompilerParams(vmem_limit_bytes=ROOM),
    )(summed, *rest)


def shards(
    layer_input,
    cotangent,
    lengths,
    gain_attn,
    gain_ffn,
    w_qkv,
    m_qkv,
    a_qkv,
    b_qkv,
    w_out,
    m_out,
    a_out,
    b_out,
    w_gu,
    m_gu,
    a_gu,
    b_gu,
    w_down,
    m_down,
    a_down,
    b_down,
):
    rows, span, width = layer_input.shape
    seqs = lax.axis_size("seq")
    tokens = rows * span
    cols = w_qkv.shape[2]
    hidden = w_gu.shape[2]
    hpad = pad_to(hidden)

    positions = lax.axis_index("seq") * span + jnp.arange(span, dtype=jnp.int32)
    freqs = ROPE_BASE ** (-jnp.arange(HD // 2, dtype=F32) * 2.0 / HD)
    turned = positions.astype(F32)[:, None] * freqs[None, :]
    cosines = jnp.concatenate([jnp.cos(turned)] * 2, axis=1)
    sines = jnp.concatenate([-jnp.sin(turned), jnp.sin(turned)], axis=1)
    x = layer_input.reshape(tokens, width)
    t_qkv, t_gu = a_qkv.transpose(0, 2, 1), a_gu.transpose(0, 2, 1)
    t_out, t_down = a_out.T, a_down.T
    (
        query,
        kept,
        mixed,
        lse,
        n2_qkv,
        n2_gu,
        n2_model,
        s_qkv,
        s_gu,
        s_out,
        s_down,
        full_t_out,
        av_out,
        av_down,
        normed1,
        vb_qkv,
        full_out,
        vb_gu,
        vb_down,
        pairs,
    ) = front(
        rows,
        seqs,
        float(lax.axis_size("row") * seqs),
        lengths,
        gain_attn[None],
        m_qkv,
        m_out[None],
        m_gu,
        m_down[None],
        t_qkv,
        b_qkv,
        t_out,
        b_out,
        t_gu,
        b_gu,
        t_down,
        b_down,
        cosines,
        sines,
        x,
        w_qkv,
        w_out,
        w_gu.transpose(0, 2, 1),
        w_down,
    )
    cot = cotangent.reshape(tokens, width)
    (
        hidden1,
        grad_h1,
        grad_mixed,
        pack,
        ffn_part,
    ) = feed(
        span,
        lengths,
        mixed,
        s_out,
        gain_ffn[None],
        s_gu,
        s_down,
        n2_gu,
        b_gu,
        t_gu.reshape(2 * RANK, width),
        t_down,
        b_down,
        b_out,
        full_t_out,
        av_out,
        av_down,
        x,
        cot,
        full_out,
        vb_gu,
        vb_down,
    )
    dqkv, e_qkv, output, e_down = back(
        rows,
        lengths,
        cosines,
        sines,
        s_qkv,
        s_down,
        query,
        mixed,
        lse,
        grad_mixed,
        kept,
        hidden1,
        cot,
        pairs,
        ffn_part,
    )
    grad_x, summed, summed_qkv = close(
        cols,
        dqkv,
        vb_qkv,
        normed1,
        x,
        grad_h1,
        pack,
        gain_attn[None],
        b_qkv,
        t_qkv.reshape(3 * RANK, width),
        e_qkv,
        n2_qkv,
        e_down,
    )
    (
        output,
        grad_x,
        gm_qkv,
        ga_qkv,
        gb_qkv,
        gm_out,
        ga_out,
        gb_out,
        gm_gu,
        ga_gu,
        gb_gu,
        gm_down,
        ga_down,
        gb_down,
    ) = finish(
        hidden,
        cols,
        summed,
        summed_qkv,
        m_qkv,
        m_out[None],
        m_gu,
        m_down[None],
        n2_model,
        b_out,
        b_down,
        vb_down,
        full_out,
        output,
        grad_x,
    )
    return (
        output.reshape(rows, span, width),
        grad_x.reshape(rows, span, width),
        gm_qkv,
        ga_qkv.transpose(0, 2, 1),
        gb_qkv,
        gm_out[0],
        ga_out.T,
        gb_out,
        gm_gu,
        ga_gu.transpose(0, 2, 1),
        gb_gu,
        gm_down[0],
        ga_down.T,
        gb_down,
    )


def solution(mesh):
    placed = (
        P("row", "seq", None),
        P("row", "seq", None),
        P("row"),
        P(),
        P(),
        P(None, None, "head"),
        P(None, "head"),
        P(),
        P(None, None, "head"),
        P("head", None),
        P(),
        P("head", None),
        P(),
        P(None, None, "head"),
        P(None, "head"),
        P(),
        P(None, None, "head"),
        P("head", None),
        P(),
        P("head", None),
        P(),
    )
    return jax.shard_map(
        shards,
        mesh=mesh,
        in_specs=placed,
        out_specs=(
            P("row", "seq", None),
            P("row", "seq", None),
            P(None, "head"),
            P(),
            P(None, None, "head"),
            P(),
            P("head", None),
            P(),
            P(None, "head"),
            P(),
            P(None, None, "head"),
            P(),
            P("head", None),
            P(),
        ),
        check_vma=False,
    )
```
